32 devices in a mesh: grp: 1, ep: 16 (over z, y, x), pd: 2 (over core).
Axes of the slice: x: 2, y: 2, z: 4, core: 2. Of those that a mesh axis runs over, the one named last changes fastest.
Arguments:
- prompt_kv: bfloat16 [256, 2, 16, 4, 128], P(('grp', 'ep'), None, None, 'pd'), may hold values from -6 to 6
- page_owner: int32 [256, 1], P('grp'), may hold values from 0 to 15; in each aligned block of 16 rows (0 to 15, 16 to 31, ...) at most 2 rows name the same one
- page_slot: int32 [256], P('grp'), may hold values from 0 to 7
- page_fill: int32 [256], P('grp'), may hold values from 1 to 16
- queries: bfloat16 [128, 3, 64, 128], P(('grp', 'ep'), None, 'pd'), may hold values from -400 to 400
- new_kv: bfloat16 [128, 3, 2, 4, 128], P(('grp', 'ep'), None, None, 'pd'), may hold values from -8 to 8
- moe_input: bfloat16 [128, 3, 4096], P(('grp', 'ep')), may hold values from -6 to 6
- expert_routes: int32 [3, 128, 8], P(None, ('grp', 'ep')), may hold values from 0 to 15, all different within a row; in each aligned block of 8 rows (0 to 7, 8 to 15, ..., all dimensions but the last counted through in order) at most 8 rows name the same one
- route_probs: float32 [128, 3, 8], P(('grp', 'ep')), may hold values from 0.02 to 0.5
- w_gate: bfloat16 [16, 4096, 768], P('ep', None, 'pd'), may hold values from -0.09375 to 0.09375
- w_up: bfloat16 [16, 4096, 768], P('ep', None, 'pd'), may hold values from -0.09375 to 0.09375
- w_down: bfloat16 [16, 768, 4096], P('ep', None, 'pd'), may hold values from -0.21875 to 0.21875
Outputs:
- attn_out: bfloat16 [128, 3, 64, 128], P(('grp', 'ep'), None, 'pd')
- moe_out: bfloat16 [128, 3, 4096], P(('grp', 'ep'), None, 'pd')
The draws below stay inside these ranges and needn't reach their ends.
Inputs may be any that keep to these rules, and one draw needn't show every extreme that they name: `page_owner`: the 16 pages of one index of ep name any decode owner at most 2 times, a bound that some block reaches. `expert_routes`: each token's 8 experts differ; in one decode step the 8 tokens of one index of ep name any expert at most 8 times, and this bound is reached.
All inputs are finite; a program needn't handle non-finite values.
Results may differ from the reference program's by a relative error of at most 0.0057.
Values may be sent and summed in bfloat16 or wider, within the bound.
No kernel may reach another device: no remote copies, remote signals or barrier semaphores. Data moves between devices by JAX's collectives and lax.ppermute only.
A program may use at most 64 MiB of HBM per device.

```python
import math
import jax
import jax.numpy as jnp
import numpy as np
from jax import lax

D = 4096
HD = 128
QH = 64
KVH = 4
MOE_FF = 768
TOP = 8
PAGE = 16
CAP = 2
STEPS = 3
REQ_OWN = 8
PAGES_DEV = 16
PAGES = 256
REQUESTS = 128
EXPERTS = 16
CAP_E = 8
N_EP = 16


def shared_fresh(key):
    fresh = jax.random.normal(jax.random.fold_in(key, 11), (REQUESTS, STEPS, 2, KVH, HD), jnp.float32)
    return fresh


def draw_new_kv(key, part):
    fresh = shared_fresh(key)
    return fresh.astype(jnp.bfloat16)


def draw_queries(key, part):
    key = jax.random.fold_in(key, 5)
    base = 1.5 * jax.random.normal(key, (REQUESTS, STEPS, QH, HD), jnp.float32)
    return base.astype(jnp.bfloat16)


def touch_ends(drawn, own_key, least, high):
    shape = drawn.shape
    index_at = [jax.random.randint(jax.random.fold_in(own_key, axis), (), 0, shape[axis]) for axis in range(len(shape))]
    drawn = drawn.at[tuple(index_at)].set(least)
    longest = shape.index(max(shape))
    index_at[longest] = (index_at[longest] + 1) % shape[longest]
    return drawn.at[tuple(index_at)].set(high)


def block_levels(key, shape, shards, least, high):
    def one(axis_at, blocks):
        heights = jax.random.uniform(jax.random.fold_in(jax.random.fold_in(key, 6), axis_at), (blocks,), jnp.float32, least / len(shards), high / len(shards))
        return jnp.repeat(jnp.exp(heights), shape[axis_at] // blocks).reshape((-1,) + (1,) * (len(shape) - axis_at - 1))

    factor_of = one(*shards[0])
    for cut in shards[1:]:
        factor_of = factor_of * one(*cut)
    return factor_of


def routed_block(rng, own, number, rows, amount, top, reach, skew):
    sequence = jax.random.permutation(rng, amount)
    crowded, ordinary = load_shares(amount, rows * top, reach, skew, True), load_shares(amount, rows * top, reach, skew, False)
    places = jnp.arange(amount)

    def named(tallies, rotation):
        used = int((tallies > 0).sum())
        fixed = max(1, used // 4)
        passed = fixed + (places - fixed + rotation * (used - fixed)) % max(1, amount - fixed)
        return jnp.zeros((amount,), jnp.int32).at[sequence[jnp.where(places < fixed, places, passed)]].set(jnp.asarray(tallies, jnp.int32))

    tallies = jnp.where(number % 4 == 0, named(crowded, number // 4), named(ordinary, number - number // 4 - 1))
    mixed = jax.random.permutation(jax.random.fold_in(own, 3), amount)
    giver, sink = mixed[0:amount // 2 * 2:2], mixed[1:amount // 2 * 2:2]
    margin = jnp.minimum(tallies[giver] - 1, reach - tallies[sink]) // 2
    margin = jnp.where((giver == sequence[0]) | (sink == sequence[0]) | (tallies[sink] == 0), 0, jnp.maximum(margin, 0))
    passed = jax.random.randint(jax.random.fold_in(own, 4), (amount // 2,), 0, 1 << 20) % (margin + 1)
    tallies = tallies.at[giver].add(-passed).at[sink].add(passed)
    labels = jnp.searchsorted(jnp.cumsum(tallies), jnp.arange(rows * top), side="right").astype(jnp.int32)
    grid = labels.reshape(top, rows).T
    grid = grid[jax.random.permutation(jax.random.fold_in(own, 1), rows)]
    rotation = jax.random.randint(jax.random.fold_in(own, 2), (rows, 1), 0, top)
    return jnp.take_along_axis(grid, (jnp.arange(top)[None, :] + rotation) % top, axis=1)


def load_shares(number_of, total, reach, lean, full):
    loads = [(1 << 20) // math.isqrt(grade ** lean) + 1 for grade in range(1, number_of + 1)]
    largest = reach if full else min(reach, max(-(-total // number_of), total * loads[0] // sum(loads)))
    least = 1 if total - largest >= number_of - 1 else 0
    holding, surplus = [largest] + [least] * (number_of - 1), total - largest - least * (number_of - 1)
    while surplus > 0:
        candidates = [i for i in range(1, number_of) if holding[i] < largest] or [i for i in range(1, number_of) if holding[i] < reach]
        whole, remaining = sum([loads[i] for i in candidates]), surplus
        for i in candidates:
            more = min(reach - holding[i], max(1, remaining * loads[i] // whole), surplus)
            holding[i] = holding[i] + more
            surplus = surplus - more
    return np.array(holding)


def gaussian(rng, extent, scale, most, shards=(), kind=jnp.bfloat16):
    array = jax.random.normal(rng, extent, jnp.float32) * scale
    if len(shards) > 0:
        array = block_levels(rng, extent, shards, -0.22, 0.18) * array
    return jnp.clip(array, min=-most, max=most).astype(kind)


def setup_inputs(seed: int = 0, part: int = 0) -> dict:
    splits = jax.random.split(jax.random.key(seed), 13)
    own_keys = jax.random.split(jax.random.fold_in(splits[12], part), 13)
    prompt_kv = gaussian(own_keys[0], (PAGES, 2, PAGE, KVH, HD), 1.0, 6.0, ((0, 16), (3, 2)))
    page_owner_keys = jax.random.split(jax.random.fold_in(own_keys[1], 1), PAGES // PAGES_DEV)
    page_owner_turns = jax.random.permutation(jax.random.fold_in(own_keys[1], 3), PAGES // PAGES_DEV)
    page_owner = jax.vmap(lambda own, number: routed_block(jax.random.fold_in(own_keys[1], 2), own, number, PAGES_DEV, N_EP, 1, CAP, 2))(page_owner_keys, page_owner_turns).reshape((PAGES, 1))
    page_slot = touch_ends(jax.random.randint(own_keys[2], (PAGES,), 0, REQ_OWN), jax.random.fold_in(own_keys[2], 1), 0, REQ_OWN - 1).astype(jnp.int32)
    page_fill = touch_ends(jax.random.randint(own_keys[3], (PAGES,), 1, PAGE + 1), jax.random.fold_in(own_keys[3], 1), 1, PAGE).astype(jnp.int32)
    queries = draw_queries(jax.random.fold_in(jax.random.fold_in(splits[12], part), 71), part)
    new_kv = draw_new_kv(jax.random.fold_in(jax.random.fold_in(splits[12], part), 71), part)
    moe_input = gaussian(own_keys[6], (REQUESTS, STEPS, D), 1.0, 6.0, ((0, 16),))
    expert_routes_keys = jax.random.split(jax.random.fold_in(own_keys[7], 1), STEPS * REQUESTS // REQ_OWN)
    expert_routes_turns = jax.random.permutation(jax.random.fold_in(own_keys[7], 3), STEPS * REQUESTS // REQ_OWN)
    expert_routes = jax.vmap(lambda own, number: routed_block(jax.random.fold_in(own_keys[7], 2), own, number, REQ_OWN, EXPERTS, TOP, CAP_E, 2))(expert_routes_keys, expert_routes_turns).reshape((STEPS, REQUESTS, TOP))
    route_probs = jnp.clip(jnp.exp(math.log(0.5) - 3.218876 * jax.random.uniform(own_keys[8], (REQUESTS, STEPS, TOP), jnp.float32) ** block_levels(own_keys[8], (REQUESTS, STEPS, TOP), ((0, 16),), -0.2, 0.2)), 0.02, 0.5)
    w_gate = gaussian(splits[9], (EXPERTS, D, MOE_FF), D ** -0.5, 0.09375, ((0, 16), (2, 2)))
    w_up = gaussian(splits[10], (EXPERTS, D, MOE_FF), D ** -0.5, 0.09375, ((0, 16), (2, 2)))
    w_down = gaussian(splits[11], (EXPERTS, MOE_FF, D), MOE_FF ** -0.5, 0.21875, ((0, 16), (2, 2)))
    return dict(prompt_kv=prompt_kv, page_owner=page_owner, page_slot=page_slot, page_fill=page_fill, queries=queries, new_kv=new_kv, moe_input=moe_input, expert_routes=expert_routes, route_probs=route_probs, w_gate=w_gate, w_up=w_up, w_down=w_down)


LIMIT = 448.0

def quantize(blocks):
    values = blocks.astype(jnp.float32)
    largest = lax.optimization_barrier(jnp.max(jnp.abs(values), axis=(2, 4), keepdims=True))
    block_scale = jnp.full(largest.shape, 2.0 ** (-16), jnp.float32)
    inverse = jnp.full(largest.shape, 2.0 ** 16, jnp.float32)
    for exponent in range(-16, 4):
        exceeds = largest > LIMIT * 2.0 ** exponent
        block_scale = jnp.where(exceeds, block_scale * 2.0, block_scale)
        inverse = jnp.where(exceeds, inverse * 0.5, inverse)
    scaled = values * inverse
    magnitude = jnp.abs(scaled)
    grid_step = jnp.full(scaled.shape, 2.0 ** (-9), jnp.float32)
    grid_inverse = jnp.full(scaled.shape, 2.0 ** 9, jnp.float32)
    for exponent in range(-5, 9):
        exceeds = magnitude >= 2.0 ** exponent
        grid_step = jnp.where(exceeds, grid_step * 2.0, grid_step)
        grid_inverse = jnp.where(exceeds, grid_inverse * 0.5, grid_inverse)
    levels = jnp.minimum(jnp.floor(magnitude * grid_inverse + 0.5) * grid_step, LIMIT)
    page_quant = (jnp.sign(scaled) * levels).astype(jnp.bfloat16)
    page_scale = block_scale.astype(jnp.bfloat16)
    return (page_quant, page_scale)

def dequantize(page_quant, page_scale):
    return (page_quant.astype(jnp.float32) * page_scale.astype(jnp.float32)).astype(jnp.bfloat16)

def attend(queries, cache_keys, cache_values, visible, fresh_keys, fresh_values):
    requests, steps, heads, width = queries.shape
    groups = cache_keys.shape[1]
    grouped = queries.astype(jnp.float32).reshape(requests, steps, groups, heads // groups, width)
    factor = 1.0 / math.sqrt(width)
    cache_scores = jnp.einsum('rskgd,jkd->rskgj', grouped, cache_keys.astype(jnp.float32)) * factor
    fresh_scores = jnp.einsum('rskgd,rtkd->rskgt', grouped, fresh_keys.astype(jnp.float32)) * factor
    cache_mask = visible[:, None, None, None, :]
    fresh_mask = (jnp.arange(steps)[None, :] <= jnp.arange(steps)[:, None])[None, :, None, None, :]
    cache_scores = jnp.where(cache_mask, cache_scores, -jnp.inf)
    fresh_scores = jnp.where(fresh_mask, fresh_scores, -jnp.inf)
    peak = jnp.maximum(lax.optimization_barrier(jnp.max(cache_scores, axis=-1, keepdims=True)), lax.optimization_barrier(jnp.max(fresh_scores, axis=-1, keepdims=True)))
    cache_weight = jnp.where(cache_mask, jnp.exp(cache_scores - peak), 0.0)
    fresh_weight = jnp.where(fresh_mask, jnp.exp(fresh_scores - peak), 0.0)
    total_weight = lax.optimization_barrier(jnp.sum(cache_weight, axis=-1, keepdims=True)) + lax.optimization_barrier(jnp.sum(fresh_weight, axis=-1, keepdims=True))
    cache_rounded = cache_weight.astype(jnp.bfloat16).astype(jnp.float32)
    fresh_rounded = fresh_weight.astype(jnp.bfloat16).astype(jnp.float32)
    mixed = jnp.einsum('rskgj,jkd->rskgd', cache_rounded, cache_values.astype(jnp.float32))
    mixed = mixed + jnp.einsum('rskgt,rtkd->rskgd', fresh_rounded, fresh_values.astype(jnp.float32))
    return (mixed / total_weight).reshape(requests, steps, heads, width).astype(jnp.bfloat16)

def reference(prompt_kv, page_owner, page_slot, page_fill, queries, new_kv, moe_input, expert_routes, route_probs, w_gate, w_up, w_down):
    page_quant, page_scale = quantize(prompt_kv)
    cache = dequantize(page_quant, page_scale)
    owners = page_owner[:, 0].astype(jnp.int32)
    slot_total = N_EP * CAP
    order = jnp.argsort(owners, stable=True).astype(jnp.int32)
    counts = lax.optimization_barrier(jnp.sum((owners[None, :] == jnp.arange(N_EP, dtype=jnp.int32)[:, None]).astype(jnp.int32), axis=1)).astype(jnp.int32)
    starts = (jnp.cumsum(counts) - counts).astype(jnp.int32)
    padded = jnp.concatenate([order, jnp.zeros((slot_total,), jnp.int32)])
    owner_queries = queries.reshape(N_EP, REQ_OWN, STEPS, QH, HD)
    owner_new = new_kv.reshape(N_EP, REQ_OWN, STEPS, 2, KVH, HD)

    def one_owner(inputs):
        owner, own_queries, own_new = inputs
        chosen = lax.dynamic_slice_in_dim(padded, starts[owner], slot_total)
        live_slot = jnp.arange(slot_total) < counts[owner]
        pages = cache[chosen]
        slots = page_slot[chosen]
        fills = page_fill[chosen]
        visible = live_slot[None, :, None] & (slots[None, :, None] == jnp.arange(REQ_OWN)[:, None, None])
        visible = visible & (jnp.arange(PAGE)[None, None, :] < fills[None, :, None])
        visible = visible.reshape(REQ_OWN, slot_total * PAGE)
        cache_keys = pages[:, 0].reshape(slot_total * PAGE, KVH, HD)
        cache_values = pages[:, 1].reshape(slot_total * PAGE, KVH, HD)
        return attend(own_queries, cache_keys, cache_values, visible, own_new[:, :, 0], own_new[:, :, 1])
    attn_out = lax.map(one_owner, (jnp.arange(N_EP, dtype=jnp.int32), owner_queries, owner_new))
    attn_out = attn_out.reshape(REQUESTS, STEPS, QH, HD)
    tokens = moe_input.reshape(REQUESTS * STEPS, D)
    routes = jnp.transpose(expert_routes, (1, 0, 2))
    flat = routes.reshape(-1).astype(jnp.int32)
    picks = flat.shape[0]
    per_expert = N_EP * STEPS * CAP_E
    expert_order = jnp.argsort(flat, stable=True).astype(jnp.int32)
    expert_counts = lax.optimization_barrier(jnp.sum((flat[None, :] == jnp.arange(EXPERTS, dtype=jnp.int32)[:, None]).astype(jnp.int32), axis=1)).astype(jnp.int32)
    expert_starts = (jnp.cumsum(expert_counts) - expert_counts).astype(jnp.int32)
    expert_padded = jnp.concatenate([expert_order, jnp.zeros((per_expert,), jnp.int32)])

    def one_expert(expert):
        chosen = lax.dynamic_slice_in_dim(expert_padded, expert_starts[expert], per_expert)
        live_pick = jnp.arange(per_expert) < expert_counts[expert]
        rows = tokens[chosen // TOP]
        gate = jnp.dot(rows, w_gate[expert], preferred_element_type=jnp.float32)
        up = jnp.dot(rows, w_up[expert], preferred_element_type=jnp.float32)
        hidden = (jax.nn.silu(gate) * up).astype(jnp.bfloat16)
        result = jnp.dot(hidden, w_down[expert], preferred_element_type=jnp.float32).astype(jnp.bfloat16)
        return (jnp.where(live_pick, chosen, picks).astype(jnp.int32), result)
    where_to, results = lax.map(one_expert, jnp.arange(EXPERTS, dtype=jnp.int32))
    gathered = jnp.zeros((picks + 1, D), jnp.bfloat16).at[where_to.reshape(-1)].set(results.reshape(-1, D))[:picks]
    gathered = gathered.reshape(REQUESTS, STEPS, TOP, D).astype(jnp.float32)
    moe_out = lax.optimization_barrier(jnp.sum(route_probs[..., None] * gathered, axis=2)).astype(jnp.bfloat16)
    return (attn_out, moe_out)
```

```python
import functools
import math

import jax
import jax.numpy as jnp
from jax import lax
from jax.experimental import pallas as pl
from jax.experimental.pallas import tpu as pltpu
from jax.sharding import PartitionSpec as P

CAP = 2
LIMIT = 448.0
MIB = 1024 * 1024


def vmem():
    return pl.BlockSpec(memory_space=pltpu.VMEM)


def smem():
    return pl.BlockSpec(memory_space=pltpu.SMEM)


def page_kernel(pages, me_ref, owner_ref, kv_ref, send_ref, count_ref):
    values = kv_ref[...].astype(jnp.float32)
    largest = jnp.max(jnp.abs(values), axis=(3, 4), keepdims=True)
    scale = jnp.full(largest.shape, 2.0 ** (-16), jnp.float32)
    inverse = jnp.full(largest.shape, 2.0**16, jnp.float32)
    for exponent in range(-16, 4):
        exceeds = largest > LIMIT * 2.0**exponent
        scale = jnp.where(exceeds, scale * 2.0, scale)
        inverse = jnp.where(exceeds, inverse * 0.5, inverse)
    scaled = values * inverse
    magnitude = jnp.abs(scaled)
    step = jnp.full(scaled.shape, 2.0 ** (-9), jnp.float32)
    back = jnp.full(scaled.shape, 2.0**9, jnp.float32)
    for exponent in range(-5, 9):
        exceeds = magnitude >= 2.0**exponent
        step = jnp.where(exceeds, step * 2.0, step)
        back = jnp.where(exceeds, back * 0.5, back)
    levels = jnp.minimum(jnp.floor(magnitude * back + 0.5) * step, LIMIT)
    cache = (jnp.where(scaled < 0.0, -levels, levels) * scale).astype(jnp.bfloat16)

    send_ref[...] = jnp.zeros(send_ref.shape, send_ref.dtype)

    def clear(o, carry):
        count_ref[o] = 0
        return carry

    lax.fori_loop(0, count_ref.shape[0], clear, 0)
    first = me_ref[0] * pages
    for page in range(pages):
        owner = owner_ref[first + page]
        rank = count_ref[owner]
        count_ref[owner] = rank + 1
        send_ref[pl.ds(owner * CAP + rank, 1)] = cache[page : page + 1]


def attention_kernel(
    pages, me_ref, owner_ref, slot_ref, fill_ref, q_ref, cache_ref, fresh_ref, out_ref
):
    owners = owner_ref.shape[0]
    slots, _, heads, page_len, width = cache_ref.shape
    requests, steps, q_heads, _ = q_ref.shape
    group = q_heads // heads
    rows = requests * steps * group
    mine = (owner_ref[...] == me_ref[0]).astype(jnp.float32)
    before = (
        lax.broadcasted_iota(jnp.int32, (pages, pages), 0)
        < lax.broadcasted_iota(jnp.int32, (pages, pages), 1)
    ).astype(jnp.float32)
    rank = jnp.dot(mine, before, preferred_element_type=jnp.float32)
    code = (slot_ref[...] * (page_len + 1) + fill_ref[...]).astype(jnp.float32)
    columns = slots * page_len
    place = lax.broadcasted_iota(jnp.int32, (owners, columns), 1)
    source = lax.broadcasted_iota(jnp.int32, (owners, columns), 0)
    spread = jnp.zeros((owners, columns), jnp.float32)
    for c in range(CAP):
        held = jnp.sum(
            jnp.where((mine > 0.0) & (rank == float(c)), code, 0.0), axis=1, keepdims=True
        )
        spread = jnp.where(place // page_len == source * CAP + c, held, spread)
    line = jnp.sum(spread, axis=0, keepdims=True).astype(jnp.int32)
    request_of = line // (page_len + 1)
    fill_of = line - request_of * (page_len + 1)
    position = lax.broadcasted_iota(jnp.int32, (1, columns), 1) % page_len
    request_of = jnp.where(position < fill_of, request_of, -1)
    row_request = lax.broadcasted_iota(jnp.int32, (rows, 1), 0) // (steps * group)
    visible = row_request == request_of
    token = lax.broadcasted_iota(jnp.int32, (rows, 1), 0) // group
    first = row_request * steps
    fresh_at = lax.broadcasted_iota(jnp.int32, (1, fresh_ref.shape[2]), 1)
    fresh_visible = (fresh_at >= first) & (fresh_at <= token)
    factor = 1.0 / math.sqrt(width)
    contract = (((1,), (1,)), ((), ()))
    for head in range(heads):
        q = q_ref[:, :, head * group : (head + 1) * group, :].reshape(rows, width)
        keys = cache_ref[:, 0, head].reshape(columns, width)
        values = cache_ref[:, 1, head].reshape(columns, width)
        scores = lax.dot_general(q, keys, contract, preferred_element_type=jnp.float32) * factor
        fresh = (
            lax.dot_general(q, fresh_ref[0, head], contract, preferred_element_type=jnp.float32)
            * factor
        )
        scores = jnp.where(visible, scores, -jnp.inf)
        fresh = jnp.where(fresh_visible, fresh, -jnp.inf)
        peak = jnp.maximum(
            jnp.max(scores, axis=1, keepdims=True), jnp.max(fresh, axis=1, keepdims=True)
        )
        weight = jnp.exp(scores - peak)
        fresh_weight = jnp.exp(fresh - peak)
        total = jnp.sum(weight, axis=1, keepdims=True) + jnp.sum(
            fresh_weight, axis=1, keepdims=True
        )
        mixed = jnp.dot(
            weight.astype(jnp.bfloat16), values, preferred_element_type=jnp.float32
        ) + jnp.dot(
            fresh_weight.astype(jnp.bfloat16), fresh_ref[1, head], preferred_element_type=jnp.float32
        )
        out_ref[:, :, head * group : (head + 1) * group, :] = (
            (mixed / total).astype(out_ref.dtype).reshape(requests, steps, group, width)
        )


def front_kernel(blocks, x_ref, gate_ref, up_ref, hidden_ref, gate_sum, up_sum):
    k = pl.program_id(0)
    gate = jnp.dot(x_ref[...], gate_ref[0], preferred_element_type=jnp.float32)
    up = jnp.dot(x_ref[...], up_ref[0], preferred_element_type=jnp.float32)

    @pl.when(k == 0)
    def _():
        gate_sum[...] = gate
        up_sum[...] = up

    @pl.when((k > 0) & (k < blocks - 1))
    def _():
        gate_sum[...] += gate
        up_sum[...] += up

    @pl.when(k == blocks - 1)
    def _():
        whole = gate_sum[...] + gate
        hidden_ref[...] = (
            whole / (1.0 + jnp.exp(-whole)) * (up_sum[...] + up)
        ).astype(hidden_ref.dtype)


def down_kernel(me_ref, hidden_ref, down_ref, probs_ref, out_ref):
    half = hidden_ref.shape[2]
    total = jnp.dot(hidden_ref[0], down_ref[0, :half], preferred_element_type=jnp.float32)
    total += jnp.dot(hidden_ref[1], down_ref[0, half:], preferred_element_type=jnp.float32)
    probs = probs_ref[...]
    mine = lax.broadcasted_iota(jnp.int32, probs.shape, 1) == me_ref[0]
    weight = jnp.sum(jnp.where(mine, probs, 0.0), axis=1, keepdims=True)
    out_ref[...] = (total * weight).astype(out_ref.dtype)


def expert_front(x, w_gate, w_up):
    tokens = x.shape[0] // 2
    half, d, f = x.shape[1], w_gate.shape[1], w_gate.shape[2]
    depth = min(half, 1024)
    per_half = half // depth
    blocks = d // depth
    return pl.pallas_call(
        functools.partial(front_kernel, blocks),
        grid=(blocks,),
        out_shape=jax.ShapeDtypeStruct((tokens, f), jnp.bfloat16),
        in_specs=[
            pl.BlockSpec((tokens, depth), lambda k: (k // per_half, k % per_half)),
            pl.BlockSpec((1, depth, f), lambda k: (0, k, 0)),
            pl.BlockSpec((1, depth, f), lambda k: (0, k, 0)),
        ],
        out_specs=pl.BlockSpec((tokens, f), lambda k: (0, 0)),
        scratch_shapes=[pltpu.VMEM((tokens, f), jnp.float32)] * 2,
        compiler_params=pltpu.CompilerParams(vmem_limit_bytes=40 * MIB),
        cost_estimate=pl.CostEstimate(
            flops=4 * tokens * d * f,
            bytes_accessed=2 * (tokens * d + 2 * d * f + tokens * f),
            transcendentals=tokens * f,
        ),
        name="expert_front",
    )(x, w_gate, w_up)


def expert_back(me, hidden, w_down, probs):
    _, tokens, f = hidden.shape
    width = w_down.shape[2]
    block = min(width, 512)
    return pl.pallas_call(
        down_kernel,
        grid=(width // block,),
        out_shape=jax.ShapeDtypeStruct((tokens, width), jnp.bfloat16),
        in_specs=[
            smem(),
            pl.BlockSpec((2, tokens, f), lambda n: (0, 0, 0)),
            pl.BlockSpec((1, 2 * f, block), lambda n: (0, 0, n)),
            pl.BlockSpec(probs.shape, lambda n: (0, 0)),
        ],
        out_specs=pl.BlockSpec((tokens, block), lambda n: (0, n)),
        compiler_params=pltpu.CompilerParams(vmem_limit_bytes=40 * MIB),
        cost_estimate=pl.CostEstimate(
            flops=4 * tokens * f * width,
            bytes_accessed=2 * (2 * tokens * f + 2 * f * width + tokens * width),
            transcendentals=0,
        ),
        name="expert_back",
    )(me, hidden, w_down, probs)


def body(
    prompt_kv,
    page_owner,
    page_slot,
    page_fill,
    queries,
    new_kv,
    moe_input,
    expert_routes,
    route_probs,
    w_gate,
    w_up,
    w_down,
):
    owners = lax.axis_size("ep")
    me = lax.axis_index("ep").astype(jnp.int32)
    me_ref = me.reshape(1)
    core = lax.axis_index("pd")
    pages, _, page_len, heads, width = prompt_kv.shape
    requests, steps, q_heads, _ = queries.shape
    d = moe_input.shape[2]
    tokens = requests * steps
    slots = owners * CAP

    mine = lax.dynamic_slice_in_dim(
        moe_input.transpose(1, 0, 2).reshape(tokens, d), core * (d // 2), d // 2, axis=1
    )
    x = lax.all_gather(mine, ("pd", "ep"), axis=0, tiled=True)
    hot = expert_routes[..., None] == jnp.arange(owners, dtype=jnp.int32)
    own_probs = jnp.sum(
        jnp.where(hot, route_probs.transpose(1, 0, 2)[..., None], 0.0), axis=2
    ).reshape(tokens, owners)
    probs = lax.all_gather(own_probs, "ep", axis=0, tiled=True)

    send = pl.pallas_call(
        functools.partial(page_kernel, pages),
        out_shape=jax.ShapeDtypeStruct((slots, 2, heads, page_len, width), jnp.bfloat16),
        in_specs=[smem(), smem(), vmem()],
        out_specs=vmem(),
        scratch_shapes=[pltpu.SMEM((owners,), jnp.int32)],
        compiler_params=pltpu.CompilerParams(vmem_limit_bytes=40 * MIB),
        name="quantize_pages",
    )(me_ref, page_owner.reshape(-1), prompt_kv.transpose(0, 1, 3, 2, 4))
    cache = lax.all_to_all(send, "ep", split_axis=0, concat_axis=0, tiled=True)

    hidden = expert_front(x, w_gate, w_up)
    hidden = lax.all_gather(hidden, "pd", axis=0)
    parts = expert_back(me_ref, hidden, w_down, probs)
    moe = lax.psum_scatter(parts, "ep", scatter_dimension=0, tiled=True)
    moe_out = moe.reshape(steps, requests, d // 2).transpose(1, 0, 2)

    fresh = new_kv.transpose(2, 3, 0, 1, 4).reshape(2, heads, tokens, width)
    fresh = jnp.pad(fresh, ((0, 0), (0, 0), (0, 128 - tokens), (0, 0)))
    attn_out = pl.pallas_call(
        functools.partial(attention_kernel, pages),
        out_shape=jax.ShapeDtypeStruct(queries.shape, jnp.bfloat16),
        in_specs=[smem()] + [vmem()] * 6,
        out_specs=vmem(),
        compiler_params=pltpu.CompilerParams(vmem_limit_bytes=48 * MIB),
        name="attention",
    )(
        me_ref,
        page_owner.reshape(owners, pages),
        page_slot.reshape(owners, pages),
        page_fill.reshape(owners, pages),
        queries,
        cache,
        fresh,
    )
    return (attn_out, moe_out)


def solution(mesh):
    return jax.shard_map(
        body,
        mesh=mesh,
        in_specs=(
            P(("grp", "ep"), None, None, "pd", None),
            P("grp", None),
            P("grp"),
            P("grp"),
            P(("grp", "ep"), None, "pd", None),
            P(("grp", "ep"), None, None, "pd", None),
            P(("grp", "ep"), None, None),
            P(None, ("grp", "ep"), None),
            P(("grp", "ep"), None, None),
            P("ep", None, "pd"),
            P("ep", None, "pd"),
            P("ep", None, "pd"),
        ),
        out_specs=(P(("grp", "ep"), None, "pd", None), P(("grp", "ep"), None, "pd")),
        check_vma=False,
    )
```

```python
import functools
import math

import jax
import jax.numpy as jnp
from jax import lax
from jax.experimental import pallas as pl
from jax.experimental.pallas import tpu as pltpu
from jax.sharding import PartitionSpec as P

CAP = 2
LIMIT = 448.0
MIB = 1024 * 1024


def vmem():
    return pl.BlockSpec(memory_space=pltpu.VMEM)


def smem():
    return pl.BlockSpec(memory_space=pltpu.SMEM)


def page_kernel(pages, me_ref, owner_ref, kv_ref, send_ref, count_ref):
    values = kv_ref[...].astype(jnp.float32)
    largest = jnp.max(jnp.abs(values), axis=(3, 4), keepdims=True)
    scale = jnp.full(largest.shape, 2.0 ** (-16), jnp.float32)
    inverse = jnp.full(largest.shape, 2.0**16, jnp.float32)
    for exponent in range(-16, 4):
        exceeds = largest > LIMIT * 2.0**exponent
        scale = jnp.where(exceeds, scale * 2.0, scale)
        inverse = jnp.where(exceeds, inverse * 0.5, inverse)
    scaled = values * inverse
    magnitude = jnp.abs(scaled)
    step = jnp.full(scaled.shape, 2.0 ** (-9), jnp.float32)
    back = jnp.full(scaled.shape, 2.0**9, jnp.float32)
    for exponent in range(-5, 9):
        exceeds = magnitude >= 2.0**exponent
        step = jnp.where(exceeds, step * 2.0, step)
        back = jnp.where(exceeds, back * 0.5, back)
    levels = jnp.minimum(jnp.floor(magnitude * back + 0.5) * step, LIMIT)
    cache = (jnp.where(scaled < 0.0, -levels, levels) * scale).astype(jnp.bfloat16)

    send_ref[...] = jnp.zeros(send_ref.shape, send_ref.dtype)

    def clear(o, carry):
        count_ref[o] = 0
        return carry

    lax.fori_loop(0, count_ref.shape[0], clear, 0)
    first = me_ref[0] * pages
    for page in range(pages):
        owner = owner_ref[first + page]
        rank = count_ref[owner]
        count_ref[owner] = rank + 1
        send_ref[pl.ds(owner * CAP + rank, 1)] = cache[page : page + 1]


def attention_kernel(
    pages, me_ref, owner_ref, slot_ref, fill_ref, q_ref, cache_ref, fresh_ref, out_ref
):
    owners = owner_ref.shape[0]
    slots, _, heads, page_len, width = cache_ref.shape
    requests, steps, q_heads, _ = q_ref.shape
    group = q_heads // heads
    rows = requests * steps * group
    mine = (owner_ref[...] == me_ref[0]).astype(jnp.float32)
    before = (
        lax.broadcasted_iota(jnp.int32, (pages, pages), 0)
        < lax.broadcasted_iota(jnp.int32, (pages, pages), 1)
    ).astype(jnp.float32)
    rank = jnp.dot(mine, before, preferred_element_type=jnp.float32)
    code = (slot_ref[...] * (page_len + 1) + fill_ref[...]).astype(jnp.float32)
    columns = slots * page_len
    place = lax.broadcasted_iota(jnp.int32, (owners, columns), 1)
    source = lax.broadcasted_iota(jnp.int32, (owners, columns), 0)
    spread = jnp.zeros((owners, columns), jnp.float32)
    for c in range(CAP):
        held = jnp.sum(
            jnp.where((mine > 0.0) & (rank == float(c)), code, 0.0), axis=1, keepdims=True
        )
        spread = jnp.where(place // page_len == source * CAP + c, held, spread)
    line = jnp.sum(spread, axis=0, keepdims=True).astype(jnp.int32)
    request_of = line // (page_len + 1)
    fill_of = line - request_of * (page_len + 1)
    position = lax.broadcasted_iota(jnp.int32, (1, columns), 1) % page_len
    request_of = jnp.where(position < fill_of, request_of, -1)
    row_request = lax.broadcasted_iota(jnp.int32, (rows, 1), 0) // (steps * group)
    visible = row_request == request_of
    token = lax.broadcasted_iota(jnp.int32, (rows, 1), 0) // group
    first = row_request * steps
    fresh_at = lax.broadcasted_iota(jnp.int32, (1, fresh_ref.shape[2]), 1)
    fresh_visible = (fresh_at >= first) & (fresh_at <= token)
    factor = 1.0 / math.sqrt(width)
    contract = (((1,), (1,)), ((), ()))
    for head in range(heads):
        q = q_ref[:, :, head * group : (head + 1) * group, :].reshape(rows, width)
        keys = cache_ref[:, 0, head].reshape(columns, width)
        values = cache_ref[:, 1, head].reshape(columns, width)
        scores = lax.dot_general(q, keys, contract, preferred_element_type=jnp.float32) * factor
        fresh = (
            lax.dot_general(q, fresh_ref[0, head], contract, preferred_element_type=jnp.float32)
            * factor
        )
        scores = jnp.where(visible, scores, -jnp.inf)
        fresh = jnp.where(fresh_visible, fresh, -jnp.inf)
        peak = jnp.maximum(
            jnp.max(scores, axis=1, keepdims=True), jnp.max(fresh, axis=1, keepdims=True)
        )
        weight = jnp.exp(scores - peak)
        fresh_weight = jnp.exp(fresh - peak)
        total = jnp.sum(weight, axis=1, keepdims=True) + jnp.sum(
            fresh_weight, axis=1, keepdims=True
        )
        mixed = jnp.dot(
            weight.astype(jnp.bfloat16), values, preferred_element_type=jnp.float32
        ) + jnp.dot(
            fresh_weight.astype(jnp.bfloat16), fresh_ref[1, head], preferred_element_type=jnp.float32
        )
        out_ref[:, :, head * group : (head + 1) * group, :] = (
            (mixed / total).astype(out_ref.dtype).reshape(requests, steps, group, width)
        )


def pack_kernel(experts, core_ref, x_ref, route_ref, prob_ref, out_ref):
    half = x_ref.shape[1] // 2
    begin = pl.multiple_of(core_ref[0] * half, 128)
    out_ref[:, :half] = x_ref[:, pl.ds(begin, half)]
    shape = (x_ref.shape[0], out_ref.shape[1] - half)
    lane = lax.broadcasted_iota(jnp.int32, shape, 1)
    expert = lane % experts
    part = lane // experts
    dense = jnp.zeros(shape, jnp.float32)
    for k in range(route_ref.shape[1]):
        dense += jnp.where(route_ref[:, k : k + 1] == expert, prob_ref[:, k : k + 1], 0.0)
    high = dense.astype(jnp.bfloat16).astype(jnp.float32)
    middle = (dense - high).astype(jnp.bfloat16).astype(jnp.float32)
    low = dense - high - middle
    chosen = jnp.where(part == 0, high, jnp.where(part == 1, middle, low))
    out_ref[:, half:] = jnp.where(part < 3, chosen, 0.0).astype(out_ref.dtype)


def partial_kernel(blocks, core_ref, sr_ref, r2_ref, gate_ref, up_ref, gate_sum, up_sum):
    k = pl.program_id(0)
    x = jnp.concatenate([sr_ref[...], r2_ref[...]], axis=0)
    gate = jnp.dot(x, gate_ref[0], preferred_element_type=jnp.float32)
    up = jnp.dot(x, up_ref[0], preferred_element_type=jnp.float32)

    @pl.when(k == 0)
    def _():
        gate_sum[...] = gate
        up_sum[...] = up

    @pl.when(k > 0)
    def _():
        gate_sum[...] += gate
        up_sum[...] += up


def hidden_kernel(
    blocks, core_ref, sr_ref, r2_ref, gate_ref, up_ref, gate_part, up_part, out_ref, gate_sum, up_sum
):
    k = pl.program_id(0)
    group = sr_ref.shape[0] // 2
    x = jnp.concatenate(
        [sr_ref[:group], r2_ref[:group], sr_ref[group:], r2_ref[group:]], axis=0
    )
    gate = jnp.dot(x, gate_ref[0], preferred_element_type=jnp.float32)
    up = jnp.dot(x, up_ref[0], preferred_element_type=jnp.float32)

    @pl.when(k == 0)
    def _():
        gate_sum[...] = gate_part[...] + gate
        up_sum[...] = up_part[...] + up

    @pl.when(k > 0)
    def _():
        gate_sum[...] += gate
        up_sum[...] += up

    @pl.when(k == blocks - 1)
    def _():
        whole = gate_sum[...]
        out_ref[...] = (whole / (1.0 + jnp.exp(-whole)) * up_sum[...]).astype(out_ref.dtype)


def expert_front(core, own, other, w_gate, w_up, parts):
    group2 = own[0].shape[0]
    tokens = 2 * group2
    d, f = w_gate.shape[1:]
    depth = min(d // 2, 512)
    blocks = d // 2 // depth
    last = parts is not None
    rows = pl.BlockSpec((group2, depth), lambda k, core: (0, k))
    if last:
        weight = pl.BlockSpec((1, depth, f), lambda k, core: (0, (1 - core[0]) * blocks + k, 0))
    else:
        weight = pl.BlockSpec((1, depth, f), lambda k, core: (0, core[0] * blocks + k, 0))
    whole = pl.BlockSpec((tokens, f), lambda k, core: (0, 0))
    total = jax.ShapeDtypeStruct((tokens, f), jnp.float32)
    return pl.pallas_call(
        functools.partial(hidden_kernel if last else partial_kernel, blocks),
        grid_spec=pltpu.PrefetchScalarGridSpec(
            num_scalar_prefetch=1,
            grid=(blocks,),
            in_specs=[rows, rows, weight, weight] + ([whole, whole] if last else []),
            out_specs=whole if last else [whole, whole],
            scratch_shapes=[pltpu.VMEM((tokens, f), jnp.float32)] * 2 if last else [],
        ),
        out_shape=jax.ShapeDtypeStruct((tokens, f), jnp.bfloat16) if last else [total, total],
        compiler_params=pltpu.CompilerParams(vmem_limit_bytes=40 * MIB),
        cost_estimate=pl.CostEstimate(
            flops=2 * tokens * d * f,
            bytes_accessed=tokens * d + 2 * d * f + 8 * tokens * f,
            transcendentals=tokens * f if last else 0,
        ),
        name="expert_hidden" if last else "expert_partial",
    )(core, *(other if last else own), w_gate, w_up, *(parts or ()))


def back_kernel(send, experts, at_ref, own_ref, other_ref, down_ref, sr_ref, r2_ref, out_ref):
    f = own_ref.shape[1]
    group = sr_ref.shape[0] // 2
    core = at_ref[1]
    first = int(send)

    def rows(ref, a, b):
        return jnp.concatenate(
            [ref[a * group : (a + 1) * group], ref[b * group : (b + 1) * group]], axis=0
        )

    own = rows(own_ref, 1, 3) if send else rows(own_ref, 0, 2)
    other = rows(other_ref, 2, 3) if send else rows(other_ref, 0, 1)
    begin = pl.multiple_of(core * f, 128)
    rest = pl.multiple_of((1 - core) * f, 128)
    total = jnp.dot(own, down_ref[0, pl.ds(begin, f), :], preferred_element_type=jnp.float32)
    total += jnp.dot(other, down_ref[0, pl.ds(rest, f), :], preferred_element_type=jnp.float32)
    probs = jnp.concatenate(
        [
            sr_ref[first * group : (first + 1) * group].astype(jnp.float32),
            r2_ref[first * group : (first + 1) * group].astype(jnp.float32),
        ],
        axis=0,
    )
    lane = lax.broadcasted_iota(jnp.int32, probs.shape, 1)
    mine = lane % experts == at_ref[0]
    weight = jnp.sum(jnp.where(mine, probs, 0.0), axis=1, keepdims=True)
    out_ref[...] = (total * weight).astype(out_ref.dtype)


def expert_back(send, experts, at, own, other, w_down, sr, r2, lanes):
    tokens, f = own.shape
    group2 = sr.shape[0]
    width = w_down.shape[2]
    block = min(width, 512)
    begin = (sr.shape[1] - lanes) // lanes
    return pl.pallas_call(
        functools.partial(back_kernel, send, experts),
        grid=(width // block,),
        out_shape=jax.ShapeDtypeStruct((group2, width), jnp.bfloat16 if send else jnp.float32),
        in_specs=[
            smem(),
            pl.BlockSpec((tokens, f), lambda n: (0, 0)),
            pl.BlockSpec((tokens, f), lambda n: (0, 0)),
            pl.BlockSpec((1, 2 * f, block), lambda n: (0, 0, n)),
            pl.BlockSpec((group2, lanes), lambda n: (0, begin)),
            pl.BlockSpec((group2, lanes), lambda n: (0, begin)),
        ],
        out_specs=pl.BlockSpec((group2, block), lambda n: (0, n)),
        compiler_params=pltpu.CompilerParams(vmem_limit_bytes=40 * MIB),
        cost_estimate=pl.CostEstimate(
            flops=2 * tokens * f * width,
            bytes_accessed=2 * (2 * tokens * f + 2 * f * width + 2 * group2 * width),
            transcendentals=0,
        ),
        name="expert_back_send" if send else "expert_back_keep",
    )(at, own, other, w_down, sr, r2)


class Moves:
    def __init__(self, owners):
        self.owners = owners
        self.lines = owners // 4

    def go(self, x, where):
        perm = [
            (ep * 2 + core, where(ep, core)) for ep in range(self.owners) for core in range(2)
        ]
        return lax.ppermute(x, ("ep", "pd"), perm)

    def along_z(self, x, shift):
        return self.go(x, lambda ep, core: (ep + 4 * shift) % self.owners * 2 + core)

    def flip(self, x, turn):
        return self.go(x, lambda ep, core: (ep ^ (1 << ((core + turn) % 2))) * 2 + core)

    def cores(self, x):
        return self.go(x, lambda ep, core: ep * 2 + 1 - core)


def body(
    prompt_kv,
    page_owner,
    page_slot,
    page_fill,
    queries,
    new_kv,
    moe_input,
    expert_routes,
    route_probs,
    w_gate,
    w_up,
    w_down,
):
    owners = lax.axis_size("ep")
    me = lax.axis_index("ep").astype(jnp.int32)
    me_ref = me.reshape(1)
    core = lax.axis_index("pd").astype(jnp.int32)
    pages, _, page_len, heads, width = prompt_kv.shape
    requests, steps, q_heads, _ = queries.shape
    d = moe_input.shape[2]
    tokens = requests * steps
    slots = owners * CAP

    moves = Moves(owners)
    top = expert_routes.shape[2]
    lanes = -(-3 * owners // 128) * 128
    at = jnp.stack([me, core])
    own_core = core.reshape(1)
    mine = pl.pallas_call(
        functools.partial(pack_kernel, owners),
        out_shape=jax.ShapeDtypeStruct((tokens, d // 2 + lanes), jnp.bfloat16),
        in_specs=[smem()] + [vmem()] * 3,
        out_specs=vmem(),
        name="pack_tokens",
    )(
        own_core,
        moe_input.transpose(1, 0, 2).reshape(tokens, d),
        expert_routes.reshape(tokens, top),
        route_probs.transpose(1, 0, 2).reshape(tokens, top),
    )
    line = [mine] + [moves.along_z(mine, -shift) for shift in range(1, moves.lines)]
    line = jnp.concatenate(line, axis=0)
    sr = jnp.concatenate([line, moves.flip(line, 0)], axis=0)
    r2 = moves.flip(sr, 1)
    other_sr, other_r2 = moves.cores(sr), moves.cores(r2)

    send = pl.pallas_call(
        functools.partial(page_kernel, pages),
        out_shape=jax.ShapeDtypeStruct((slots, 2, heads, page_len, width), jnp.bfloat16),
        in_specs=[smem(), smem(), vmem()],
        out_specs=vmem(),
        scratch_shapes=[pltpu.SMEM((owners,), jnp.int32)],
        compiler_params=pltpu.CompilerParams(vmem_limit_bytes=40 * MIB),
        name="quantize_pages",
    )(me_ref, page_owner.reshape(-1), prompt_kv.transpose(0, 1, 3, 2, 4))
    cache = lax.all_to_all(send, "ep", split_axis=0, concat_axis=0, tiled=True)

    parts = expert_front(own_core, (sr, r2), None, w_gate, w_up, None)
    hidden = expert_front(own_core, (sr, r2), (other_sr, other_r2), w_gate, w_up, parts)
    other_hidden = moves.cores(hidden)
    sent = expert_back(True, owners, at, hidden, other_hidden, w_down, sr, r2, lanes)
    kept = expert_back(False, owners, at, hidden, other_hidden, w_down, sr, r2, lanes)
    group = moves.lines * tokens
    kept = kept + moves.flip(sent, 0).astype(jnp.float32)
    kept = kept[:group] + moves.flip(kept[group:].astype(jnp.bfloat16), 1).astype(jnp.float32)
    moe = kept[:tokens]
    for shift in range(1, moves.lines):
        block = kept[shift * tokens : (shift + 1) * tokens].astype(jnp.bfloat16)
        moe = moe + moves.along_z(block, shift).astype(jnp.float32)
    moe = moe.astype(jnp.bfloat16)
    moe_out = moe.reshape(steps, requests, d // 2).transpose(1, 0, 2)

    fresh = new_kv.transpose(2, 3, 0, 1, 4).reshape(2, heads, tokens, width)
    fresh = jnp.pad(fresh, ((0, 0), (0, 0), (0, 128 - tokens), (0, 0)))
    attn_out = pl.pallas_call(
        functools.partial(attention_kernel, pages),
        out_shape=jax.ShapeDtypeStruct(queries.shape, jnp.bfloat16),
        in_specs=[smem()] + [vmem()] * 6,
        out_specs=vmem(),
        compiler_params=pltpu.CompilerParams(vmem_limit_bytes=48 * MIB),
        name="attention",
    )(
        me_ref,
        page_owner.reshape(owners, pages),
        page_slot.reshape(owners, pages),
        page_fill.reshape(owners, pages),
        queries,
        cache,
        fresh,
    )
    return (attn_out, moe_out)


def solution(mesh):
    return jax.shard_map(
        body,
        mesh=mesh,
        in_specs=(
            P(("grp", "ep"), None, None, "pd", None),
            P("grp", None),
            P("grp"),
            P("grp"),
            P(("grp", "ep"), None, "pd", None),
            P(("grp", "ep"), None, None, "pd", None),
            P(("grp", "ep"), None, None),
            P(None, ("grp", "ep"), None),
            P(("grp", "ep"), None, None),
            P("ep", None, "pd"),
            P("ep", None, "pd"),
            P("ep", None, "pd"),
        ),
        out_specs=(P(("grp", "ep"), None, "pd", None), P(("grp", "ep"), None, "pd")),
        check_vma=False,
    )
```

```python
import functools
import math

import jax
import jax.numpy as jnp
from jax import lax
from jax.experimental import pallas as pl
from jax.experimental.pallas import tpu as pltpu
from jax.sharding import PartitionSpec as P

CAP = 2
LIMIT = 448.0
MIB = 1024 * 1024


def vmem():
    return pl.BlockSpec(memory_space=pltpu.VMEM)


def smem():
    return pl.BlockSpec(memory_space=pltpu.SMEM)


def hbm():
    return pl.BlockSpec(memory_space=pltpu.HBM)


def page_kernel(pages, me_ref, owner_ref, kv_ref, send_ref, count_ref):
    values = kv_ref[...].astype(jnp.float32)
    largest = jnp.max(jnp.abs(values), axis=(3, 4), keepdims=True)
    scale = jnp.full(largest.shape, 2.0 ** (-16), jnp.float32)
    inverse = jnp.full(largest.shape, 2.0**16, jnp.float32)
    for exponent in range(-16, 4):
        exceeds = largest > LIMIT * 2.0**exponent
        scale = jnp.where(exceeds, scale * 2.0, scale)
        inverse = jnp.where(exceeds, inverse * 0.5, inverse)
    scaled = values * inverse
    magnitude = jnp.abs(scaled)
    step = jnp.full(scaled.shape, 2.0 ** (-9), jnp.float32)
    back = jnp.full(scaled.shape, 2.0**9, jnp.float32)
    for exponent in range(-5, 9):
        exceeds = magnitude >= 2.0**exponent
        step = jnp.where(exceeds, step * 2.0, step)
        back = jnp.where(exceeds, back * 0.5, back)
    levels = jnp.minimum(jnp.floor(magnitude * back + 0.5) * step, LIMIT)
    cache = (jnp.where(scaled < 0.0, -levels, levels) * scale).astype(jnp.bfloat16)

    send_ref[...] = jnp.zeros(send_ref.shape, send_ref.dtype)

    def clear(o, carry):
        count_ref[o] = 0
        return carry

    lax.fori_loop(0, count_ref.shape[0], clear, 0)
    first = me_ref[0] * pages
    for page in range(pages):
        owner = owner_ref[first + page]
        rank = count_ref[owner]
        count_ref[owner] = rank + 1
        send_ref[pl.ds(owner * CAP + rank, 1)] = cache[page : page + 1]


def attention_kernel(
    pages, me_ref, owner_ref, slot_ref, fill_ref, q_ref, cache_ref, fresh_ref, out_ref
):
    owners = owner_ref.shape[0]
    slots, _, heads, page_len, width = cache_ref.shape
    requests, steps, q_heads, _ = q_ref.shape
    group = q_heads // heads
    rows = requests * steps * group
    mine = (owner_ref[...] == me_ref[0]).astype(jnp.float32)
    before = (
        lax.broadcasted_iota(jnp.int32, (pages, pages), 0)
        < lax.broadcasted_iota(jnp.int32, (pages, pages), 1)
    ).astype(jnp.float32)
    rank = jnp.dot(mine, before, preferred_element_type=jnp.float32)
    code = (slot_ref[...] * (page_len + 1) + fill_ref[...]).astype(jnp.float32)
    columns = slots * page_len
    place = lax.broadcasted_iota(jnp.int32, (owners, columns), 1)
    source = lax.broadcasted_iota(jnp.int32, (owners, columns), 0)
    spread = jnp.zeros((owners, columns), jnp.float32)
    for c in range(CAP):
        held = jnp.sum(
            jnp.where((mine > 0.0) & (rank == float(c)), code, 0.0), axis=1, keepdims=True
        )
        spread = jnp.where(place // page_len == source * CAP + c, held, spread)
    line = jnp.sum(spread, axis=0, keepdims=True).astype(jnp.int32)
    request_of = line // (page_len + 1)
    fill_of = line - request_of * (page_len + 1)
    position = lax.broadcasted_iota(jnp.int32, (1, columns), 1) % page_len
    request_of = jnp.where(position < fill_of, request_of, -1)
    row_request = lax.broadcasted_iota(jnp.int32, (rows, 1), 0) // (steps * group)
    visible = row_request == request_of
    token = lax.broadcasted_iota(jnp.int32, (rows, 1), 0) // group
    first = row_request * steps
    fresh_at = lax.broadcasted_iota(jnp.int32, (1, fresh_ref.shape[2]), 1)
    fresh_visible = (fresh_at >= first) & (fresh_at <= token)
    factor = 1.0 / math.sqrt(width)
    contract = (((1,), (1,)), ((), ()))
    for head in range(heads):
        q = q_ref[:, :, head * group : (head + 1) * group, :].reshape(rows, width)
        keys = cache_ref[:, 0, head].reshape(columns, width)
        values = cache_ref[:, 1, head].reshape(columns, width)
        scores = lax.dot_general(q, keys, contract, preferred_element_type=jnp.float32) * factor
        fresh = (
            lax.dot_general(q, fresh_ref[0, head], contract, preferred_element_type=jnp.float32)
            * factor
        )
        scores = jnp.where(visible, scores, -jnp.inf)
        fresh = jnp.where(fresh_visible, fresh, -jnp.inf)
        peak = jnp.maximum(
            jnp.max(scores, axis=1, keepdims=True), jnp.max(fresh, axis=1, keepdims=True)
        )
        weight = jnp.exp(scores - peak)
        fresh_weight = jnp.exp(fresh - peak)
        total = jnp.sum(weight, axis=1, keepdims=True) + jnp.sum(
            fresh_weight, axis=1, keepdims=True
        )
        mixed = jnp.dot(
            weight.astype(jnp.bfloat16), values, preferred_element_type=jnp.float32
        ) + jnp.dot(
            fresh_weight.astype(jnp.bfloat16), fresh_ref[1, head], preferred_element_type=jnp.float32
        )
        out_ref[:, :, head * group : (head + 1) * group, :] = (
            (mixed / total).astype(out_ref.dtype).reshape(requests, steps, group, width)
        )


def pack_kernel(experts, core_ref, x_ref, route_ref, prob_ref, out_ref):
    half = x_ref.shape[1] // 2
    begin = pl.multiple_of(core_ref[0] * half, 128)
    out_ref[:, :half] = x_ref[:, pl.ds(begin, half)]
    shape = (x_ref.shape[0], out_ref.shape[1] - half)
    lane = lax.broadcasted_iota(jnp.int32, shape, 1)
    expert = lane % experts
    part = lane // experts
    dense = jnp.zeros(shape, jnp.float32)
    for k in range(route_ref.shape[1]):
        dense += jnp.where(route_ref[:, k : k + 1] == expert, prob_ref[:, k : k + 1], 0.0)
    high = dense.astype(jnp.bfloat16).astype(jnp.float32)
    middle = (dense - high).astype(jnp.bfloat16).astype(jnp.float32)
    low = dense - high - middle
    chosen = jnp.where(part == 0, high, jnp.where(part == 1, middle, low))
    out_ref[:, half:] = jnp.where(part < 3, chosen, 0.0).astype(out_ref.dtype)


def weight_copies(half, core, gate_ref, up_ref, held, sems):
    depth = half // sems.shape[1]
    pairs = []
    for c in range(sems.shape[1]):
        rows = pl.ds(pl.multiple_of(core * half + c * depth, 128), depth)
        pairs.append(
            [
                pltpu.make_async_copy(
                    ref.at[0, rows], held.at[i, pl.ds(c * depth, depth)], sems.at[i, c]
                )
                for i, ref in enumerate((gate_ref, up_ref))
            ]
        )
    for pair in pairs:
        for copy in pair:
            copy.start()
    return pairs, depth


def partial_kernel(core_ref, sr_ref, r2_ref, gate_ref, up_ref, gate_sum, up_sum, held, sems):
    half = held.shape[1]
    pairs, depth = weight_copies(half, core_ref[0], gate_ref, up_ref, held, sems)
    for c, pair in enumerate(pairs):
        at = slice(c * depth, (c + 1) * depth)
        x = jnp.concatenate([sr_ref[:, at], r2_ref[:, at]], axis=0)
        for i, total in enumerate((gate_sum, up_sum)):
            pair[i].wait()
            part = jnp.dot(x, held[i, at], preferred_element_type=jnp.float32)
            total[...] = part if c == 0 else total[...] + part


def hidden_kernel(
    core_ref, sr_ref, r2_ref, gate_ref, up_ref, gate_part, up_part, out_ref, held, sems, sums
):
    half = held.shape[1]
    group = sr_ref.shape[0] // 2
    pairs, depth = weight_copies(half, 1 - core_ref[0], gate_ref, up_ref, held, sems)
    last = len(pairs) - 1
    for c, pair in enumerate(pairs):
        at = slice(c * depth, (c + 1) * depth)
        x = jnp.concatenate(
            [sr_ref[:group, at], r2_ref[:group, at], sr_ref[group:, at], r2_ref[group:, at]],
            axis=0,
        )
        for i, start in enumerate((gate_part, up_part)):
            pair[i].wait()
            part = jnp.dot(x, held[i, at], preferred_element_type=jnp.float32)
            sums[i] = (start[...] if c == 0 else sums[i]) + part
    gate = sums[0]
    out_ref[...] = (gate / (1.0 + jnp.exp(-gate)) * sums[1]).astype(out_ref.dtype)


def expert_front(core, rows, w_gate, w_up, parts):
    tokens = 2 * rows[0].shape[0]
    d, f = w_gate.shape[1:]
    last = parts is not None
    total = jax.ShapeDtypeStruct((tokens, f), jnp.float32)
    scratch = [pltpu.VMEM((2, d // 2, f), jnp.bfloat16), pltpu.SemaphoreType.DMA((2, 4))]
    return pl.pallas_call(
        hidden_kernel if last else partial_kernel,
        in_specs=[smem(), vmem(), vmem(), hbm(), hbm()] + ([vmem(), vmem()] if last else []),
        out_specs=vmem() if last else [vmem(), vmem()],
        scratch_shapes=scratch + ([pltpu.VMEM((2, tokens, f), jnp.float32)] if last else []),
        out_shape=jax.ShapeDtypeStruct((tokens, f), jnp.bfloat16) if last else [total, total],
        compiler_params=pltpu.CompilerParams(vmem_limit_bytes=40 * MIB),
        cost_estimate=pl.CostEstimate(
            flops=2 * tokens * d * f,
            bytes_accessed=tokens * d + 2 * d * f + 8 * tokens * f,
            transcendentals=tokens * f if last else 0,
        ),
        name="expert_hidden" if last else "expert_partial",
    )(core, *rows, w_gate, w_up, *(parts or ()))


def back_kernel(
    send, experts, lanes, at_ref, own_ref, other_ref, sr_ref, r2_ref, down_ref, out_ref, held, sems
):
    chunks = sems.shape[0]
    block = held.shape[1] // chunks
    copies = [
        pltpu.make_async_copy(
            down_ref.at[0, :, pl.ds(c * block, block)],
            held.at[:, pl.ds(c * block, block)],
            sems.at[c],
        )
        for c in range(chunks)
    ]
    for copy in copies:
        copy.start()
    f = own_ref.shape[1]
    group = sr_ref.shape[0] // 2
    core = at_ref[1]
    first = int(send)

    def rows(ref, a, b):
        return jnp.concatenate(
            [ref[a * group : (a + 1) * group], ref[b * group : (b + 1) * group]], axis=0
        )

    own = rows(own_ref, 1, 3) if send else rows(own_ref, 0, 2)
    other = rows(other_ref, 2, 3) if send else rows(other_ref, 0, 1)
    begin = pl.multiple_of(core * f, 128)
    rest = pl.multiple_of((1 - core) * f, 128)
    tail = slice(sr_ref.shape[1] - lanes, sr_ref.shape[1])
    picked = slice(first * group, (first + 1) * group)
    probs = jnp.concatenate(
        [sr_ref[picked, tail].astype(jnp.float32), r2_ref[picked, tail].astype(jnp.float32)],
        axis=0,
    )
    lane = lax.broadcasted_iota(jnp.int32, probs.shape, 1)
    mine = lane % experts == at_ref[0]
    weight = jnp.sum(jnp.where(mine, probs, 0.0), axis=1, keepdims=True)
    for c, copy in enumerate(copies):
        at = slice(c * block, (c + 1) * block)
        copy.wait()
        total = jnp.dot(own, held[pl.ds(begin, f), at], preferred_element_type=jnp.float32)
        total += jnp.dot(other, held[pl.ds(rest, f), at], preferred_element_type=jnp.float32)
        out_ref[:, at] = (total * weight).astype(out_ref.dtype)


def expert_back(send, experts, at, own, other, w_down, sr, r2, lanes):
    tokens, f = own.shape
    group2 = sr.shape[0]
    width = w_down.shape[2]
    return pl.pallas_call(
        functools.partial(back_kernel, send, experts, lanes),
        out_shape=jax.ShapeDtypeStruct((group2, width), jnp.bfloat16 if send else jnp.float32),
        in_specs=[smem()] + [vmem()] * 4 + [hbm()],
        out_specs=vmem(),
        scratch_shapes=[
            pltpu.VMEM(w_down.shape[1:], jnp.bfloat16),
            pltpu.SemaphoreType.DMA((4,)),
        ],
        compiler_params=pltpu.CompilerParams(vmem_limit_bytes=40 * MIB),
        cost_estimate=pl.CostEstimate(
            flops=2 * tokens * f * width,
            bytes_accessed=2 * (2 * tokens * f + 2 * f * width + 2 * group2 * width),
            transcendentals=0,
        ),
        name="expert_back_send" if send else "expert_back_keep",
    )(at, own, other, sr, r2, w_down)


class Moves:
    def __init__(self, owners):
        self.owners = owners
        self.lines = owners // 4

    def go(self, x, where):
        perm = [
            (ep * 2 + core, where(ep, core)) for ep in range(self.owners) for core in range(2)
        ]
        return lax.ppermute(x, ("ep", "pd"), perm)

    def along_z(self, x, shift):
        return self.go(x, lambda ep, core: (ep + 4 * shift) % self.owners * 2 + core)

    def flip(self, x, turn):
        return self.go(x, lambda ep, core: (ep ^ (1 << ((core + turn) % 2))) * 2 + core)

    def cores(self, x):
        return self.go(x, lambda ep, core: ep * 2 + 1 - core)


def body(
    prompt_kv,
    page_owner,
    page_slot,
    page_fill,
    queries,
    new_kv,
    moe_input,
    expert_routes,
    route_probs,
    w_gate,
    w_up,
    w_down,
):
    owners = lax.axis_size("ep")
    me = lax.axis_index("ep").astype(jnp.int32)
    me_ref = me.reshape(1)
    core = lax.axis_index("pd").astype(jnp.int32)
    pages, _, page_len, heads, width = prompt_kv.shape
    requests, steps, q_heads, _ = queries.shape
    d = moe_input.shape[2]
    tokens = requests * steps
    slots = owners * CAP

    moves = Moves(owners)
    top = expert_routes.shape[2]
    lanes = -(-3 * owners // 128) * 128
    at = jnp.stack([me, core])
    own_core = core.reshape(1)
    mine = pl.pallas_call(
        functools.partial(pack_kernel, owners),
        out_shape=jax.ShapeDtypeStruct((tokens, d // 2 + lanes), jnp.bfloat16),
        in_specs=[smem()] + [vmem()] * 3,
        out_specs=vmem(),
        name="pack_tokens",
    )(
        own_core,
        moe_input.transpose(1, 0, 2).reshape(tokens, d),
        expert_routes.reshape(tokens, top),
        route_probs.transpose(1, 0, 2).reshape(tokens, top),
    )
    send = pl.pallas_call(
        functools.partial(page_kernel, pages),
        out_shape=jax.ShapeDtypeStruct((slots, 2, heads, page_len, width), jnp.bfloat16),
        in_specs=[smem(), smem(), vmem()],
        out_specs=vmem(),
        scratch_shapes=[pltpu.SMEM((owners,), jnp.int32)],
        compiler_params=pltpu.CompilerParams(vmem_limit_bytes=40 * MIB),
        name="quantize_pages",
    )(me_ref, page_owner.reshape(-1), prompt_kv.transpose(0, 1, 3, 2, 4))
    line = [mine] + [moves.along_z(mine, -shift) for shift in range(1, moves.lines)]
    line = jnp.concatenate(line, axis=0)
    fresh = new_kv.transpose(2, 3, 0, 1, 4).reshape(2, heads, tokens, width)
    fresh = jnp.pad(fresh, ((0, 0), (0, 0), (0, 128 - tokens), (0, 0)))
    tables = [t.reshape(owners, pages) for t in (page_owner, page_slot, page_fill)]
    line, send, fresh, tables = lax.optimization_barrier((line, send, fresh, tables))
    sr = jnp.concatenate([line, moves.flip(line, 0)], axis=0)
    r2 = moves.flip(sr, 1)
    cache = lax.all_to_all(send, "ep", split_axis=0, concat_axis=0, tiled=True)
    other_sr, other_r2 = moves.cores(sr), moves.cores(r2)

    parts = expert_front(own_core, (sr, r2), w_gate, w_up, None)
    hidden = expert_front(own_core, (other_sr, other_r2), w_gate, w_up, parts)
    other_hidden = moves.cores(hidden)
    sent = expert_back(True, owners, at, hidden, other_hidden, w_down, sr, r2, lanes)
    kept = expert_back(False, owners, at, hidden, other_hidden, w_down, sr, r2, lanes)
    attn_out = pl.pallas_call(
        functools.partial(attention_kernel, pages),
        out_shape=jax.ShapeDtypeStruct(queries.shape, jnp.bfloat16),
        in_specs=[smem()] + [vmem()] * 6,
        out_specs=vmem(),
        compiler_params=pltpu.CompilerParams(vmem_limit_bytes=48 * MIB),
        name="attention",
    )(
        me_ref,
        *tables,
        queries,
        cache,
        fresh,
    )
    group = moves.lines * tokens
    kept = kept + moves.flip(sent, 0).astype(jnp.float32)
    kept, attn_out = lax.optimization_barrier((kept, attn_out))
    kept = kept[:group] + moves.flip(kept[group:].astype(jnp.bfloat16), 1).astype(jnp.float32)
    moe = kept[:tokens]
    for shift in range(1, moves.lines):
        block = kept[shift * tokens : (shift + 1) * tokens].astype(jnp.bfloat16)
        moe = moe + moves.along_z(block, shift).astype(jnp.float32)
    moe = moe.astype(jnp.bfloat16)
    moe_out = moe.reshape(steps, requests, d // 2).transpose(1, 0, 2)

    return (attn_out, moe_out)


def solution(mesh):
    return jax.shard_map(
        body,
        mesh=mesh,
        in_specs=(
            P(("grp", "ep"), None, None, "pd", None),
            P("grp", None),
            P("grp"),
            P("grp"),
            P(("grp", "ep"), None, "pd", None),
            P(("grp", "ep"), None, None, "pd", None),
            P(("grp", "ep"), None, None),
            P(None, ("grp", "ep"), None),
            P(("grp", "ep"), None, None),
            P("ep", None, "pd"),
            P("ep", None, "pd"),
            P("ep", None, "pd"),
        ),
        out_specs=(P(("grp", "ep"), None, "pd", None), P(("grp", "ep"), None, "pd")),
        check_vma=False,
    )
```

```python
import functools
import math

import jax
import jax.numpy as jnp
from jax import lax
from jax.experimental import pallas as pl
from jax.experimental.pallas import tpu as pltpu
from jax.sharding import PartitionSpec as P

CAP = 2
LIMIT = 448.0
MIB = 1024 * 1024


def vmem():
    return pl.BlockSpec(memory_space=pltpu.VMEM)


def smem():
    return pl.BlockSpec(memory_space=pltpu.SMEM)


def page_kernel(pages, me_ref, owner_ref, kv_ref, send_ref, count_ref):
    values = kv_ref[...].astype(jnp.float32)
    largest = jnp.max(jnp.abs(values), axis=(3, 4), keepdims=True)
    scale = jnp.full(largest.shape, 2.0 ** (-16), jnp.float32)
    inverse = jnp.full(largest.shape, 2.0**16, jnp.float32)
    for exponent in range(-16, 4):
        exceeds = largest > LIMIT * 2.0**exponent
        scale = jnp.where(exceeds, scale * 2.0, scale)
        inverse = jnp.where(exceeds, inverse * 0.5, inverse)
    scaled = values * inverse
    magnitude = jnp.abs(scaled)
    step = jnp.full(scaled.shape, 2.0 ** (-9), jnp.float32)
    back = jnp.full(scaled.shape, 2.0**9, jnp.float32)
    for exponent in range(-5, 9):
        exceeds = magnitude >= 2.0**exponent
        step = jnp.where(exceeds, step * 2.0, step)
        back = jnp.where(exceeds, back * 0.5, back)
    levels = jnp.minimum(jnp.floor(magnitude * back + 0.5) * step, LIMIT)
    cache = (jnp.where(scaled < 0.0, -levels, levels) * scale).astype(jnp.bfloat16)

    send_ref[...] = jnp.zeros(send_ref.shape, send_ref.dtype)

    def clear(o, carry):
        count_ref[o] = 0
        return carry

    lax.fori_loop(0, count_ref.shape[0], clear, 0)
    first = me_ref[0] * pages
    for page in range(pages):
        owner = owner_ref[first + page]
        rank = count_ref[owner]
        count_ref[owner] = rank + 1
        send_ref[pl.ds(owner * CAP + rank, 1)] = cache[page : page + 1]


def attention_kernel(
    pages, me_ref, owner_ref, slot_ref, fill_ref, q_ref, cache_ref, fresh_ref, out_ref
):
    owners = owner_ref.shape[0]
    slots, _, heads, page_len, width = cache_ref.shape
    requests, steps, q_heads, _ = q_ref.shape
    group = q_heads // heads
    rows = requests * steps * group
    mine = (owner_ref[...] == me_ref[0]).astype(jnp.float32)
    before = (
        lax.broadcasted_iota(jnp.int32, (pages, pages), 0)
        < lax.broadcasted_iota(jnp.int32, (pages, pages), 1)
    ).astype(jnp.float32)
    rank = jnp.dot(mine, before, preferred_element_type=jnp.float32)
    code = (slot_ref[...] * (page_len + 1) + fill_ref[...]).astype(jnp.float32)
    columns = slots * page_len
    place = lax.broadcasted_iota(jnp.int32, (owners, columns), 1)
    source = lax.broadcasted_iota(jnp.int32, (owners, columns), 0)
    spread = jnp.zeros((owners, columns), jnp.float32)
    for c in range(CAP):
        held = jnp.sum(
            jnp.where((mine > 0.0) & (rank == float(c)), code, 0.0), axis=1, keepdims=True
        )
        spread = jnp.where(place // page_len == source * CAP + c, held, spread)
    line = jnp.sum(spread, axis=0, keepdims=True).astype(jnp.int32)
    request_of = line // (page_len + 1)
    fill_of = line - request_of * (page_len + 1)
    position = lax.broadcasted_iota(jnp.int32, (1, columns), 1) % page_len
    request_of = jnp.where(position < fill_of, request_of, -1)
    row_request = lax.broadcasted_iota(jnp.int32, (rows, 1), 0) // (steps * group)
    visible = row_request == request_of
    token = lax.broadcasted_iota(jnp.int32, (rows, 1), 0) // group
    first = row_request * steps
    fresh_at = lax.broadcasted_iota(jnp.int32, (1, fresh_ref.shape[2]), 1)
    fresh_visible = (fresh_at >= first) & (fresh_at <= token)
    factor = 1.0 / math.sqrt(width)
    contract = (((1,), (1,)), ((), ()))
    for head in range(heads):
        q = q_ref[:, :, head * group : (head + 1) * group, :].reshape(rows, width)
        keys = cache_ref[:, 0, head].reshape(columns, width)
        values = cache_ref[:, 1, head].reshape(columns, width)
        scores = lax.dot_general(q, keys, contract, preferred_element_type=jnp.float32) * factor
        fresh = (
            lax.dot_general(q, fresh_ref[0, head], contract, preferred_element_type=jnp.float32)
            * factor
        )
        scores = jnp.where(visible, scores, -jnp.inf)
        fresh = jnp.where(fresh_visible, fresh, -jnp.inf)
        peak = jnp.maximum(
            jnp.max(scores, axis=1, keepdims=True), jnp.max(fresh, axis=1, keepdims=True)
        )
        weight = jnp.exp(scores - peak)
        fresh_weight = jnp.exp(fresh - peak)
        total = jnp.sum(weight, axis=1, keepdims=True) + jnp.sum(
            fresh_weight, axis=1, keepdims=True
        )
        mixed = jnp.dot(
            weight.astype(jnp.bfloat16), values, preferred_element_type=jnp.float32
        ) + jnp.dot(
            fresh_weight.astype(jnp.bfloat16), fresh_ref[1, head], preferred_element_type=jnp.float32
        )
        out_ref[:, :, head * group : (head + 1) * group, :] = (
            (mixed / total).astype(out_ref.dtype).reshape(requests, steps, group, width)
        )


def pack_kernel(experts, core_ref, x_ref, route_ref, prob_ref, out_ref):
    half = x_ref.shape[1] // 2
    begin = pl.multiple_of(core_ref[0] * half, 128)
    out_ref[:, :half] = x_ref[:, pl.ds(begin, half)]
    shape = (x_ref.shape[0], out_ref.shape[1] - half)
    lane = lax.broadcasted_iota(jnp.int32, shape, 1)
    expert = lane % experts
    part = lane // experts
    dense = jnp.zeros(shape, jnp.float32)
    for k in range(route_ref.shape[1]):
        dense += jnp.where(route_ref[:, k : k + 1] == expert, prob_ref[:, k : k + 1], 0.0)
    high = dense.astype(jnp.bfloat16).astype(jnp.float32)
    middle = (dense - high).astype(jnp.bfloat16).astype(jnp.float32)
    low = dense - high - middle
    chosen = jnp.where(part == 0, high, jnp.where(part == 1, middle, low))
    out_ref[:, half:] = jnp.where(part < 3, chosen, 0.0).astype(out_ref.dtype)


def partial_kernel(chunks, core_ref, sr_ref, r2_ref, gate_ref, up_ref, gate_sum, up_sum):
    half = gate_ref.shape[1] // 2
    depth = half // chunks
    for c in range(chunks):
        at = slice(c * depth, (c + 1) * depth)
        rows = pl.ds(pl.multiple_of(core_ref[0] * half + c * depth, 128), depth)
        x = jnp.concatenate([sr_ref[:, at], r2_ref[:, at]], axis=0)
        for weight, total in ((gate_ref, gate_sum), (up_ref, up_sum)):
            part = jnp.dot(x, weight[0, rows], preferred_element_type=jnp.float32)
            total[...] = part if c == 0 else total[...] + part


def hidden_kernel(
    chunks, core_ref, sr_ref, r2_ref, gate_ref, up_ref, gate_part, up_part, out_ref, sums
):
    half = gate_ref.shape[1] // 2
    depth = half // chunks
    group = sr_ref.shape[0] // 2
    for c in range(chunks):
        at = slice(c * depth, (c + 1) * depth)
        rows = pl.ds(pl.multiple_of((1 - core_ref[0]) * half + c * depth, 128), depth)
        x = jnp.concatenate(
            [sr_ref[:group, at], r2_ref[:group, at], sr_ref[group:, at], r2_ref[group:, at]],
            axis=0,
        )
        for i, (weight, start) in enumerate(((gate_ref, gate_part), (up_ref, up_part))):
            part = jnp.dot(x, weight[0, rows], preferred_element_type=jnp.float32)
            sums[i] = (start[...] if c == 0 else sums[i]) + part
    gate = sums[0]
    out_ref[...] = (gate / (1.0 + jnp.exp(-gate)) * sums[1]).astype(out_ref.dtype)


def room(*arrays):
    return sum(math.prod(a.shape) * a.dtype.itemsize for a in arrays) * 9 // 8 + 4 * MIB


def expert_front(core, rows, w_gate, w_up, parts):
    tokens = 2 * rows[0].shape[0]
    d, f = w_gate.shape[1:]
    last = parts is not None
    total = jax.ShapeDtypeStruct((tokens, f), jnp.float32)
    scratch = [pltpu.VMEM((2, tokens, f), jnp.float32)] if last else []
    return pl.pallas_call(
        functools.partial(hidden_kernel if last else partial_kernel, 4),
        in_specs=[smem()] + [vmem()] * (6 if last else 4),
        out_specs=vmem() if last else [vmem(), vmem()],
        scratch_shapes=scratch,
        out_shape=jax.ShapeDtypeStruct((tokens, f), jnp.bfloat16) if last else [total, total],
        compiler_params=pltpu.CompilerParams(
            vmem_limit_bytes=room(*rows, w_gate, w_up, *[total] * (5 if last else 2))
        ),
        cost_estimate=pl.CostEstimate(
            flops=2 * tokens * d * f,
            bytes_accessed=tokens * d + 2 * d * f + 8 * tokens * f,
            transcendentals=tokens * f if last else 0,
        ),
        name="expert_hidden" if last else "expert_partial",
    )(core, *rows, w_gate, w_up, *(parts or ()))


def back_kernel(
    send, experts, lanes, chunks, at_ref, own_ref, other_ref, sr_ref, r2_ref, down_ref, out_ref
):
    block = down_ref.shape[2] // chunks
    f = own_ref.shape[1]
    group = sr_ref.shape[0] // 2
    core = at_ref[1]
    first = int(send)

    def rows(ref, a, b):
        return jnp.concatenate(
            [ref[a * group : (a + 1) * group], ref[b * group : (b + 1) * group]], axis=0
        )

    own = rows(own_ref, 1, 3) if send else rows(own_ref, 0, 2)
    other = rows(other_ref, 2, 3) if send else rows(other_ref, 0, 1)
    begin = pl.multiple_of(core * f, 128)
    rest = pl.multiple_of((1 - core) * f, 128)
    tail = slice(sr_ref.shape[1] - lanes, sr_ref.shape[1])
    picked = slice(first * group, (first + 1) * group)
    probs = jnp.concatenate(
        [sr_ref[picked, tail].astype(jnp.float32), r2_ref[picked, tail].astype(jnp.float32)],
        axis=0,
    )
    lane = lax.broadcasted_iota(jnp.int32, probs.shape, 1)
    mine = lane % experts == at_ref[0]
    weight = jnp.sum(jnp.where(mine, probs, 0.0), axis=1, keepdims=True)
    for c in range(chunks):
        at = slice(c * block, (c + 1) * block)
        total = jnp.dot(own, down_ref[0, pl.ds(begin, f), at], preferred_element_type=jnp.float32)
        total += jnp.dot(
            other, down_ref[0, pl.ds(rest, f), at], preferred_element_type=jnp.float32
        )
        out_ref[:, at] = (total * weight).astype(out_ref.dtype)


def expert_back(send, experts, at, own, other, w_down, sr, r2, lanes):
    tokens, f = own.shape
    group2 = sr.shape[0]
    width = w_down.shape[2]
    out = jax.ShapeDtypeStruct((group2, width), jnp.bfloat16 if send else jnp.float32)
    return pl.pallas_call(
        functools.partial(back_kernel, send, experts, lanes, 4),
        out_shape=out,
        in_specs=[smem()] + [vmem()] * 5,
        out_specs=vmem(),
        compiler_params=pltpu.CompilerParams(
            vmem_limit_bytes=room(own, other, w_down, sr, r2, out, out)
        ),
        cost_estimate=pl.CostEstimate(
            flops=2 * tokens * f * width,
            bytes_accessed=2 * (2 * tokens * f + 2 * f * width + 2 * group2 * width),
            transcendentals=0,
        ),
        name="expert_back_send" if send else "expert_back_keep",
    )(at, own, other, sr, r2, w_down)


class Moves:
    def __init__(self, owners):
        self.owners = owners
        self.lines = owners // 4

    def go(self, x, where):
        perm = [
            (ep * 2 + core, where(ep, core)) for ep in range(self.owners) for core in range(2)
        ]
        return lax.ppermute(x, ("ep", "pd"), perm)

    def along_z(self, x, shift):
        return self.go(x, lambda ep, core: (ep + 4 * shift) % self.owners * 2 + core)

    def flip(self, x, turn):
        return self.go(x, lambda ep, core: (ep ^ (1 << ((core + turn) % 2))) * 2 + core)

    def cores(self, x):
        return self.go(x, lambda ep, core: ep * 2 + 1 - core)


def body(
    prompt_kv,
    page_owner,
    page_slot,
    page_fill,
    queries,
    new_kv,
    moe_input,
    expert_routes,
    route_probs,
    w_gate,
    w_up,
    w_down,
):
    owners = lax.axis_size("ep")
    me = lax.axis_index("ep").astype(jnp.int32)
    me_ref = me.reshape(1)
    core = lax.axis_index("pd").astype(jnp.int32)
    pages, _, page_len, heads, width = prompt_kv.shape
    requests, steps, q_heads, _ = queries.shape
    d = moe_input.shape[2]
    tokens = requests * steps
    slots = owners * CAP

    moves = Moves(owners)
    top = expert_routes.shape[2]
    lanes = -(-3 * owners // 128) * 128
    at = jnp.stack([me, core])
    own_core = core.reshape(1)
    mine = pl.pallas_call(
        functools.partial(pack_kernel, owners),
        out_shape=jax.ShapeDtypeStruct((tokens, d // 2 + lanes), jnp.bfloat16),
        in_specs=[smem()] + [vmem()] * 3,
        out_specs=vmem(),
        name="pack_tokens",
    )(
        own_core,
        moe_input.transpose(1, 0, 2).reshape(tokens, d),
        expert_routes.reshape(tokens, top),
        route_probs.transpose(1, 0, 2).reshape(tokens, top),
    )
    send = pl.pallas_call(
        functools.partial(page_kernel, pages),
        out_shape=jax.ShapeDtypeStruct((slots, 2, heads, page_len, width), jnp.bfloat16),
        in_specs=[smem(), smem(), vmem()],
        out_specs=vmem(),
        scratch_shapes=[pltpu.SMEM((owners,), jnp.int32)],
        compiler_params=pltpu.CompilerParams(vmem_limit_bytes=room(prompt_kv) * 4),
        name="quantize_pages",
    )(me_ref, page_owner.reshape(-1), prompt_kv.transpose(0, 1, 3, 2, 4))
    line = [mine] + [moves.along_z(mine, -shift) for shift in range(1, moves.lines)]
    line = jnp.concatenate(line, axis=0)
    fresh = new_kv.transpose(2, 3, 0, 1, 4).reshape(2, heads, tokens, width)
    fresh = jnp.pad(fresh, ((0, 0), (0, 0), (0, 128 - tokens), (0, 0)))
    tables = [t.reshape(owners, pages) for t in (page_owner, page_slot, page_fill)]
    line, send = lax.optimization_barrier((line, send))
    sr = jnp.concatenate([line, moves.flip(line, 0)], axis=0)
    sr, fresh, tables = lax.optimization_barrier((sr, fresh, tables))
    r2 = moves.flip(sr, 1)
    cache = lax.all_to_all(send, "ep", split_axis=0, concat_axis=0, tiled=True)
    r2, cache = lax.optimization_barrier((r2, cache))
    other_sr, other_r2 = moves.cores(sr), moves.cores(r2)

    parts = expert_front(own_core, (sr, r2), w_gate, w_up, None)
    hidden = expert_front(own_core, (other_sr, other_r2), w_gate, w_up, parts)
    other_hidden = moves.cores(hidden)
    sent = expert_back(True, owners, at, hidden, other_hidden, w_down, sr, r2, lanes)
    kept = expert_back(False, owners, at, hidden, other_hidden, w_down, sr, r2, lanes)
    attn_out = pl.pallas_call(
        functools.partial(attention_kernel, pages),
        out_shape=jax.ShapeDtypeStruct(queries.shape, jnp.bfloat16),
        in_specs=[smem()] + [vmem()] * 6,
        out_specs=vmem(),
        compiler_params=pltpu.CompilerParams(vmem_limit_bytes=8 * MIB + 16 * slots * page_len * tokens * q_heads),
        name="attention",
    )(
        me_ref,
        *tables,
        queries,
        cache,
        fresh,
    )
    group = moves.lines * tokens
    kept = kept + moves.flip(sent, 0).astype(jnp.float32)
    kept, attn_out = lax.optimization_barrier((kept, attn_out))
    kept = kept[:group] + moves.flip(kept[group:].astype(jnp.bfloat16), 1).astype(jnp.float32)
    moe = kept[:tokens]
    for shift in range(1, moves.lines):
        block = kept[shift * tokens : (shift + 1) * tokens].astype(jnp.bfloat16)
        moe = moe + moves.along_z(block, shift).astype(jnp.float32)
    moe = moe.astype(jnp.bfloat16)
    moe_out = moe.reshape(steps, requests, d // 2).transpose(1, 0, 2)

    return (attn_out, moe_out)


def solution(mesh):
    return jax.shard_map(
        body,
        mesh=mesh,
        in_specs=(
            P(("grp", "ep"), None, None, "pd", None),
            P("grp", None),
            P("grp"),
            P("grp"),
            P(("grp", "ep"), None, "pd", None),
            P(("grp", "ep"), None, None, "pd", None),
            P(("grp", "ep"), None, None),
            P(None, ("grp", "ep"), None),
            P(("grp", "ep"), None, None),
            P("ep", None, "pd"),
            P("ep", None, "pd"),
            P("ep", None, "pd"),
        ),
        out_specs=(P(("grp", "ep"), None, "pd", None), P(("grp", "ep"), None, "pd")),
        check_vma=False,
    )
```

```python
import functools
import math

import jax
import jax.numpy as jnp
from jax import lax
from jax.experimental import pallas as pl
from jax.experimental.pallas import tpu as pltpu
from jax.sharding import PartitionSpec as P

CAP = 2
LIMIT = 448.0
MIB = 1024 * 1024


def vmem():
    return pl.BlockSpec(memory_space=pltpu.VMEM)


def smem():
    return pl.BlockSpec(memory_space=pltpu.SMEM)


def page_kernel(pages, me_ref, owner_ref, kv_ref, send_ref, count_ref):
    values = kv_ref[...].astype(jnp.float32)
    largest = jnp.max(jnp.abs(values), axis=(3, 4), keepdims=True)
    scale = jnp.full(largest.shape, 2.0 ** (-16), jnp.float32)
    inverse = jnp.full(largest.shape, 2.0**16, jnp.float32)
    for exponent in range(-16, 4):
        exceeds = largest > LIMIT * 2.0**exponent
        scale = jnp.where(exceeds, scale * 2.0, scale)
        inverse = jnp.where(exceeds, inverse * 0.5, inverse)
    scaled = values * inverse
    magnitude = jnp.abs(scaled)
    step = jnp.full(scaled.shape, 2.0 ** (-9), jnp.float32)
    back = jnp.full(scaled.shape, 2.0**9, jnp.float32)
    for exponent in range(-5, 9):
        exceeds = magnitude >= 2.0**exponent
        step = jnp.where(exceeds, step * 2.0, step)
        back = jnp.where(exceeds, back * 0.5, back)
    levels = jnp.minimum(jnp.floor(magnitude * back + 0.5) * step, LIMIT)
    cache = (jnp.where(scaled < 0.0, -levels, levels) * scale).astype(jnp.bfloat16)

    send_ref[...] = jnp.zeros(send_ref.shape, send_ref.dtype)

    def clear(o, carry):
        count_ref[o] = 0
        return carry

    lax.fori_loop(0, count_ref.shape[0], clear, 0)
    first = me_ref[0] * pages
    for page in range(pages):
        owner = owner_ref[first + page]
        rank = count_ref[owner]
        count_ref[owner] = rank + 1
        send_ref[pl.ds(owner * CAP + rank, 1)] = cache[page : page + 1]


def attention_kernel(
    pages, me_ref, owner_ref, slot_ref, fill_ref, q_ref, cache_ref, fresh_ref, out_ref
):
    owners = owner_ref.shape[0]
    slots, _, heads, page_len, width = cache_ref.shape
    requests, steps, q_heads, _ = q_ref.shape
    group = q_heads // heads
    rows = requests * steps * group
    mine = (owner_ref[...] == me_ref[0]).astype(jnp.float32)
    before = (
        lax.broadcasted_iota(jnp.int32, (pages, pages), 0)
        < lax.broadcasted_iota(jnp.int32, (pages, pages), 1)
    ).astype(jnp.float32)
    rank = jnp.dot(mine, before, preferred_element_type=jnp.float32)
    code = (slot_ref[...] * (page_len + 1) + fill_ref[...]).astype(jnp.float32)
    columns = slots * page_len
    place = lax.broadcasted_iota(jnp.int32, (owners, columns), 1)
    source = lax.broadcasted_iota(jnp.int32, (owners, columns), 0)
    spread = jnp.zeros((owners, columns), jnp.float32)
    for c in range(CAP):
        held = jnp.sum(
            jnp.where((mine > 0.0) & (rank == float(c)), code, 0.0), axis=1, keepdims=True
        )
        spread = jnp.where(place // page_len == source * CAP + c, held, spread)
    line = jnp.sum(spread, axis=0, keepdims=True).astype(jnp.int32)
    request_of = line // (page_len + 1)
    fill_of = line - request_of * (page_len + 1)
    position = lax.broadcasted_iota(jnp.int32, (1, columns), 1) % page_len
    request_of = jnp.where(position < fill_of, request_of, -1)
    row_request = lax.broadcasted_iota(jnp.int32, (rows, 1), 0) // (steps * group)
    visible = row_request == request_of
    token = lax.broadcasted_iota(jnp.int32, (rows, 1), 0) // group
    first = row_request * steps
    fresh_at = lax.broadcasted_iota(jnp.int32, (1, fresh_ref.shape[2]), 1)
    fresh_visible = (fresh_at >= first) & (fresh_at <= token)
    factor = 1.0 / math.sqrt(width)
    contract = (((1,), (1,)), ((), ()))
    for head in range(heads):
        q = q_ref[:, :, head * group : (head + 1) * group, :].reshape(rows, width)
        keys = cache_ref[:, 0, head].reshape(columns, width)
        values = cache_ref[:, 1, head].reshape(columns, width)
        scores = lax.dot_general(q, keys, contract, preferred_element_type=jnp.float32) * factor
        fresh = (
            lax.dot_general(q, fresh_ref[0, head], contract, preferred_element_type=jnp.float32)
            * factor
        )
        scores = jnp.where(visible, scores, -jnp.inf)
        fresh = jnp.where(fresh_visible, fresh, -jnp.inf)
        peak = jnp.maximum(
            jnp.max(scores, axis=1, keepdims=True), jnp.max(fresh, axis=1, keepdims=True)
        )
        weight = jnp.exp(scores - peak)
        fresh_weight = jnp.exp(fresh - peak)
        total = jnp.sum(weight, axis=1, keepdims=True) + jnp.sum(
            fresh_weight, axis=1, keepdims=True
        )
        mixed = jnp.dot(
            weight.astype(jnp.bfloat16), values, preferred_element_type=jnp.float32
        ) + jnp.dot(
            fresh_weight.astype(jnp.bfloat16), fresh_ref[1, head], preferred_element_type=jnp.float32
        )
        out_ref[:, :, head * group : (head + 1) * group, :] = (
            (mixed / total).astype(out_ref.dtype).reshape(requests, steps, group, width)
        )


def pack_kernel(experts, core_ref, x_ref, route_ref, prob_ref, out_ref):
    half = x_ref.shape[1] // 2
    begin = pl.multiple_of(core_ref[0] * half, 128)
    out_ref[:, :half] = x_ref[:, pl.ds(begin, half)]
    shape = (x_ref.shape[0], out_ref.shape[1] - half)
    lane = lax.broadcasted_iota(jnp.int32, shape, 1)
    expert = lane % experts
    part = lane // experts
    dense = jnp.zeros(shape, jnp.float32)
    for k in range(route_ref.shape[1]):
        dense += jnp.where(route_ref[:, k : k + 1] == expert, prob_ref[:, k : k + 1], 0.0)
    high = dense.astype(jnp.bfloat16).astype(jnp.float32)
    middle = (dense - high).astype(jnp.bfloat16).astype(jnp.float32)
    low = dense - high - middle
    chosen = jnp.where(part == 0, high, jnp.where(part == 1, middle, low))
    out_ref[:, half:] = jnp.where(part < 3, chosen, 0.0).astype(out_ref.dtype)


def partial_kernel(chunks, core_ref, sr_ref, r2_ref, gate_ref, up_ref, gate_sum, up_sum):
    half = gate_ref.shape[1] // 2
    depth = half // chunks
    for c in range(chunks):
        at = slice(c * depth, (c + 1) * depth)
        rows = pl.ds(pl.multiple_of(core_ref[0] * half + c * depth, 128), depth)
        x = jnp.concatenate([sr_ref[:, at], r2_ref[:, at]], axis=0)
        for weight, total in ((gate_ref, gate_sum), (up_ref, up_sum)):
            part = jnp.dot(x, weight[0, rows], preferred_element_type=jnp.float32)
            total[...] = part if c == 0 else total[...] + part


def hidden_kernel(
    chunks, core_ref, sr_ref, r2_ref, gate_ref, up_ref, gate_part, up_part, out_ref, sums
):
    half = gate_ref.shape[1] // 2
    depth = half // chunks
    group = sr_ref.shape[0] // 2
    for c in range(chunks):
        at = slice(c * depth, (c + 1) * depth)
        rows = pl.ds(pl.multiple_of((1 - core_ref[0]) * half + c * depth, 128), depth)
        x = jnp.concatenate(
            [sr_ref[:group, at], r2_ref[:group, at], sr_ref[group:, at], r2_ref[group:, at]],
            axis=0,
        )
        for i, (weight, start) in enumerate(((gate_ref, gate_part), (up_ref, up_part))):
            part = jnp.dot(x, weight[0, rows], preferred_element_type=jnp.float32)
            sums[i] = (start[...] if c == 0 else sums[i]) + part
    gate = sums[0]
    out_ref[...] = (gate / (1.0 + jnp.exp(-gate)) * sums[1]).astype(out_ref.dtype)


def room(*arrays):
    return sum(math.prod(a.shape) * a.dtype.itemsize for a in arrays) * 9 // 8 + 4 * MIB


def expert_front(core, rows, w_gate, w_up, parts):
    tokens = 2 * rows[0].shape[0]
    d, f = w_gate.shape[1:]
    last = parts is not None
    total = jax.ShapeDtypeStruct((tokens, f), jnp.float32)
    scratch = [pltpu.VMEM((2, tokens, f), jnp.float32)] if last else []
    return pl.pallas_call(
        functools.partial(hidden_kernel if last else partial_kernel, 4),
        in_specs=[smem()] + [vmem()] * (6 if last else 4),
        out_specs=vmem() if last else [vmem(), vmem()],
        scratch_shapes=scratch,
        out_shape=jax.ShapeDtypeStruct((tokens, f), jnp.bfloat16) if last else [total, total],
        compiler_params=pltpu.CompilerParams(
            vmem_limit_bytes=room(*rows, w_gate, w_up, *[total] * (5 if last else 2))
        ),
        cost_estimate=pl.CostEstimate(
            flops=2 * tokens * d * f,
            bytes_accessed=tokens * d + 2 * d * f + 8 * tokens * f,
            transcendentals=tokens * f if last else 0,
        ),
        name="expert_hidden" if last else "expert_partial",
    )(core, *rows, w_gate, w_up, *(parts or ()))


def back_kernel(
    experts, lanes, chunks, at_ref, own_ref, other_ref, sr_ref, r2_ref, down_ref, send_ref, keep_ref
):
    block = down_ref.shape[2] // chunks
    f = own_ref.shape[1]
    group = sr_ref.shape[0] // 2
    core = at_ref[1]

    def rows(ref, order):
        return jnp.concatenate([ref[i * group : (i + 1) * group] for i in order], axis=0)

    own = rows(own_ref, (1, 3, 0, 2))
    other = rows(other_ref, (2, 3, 0, 1))
    begin = pl.multiple_of(core * f, 128)
    rest = pl.multiple_of((1 - core) * f, 128)
    tail = slice(sr_ref.shape[1] - lanes, sr_ref.shape[1])
    probs = jnp.concatenate(
        [
            ref[i * group : (i + 1) * group, tail].astype(jnp.float32)
            for i in (1, 0)
            for ref in (sr_ref, r2_ref)
        ],
        axis=0,
    )
    lane = lax.broadcasted_iota(jnp.int32, probs.shape, 1)
    mine = lane % experts == at_ref[0]
    weight = jnp.sum(jnp.where(mine, probs, 0.0), axis=1, keepdims=True)
    for c in range(chunks):
        at = slice(c * block, (c + 1) * block)
        total = jnp.dot(own, down_ref[0, pl.ds(begin, f), at], preferred_element_type=jnp.float32)
        total += jnp.dot(
            other, down_ref[0, pl.ds(rest, f), at], preferred_element_type=jnp.float32
        )
        total = total * weight
        send_ref[:, at] = total[: 2 * group].astype(send_ref.dtype)
        keep_ref[:, at] = total[2 * group :]


def expert_back(experts, at, own, other, w_down, sr, r2, lanes):
    tokens, f = own.shape
    group2 = sr.shape[0]
    width = w_down.shape[2]
    send = jax.ShapeDtypeStruct((group2, width), jnp.bfloat16)
    keep = jax.ShapeDtypeStruct((group2, width), jnp.float32)
    return pl.pallas_call(
        functools.partial(back_kernel, experts, lanes, 4),
        out_shape=[send, keep],
        in_specs=[smem()] + [vmem()] * 5,
        out_specs=[vmem(), vmem()],
        compiler_params=pltpu.CompilerParams(
            vmem_limit_bytes=room(own, other, w_down, sr, r2, send, keep, keep)
        ),
        cost_estimate=pl.CostEstimate(
            flops=4 * tokens * f * width,
            bytes_accessed=2 * (2 * tokens * f + 2 * f * width + 3 * group2 * width),
            transcendentals=0,
        ),
        name="expert_back",
    )(at, own, other, sr, r2, w_down)


def stage_kernel(pieces, *refs):
    count = len(refs) // 2
    sems = refs[-1]
    copies = []
    for i in range(count):
        source, target = refs[i], refs[count + i]
        depth = source.shape[1] // pieces
        for c in range(pieces):
            rows = pl.ds(c * depth, depth)
            copies.append(
                pltpu.make_async_copy(source.at[:, rows], target.at[:, rows], sems.at[i, c])
            )
    for copy in copies:
        copy.start()
    for copy in copies:
        copy.wait()


def stage(*weights):
    return pl.pallas_call(
        functools.partial(stage_kernel, 4),
        out_shape=[jax.ShapeDtypeStruct(w.shape, w.dtype) for w in weights],
        in_specs=[pl.BlockSpec(memory_space=pltpu.HBM)] * len(weights),
        out_specs=[vmem()] * len(weights),
        scratch_shapes=[pltpu.SemaphoreType.DMA((len(weights), 4))],
        compiler_params=pltpu.CompilerParams(vmem_limit_bytes=48 * MIB),
        name="stage_weights",
    )(*weights)


class Moves:
    def __init__(self, owners):
        self.owners = owners
        self.lines = owners // 4

    def go(self, x, where):
        perm = [
            (ep * 2 + core, where(ep, core)) for ep in range(self.owners) for core in range(2)
        ]
        return lax.ppermute(x, ("ep", "pd"), perm)

    def along_z(self, x, turn):
        return self.go(x, lambda ep, core: (ep ^ (4 * turn)) * 2 + core)

    def flip(self, x, turn):
        return self.go(x, lambda ep, core: (ep ^ (1 << ((core + turn) % 2))) * 2 + core)

    def cores(self, x):
        return self.go(x, lambda ep, core: ep * 2 + 1 - core)


def body(
    prompt_kv,
    page_owner,
    page_slot,
    page_fill,
    queries,
    new_kv,
    moe_input,
    expert_routes,
    route_probs,
    w_gate,
    w_up,
    w_down,
):
    owners = lax.axis_size("ep")
    me = lax.axis_index("ep").astype(jnp.int32)
    me_ref = me.reshape(1)
    core = lax.axis_index("pd").astype(jnp.int32)
    pages, _, page_len, heads, width = prompt_kv.shape
    requests, steps, q_heads, _ = queries.shape
    d = moe_input.shape[2]
    tokens = requests * steps
    slots = owners * CAP

    moves = Moves(owners)
    top = expert_routes.shape[2]
    lanes = -(-3 * owners // 128) * 128
    at = jnp.stack([me, core])
    own_core = core.reshape(1)
    mine = pl.pallas_call(
        functools.partial(pack_kernel, owners),
        out_shape=jax.ShapeDtypeStruct((tokens, d // 2 + lanes), jnp.bfloat16),
        in_specs=[smem()] + [vmem()] * 3,
        out_specs=vmem(),
        name="pack_tokens",
    )(
        own_core,
        moe_input.transpose(1, 0, 2).reshape(tokens, d),
        expert_routes.reshape(tokens, top),
        route_probs.transpose(1, 0, 2).reshape(tokens, top),
    )
    send = pl.pallas_call(
        functools.partial(page_kernel, pages),
        out_shape=jax.ShapeDtypeStruct((slots, 2, heads, page_len, width), jnp.bfloat16),
        in_specs=[smem(), smem(), vmem()],
        out_specs=vmem(),
        scratch_shapes=[pltpu.SMEM((owners,), jnp.int32)],
        compiler_params=pltpu.CompilerParams(vmem_limit_bytes=room(prompt_kv) * 4),
        name="quantize_pages",
    )(me_ref, page_owner.reshape(-1), prompt_kv.transpose(0, 1, 3, 2, 4))
    fresh = new_kv.transpose(2, 3, 0, 1, 4).reshape(2, heads, tokens, width)
    fresh = jnp.pad(fresh, ((0, 0), (0, 0), (0, 128 - tokens), (0, 0)))
    tables = [t.reshape(owners, pages) for t in (page_owner, page_slot, page_fill)]

    mine, w_gate, w_up = lax.optimization_barrier((mine, w_gate, w_up))
    w_gate, w_up = stage(w_gate, w_up)

    chunks = [range(0, moves.lines, 2), range(1, moves.lines, 2)]
    line = [
        jnp.concatenate([moves.along_z(mine, turn) if turn else mine for turn in chunk], axis=0)
        for chunk in chunks
    ]
    near, w_gate, w_up = lax.optimization_barrier((line[0], w_gate, w_up))
    sr = jnp.concatenate([near, moves.flip(near, 0)], axis=0)
    cache = lax.all_to_all(send, "ep", split_axis=0, concat_axis=0, tiled=True)
    gathered = [(sr, moves.flip(sr, 1))]
    sr = jnp.concatenate([line[1], moves.flip(line[1], 0)], axis=0)
    sr, fresh, tables = lax.optimization_barrier((sr, fresh, tables))
    r2 = moves.flip(sr, 1)
    r2, cache = lax.optimization_barrier((r2, cache))
    gathered.append((sr, r2))

    kept = []
    for sr, r2 in gathered:
        others = moves.cores(sr), moves.cores(r2)
        parts = expert_front(own_core, (sr, r2), w_gate, w_up, None)
        hidden = expert_front(own_core, others, w_gate, w_up, parts)
        sent, keep = expert_back(
            owners, at, hidden, moves.cores(hidden), w_down, sr, r2, lanes
        )
        kept.append(keep + moves.flip(sent, 0).astype(jnp.float32))
    attn_out = pl.pallas_call(
        functools.partial(attention_kernel, pages),
        out_shape=jax.ShapeDtypeStruct(queries.shape, jnp.bfloat16),
        in_specs=[smem()] + [vmem()] * 6,
        out_specs=vmem(),
        compiler_params=pltpu.CompilerParams(vmem_limit_bytes=8 * MIB + 16 * slots * page_len * tokens * q_heads),
        name="attention",
    )(
        me_ref,
        *tables,
        queries,
        cache,
        fresh,
    )
    kept[1], attn_out = lax.optimization_barrier((kept[1], attn_out))
    moe = None
    for chunk, keep in zip(chunks, kept):
        group = len(chunk) * tokens
        back = moves.flip(keep[group:].astype(jnp.bfloat16), 1)
        keep = keep[:group] + back.astype(jnp.float32)
        for i, turn in enumerate(chunk):
            block = keep[i * tokens : (i + 1) * tokens]
            if turn:
                block = moves.along_z(block.astype(jnp.bfloat16), turn).astype(jnp.float32)
            moe = block if moe is None else moe + block
    moe = moe.astype(jnp.bfloat16)
    moe_out = moe.reshape(steps, requests, d // 2).transpose(1, 0, 2)

    return (attn_out, moe_out)


def solution(mesh):
    return jax.shard_map(
        body,
        mesh=mesh,
        in_specs=(
            P(("grp", "ep"), None, None, "pd", None),
            P("grp", None),
            P("grp"),
            P("grp"),
            P(("grp", "ep"), None, "pd", None),
            P(("grp", "ep"), None, None, "pd", None),
            P(("grp", "ep"), None, None),
            P(None, ("grp", "ep"), None),
            P(("grp", "ep"), None, None),
            P("ep", None, "pd"),
            P("ep", None, "pd"),
            P("ep", None, "pd"),
        ),
        out_specs=(P(("grp", "ep"), None, "pd", None), P(("grp", "ep"), None, "pd")),
        check_vma=False,
    )
```

```python
import functools
import math

import jax
import jax.numpy as jnp
from jax import lax
from jax.experimental import pallas as pl
from jax.experimental.pallas import tpu as pltpu
from jax.sharding import PartitionSpec as P

CAP = 2
LIMIT = 448.0
MIB = 1024 * 1024


def vmem():
    return pl.BlockSpec(memory_space=pltpu.VMEM)


def smem():
    return pl.BlockSpec(memory_space=pltpu.SMEM)


def page_kernel(pages, me_ref, owner_ref, kv_ref, gate_ref, up_ref, send_ref, count_ref):
    values = kv_ref[...].astype(jnp.float32)
    largest = jnp.max(jnp.abs(values), axis=(3, 4), keepdims=True)
    scale = jnp.full(largest.shape, 2.0 ** (-16), jnp.float32)
    inverse = jnp.full(largest.shape, 2.0**16, jnp.float32)
    for exponent in range(-16, 4):
        exceeds = largest > LIMIT * 2.0**exponent
        scale = jnp.where(exceeds, scale * 2.0, scale)
        inverse = jnp.where(exceeds, inverse * 0.5, inverse)
    scaled = values * inverse
    magnitude = jnp.abs(scaled)
    step = jnp.full(scaled.shape, 2.0 ** (-9), jnp.float32)
    back = jnp.full(scaled.shape, 2.0**9, jnp.float32)
    for exponent in range(-5, 9):
        exceeds = magnitude >= 2.0**exponent
        step = jnp.where(exceeds, step * 2.0, step)
        back = jnp.where(exceeds, back * 0.5, back)
    levels = jnp.minimum(jnp.floor(magnitude * back + 0.5) * step, LIMIT)
    cache = (jnp.where(scaled < 0.0, -levels, levels) * scale).astype(jnp.bfloat16)

    send_ref[...] = jnp.zeros(send_ref.shape, send_ref.dtype)

    def clear(o, carry):
        count_ref[o] = 0
        return carry

    lax.fori_loop(0, count_ref.shape[0], clear, 0)
    first = me_ref[0] * pages
    for page in range(pages):
        owner = owner_ref[first + page]
        rank = count_ref[owner]
        count_ref[owner] = rank + 1
        send_ref[pl.ds(owner * CAP + rank, 1)] = cache[page : page + 1]


def attention_kernel(
    pages, me_ref, owner_ref, slot_ref, fill_ref, q_ref, cache_ref, fresh_ref, out_ref
):
    owners = owner_ref.shape[0]
    slots, _, heads, page_len, width = cache_ref.shape
    requests, steps, q_heads, _ = q_ref.shape
    group = q_heads // heads
    rows = requests * steps * group
    mine = (owner_ref[...] == me_ref[0]).astype(jnp.float32)
    before = (
        lax.broadcasted_iota(jnp.int32, (pages, pages), 0)
        < lax.broadcasted_iota(jnp.int32, (pages, pages), 1)
    ).astype(jnp.float32)
    rank = jnp.dot(mine, before, preferred_element_type=jnp.float32)
    code = (slot_ref[...] * (page_len + 1) + fill_ref[...]).astype(jnp.float32)
    columns = slots * page_len
    place = lax.broadcasted_iota(jnp.int32, (owners, columns), 1)
    source = lax.broadcasted_iota(jnp.int32, (owners, columns), 0)
    spread = jnp.zeros((owners, columns), jnp.float32)
    for c in range(CAP):
        held = jnp.sum(
            jnp.where((mine > 0.0) & (rank == float(c)), code, 0.0), axis=1, keepdims=True
        )
        spread = jnp.where(place // page_len == source * CAP + c, held, spread)
    line = jnp.sum(spread, axis=0, keepdims=True).astype(jnp.int32)
    request_of = line // (page_len + 1)
    fill_of = line - request_of * (page_len + 1)
    position = lax.broadcasted_iota(jnp.int32, (1, columns), 1) % page_len
    request_of = jnp.where(position < fill_of, request_of, -1)
    row_request = lax.broadcasted_iota(jnp.int32, (rows, 1), 0) // (steps * group)
    visible = row_request == request_of
    token = lax.broadcasted_iota(jnp.int32, (rows, 1), 0) // group
    first = row_request * steps
    fresh_at = lax.broadcasted_iota(jnp.int32, (1, fresh_ref.shape[2]), 1)
    fresh_visible = (fresh_at >= first) & (fresh_at <= token)
    factor = 1.0 / math.sqrt(width)
    contract = (((1,), (1,)), ((), ()))
    for head in range(heads):
        q = q_ref[:, :, head * group : (head + 1) * group, :].reshape(rows, width)
        keys = cache_ref[:, 0, head].reshape(columns, width)
        values = cache_ref[:, 1, head].reshape(columns, width)
        scores = lax.dot_general(q, keys, contract, preferred_element_type=jnp.float32) * factor
        fresh = (
            lax.dot_general(q, fresh_ref[0, head], contract, preferred_element_type=jnp.float32)
            * factor
        )
        scores = jnp.where(visible, scores, -jnp.inf)
        fresh = jnp.where(fresh_visible, fresh, -jnp.inf)
        peak = jnp.maximum(
            jnp.max(scores, axis=1, keepdims=True), jnp.max(fresh, axis=1, keepdims=True)
        )
        weight = jnp.exp(scores - peak)
        fresh_weight = jnp.exp(fresh - peak)
        total = jnp.sum(weight, axis=1, keepdims=True) + jnp.sum(
            fresh_weight, axis=1, keepdims=True
        )
        mixed = jnp.dot(
            weight.astype(jnp.bfloat16), values, preferred_element_type=jnp.float32
        ) + jnp.dot(
            fresh_weight.astype(jnp.bfloat16), fresh_ref[1, head], preferred_element_type=jnp.float32
        )
        out_ref[:, :, head * group : (head + 1) * group, :] = (
            (mixed / total).astype(out_ref.dtype).reshape(requests, steps, group, width)
        )


def pack_kernel(experts, core_ref, x_ref, route_ref, prob_ref, out_ref):
    half = x_ref.shape[1] // 2
    begin = pl.multiple_of(core_ref[0] * half, 128)
    out_ref[:, :half] = x_ref[:, pl.ds(begin, half)]
    shape = (x_ref.shape[0], out_ref.shape[1] - half)
    lane = lax.broadcasted_iota(jnp.int32, shape, 1)
    expert = lane % experts
    part = lane // experts
    dense = jnp.zeros(shape, jnp.float32)
    for k in range(route_ref.shape[1]):
        dense += jnp.where(route_ref[:, k : k + 1] == expert, prob_ref[:, k : k + 1], 0.0)
    high = dense.astype(jnp.bfloat16).astype(jnp.float32)
    middle = (dense - high).astype(jnp.bfloat16).astype(jnp.float32)
    low = dense - high - middle
    chosen = jnp.where(part == 0, high, jnp.where(part == 1, middle, low))
    out_ref[:, half:] = jnp.where(part < 3, chosen, 0.0).astype(out_ref.dtype)


def partial_kernel(chunks, count, core_ref, *refs):
    x_refs, (gate_ref, up_ref, gate_sum, up_sum) = refs[:count], refs[count:]
    half = gate_ref.shape[1] // 2
    depth = half // chunks
    for c in range(chunks):
        at = slice(c * depth, (c + 1) * depth)
        rows = pl.ds(pl.multiple_of(core_ref[0] * half + c * depth, 128), depth)
        x = jnp.concatenate([ref[:, at] for ref in x_refs], axis=0)
        for weight, total in ((gate_ref, gate_sum), (up_ref, up_sum)):
            part = jnp.dot(x, weight[0, rows], preferred_element_type=jnp.float32)
            total[...] = part if c == 0 else total[...] + part


def hidden_kernel(chunks, count, core_ref, *refs):
    x_refs = refs[:count]
    gate_ref, up_ref, gate_part, up_part, out_ref, sums = refs[count:]
    half = gate_ref.shape[1] // 2
    depth = half // chunks
    for c in range(chunks):
        at = slice(c * depth, (c + 1) * depth)
        rows = pl.ds(pl.multiple_of((1 - core_ref[0]) * half + c * depth, 128), depth)
        x = jnp.concatenate([ref[:, at] for ref in x_refs], axis=0)
        for i, (weight, start) in enumerate(((gate_ref, gate_part), (up_ref, up_part))):
            part = jnp.dot(x, weight[0, rows], preferred_element_type=jnp.float32)
            sums[i] = (start[...] if c == 0 else sums[i]) + part
    gate = sums[0]
    out_ref[...] = (gate / (1.0 + jnp.exp(-gate)) * sums[1]).astype(out_ref.dtype)


def room(*arrays):
    return sum(math.prod(a.shape) * a.dtype.itemsize for a in arrays) * 9 // 8 + 4 * MIB


def expert_front(core, rows, w_gate, w_up, parts):
    tokens = sum(x.shape[0] for x in rows)
    d, f = w_gate.shape[1:]
    last = parts is not None
    total = jax.ShapeDtypeStruct((tokens, f), jnp.float32)
    scratch = [pltpu.VMEM((2, tokens, f), jnp.float32)] if last else []
    return pl.pallas_call(
        functools.partial(hidden_kernel if last else partial_kernel, 4, len(rows)),
        in_specs=[smem()] + [vmem()] * (len(rows) + (4 if last else 2)),
        out_specs=vmem() if last else [vmem(), vmem()],
        scratch_shapes=scratch,
        out_shape=jax.ShapeDtypeStruct((tokens, f), jnp.bfloat16) if last else [total, total],
        compiler_params=pltpu.CompilerParams(
            vmem_limit_bytes=room(*rows, w_gate, w_up, *[total] * (5 if last else 2))
        ),
        cost_estimate=pl.CostEstimate(
            flops=2 * tokens * d * f,
            bytes_accessed=tokens * d + 2 * d * f + 8 * tokens * f,
            transcendentals=tokens * f if last else 0,
        ),
        name="expert_hidden" if last else "expert_partial",
    )(core, *rows, w_gate, w_up, *(parts or ()))


def back_kernel(experts, begin, count, chunks, at_ref, own_ref, other_ref, *refs):
    prob_refs, (down_ref, keep_ref, *send_refs) = refs[:count], refs[count:]
    block = down_ref.shape[2] // chunks
    f = own_ref.shape[1]
    piece = keep_ref.shape[0]
    rows = (len(send_refs) + 1) * piece
    lanes = 128 * (-(-3 * experts // 128))
    core = at_ref[1]
    own = own_ref[begin : begin + rows]
    other = other_ref[begin : begin + rows]
    first = pl.multiple_of(core * f, 128)
    rest = pl.multiple_of((1 - core) * f, 128)
    probs = jnp.concatenate(
        [ref[:, ref.shape[1] - lanes :].astype(jnp.float32) for ref in prob_refs], axis=0
    )
    lane = lax.broadcasted_iota(jnp.int32, probs.shape, 1)
    mine = lane % experts == at_ref[0]
    weight = jnp.sum(jnp.where(mine, probs, 0.0), axis=1, keepdims=True)
    for c in range(chunks):
        at = slice(c * block, (c + 1) * block)
        total = jnp.dot(own, down_ref[0, pl.ds(first, f), at], preferred_element_type=jnp.float32)
        total += jnp.dot(
            other, down_ref[0, pl.ds(rest, f), at], preferred_element_type=jnp.float32
        )
        total = total * weight
        keep_ref[:, at] = total[:piece]
        for i, ref in enumerate(send_refs):
            ref[:, at] = total[(i + 1) * piece : (i + 2) * piece].astype(ref.dtype)


def expert_back(experts, begin, at, own, other, w_down, pieces):
    rows = sum(x.shape[0] for x in pieces)
    f = own.shape[1]
    width = w_down.shape[2]
    send = jax.ShapeDtypeStruct((rows // 4, width), jnp.bfloat16)
    keep = jax.ShapeDtypeStruct((rows // 4, width), jnp.float32)
    return pl.pallas_call(
        functools.partial(back_kernel, experts, begin, len(pieces), 4),
        out_shape=[keep, send, send, send],
        in_specs=[smem()] + [vmem()] * (3 + len(pieces)),
        out_specs=[vmem()] * 4,
        compiler_params=pltpu.CompilerParams(
            vmem_limit_bytes=room(own, other, w_down, *pieces, *[keep] * 4)
        ),
        cost_estimate=pl.CostEstimate(
            flops=4 * rows * f * width,
            bytes_accessed=2 * (4 * rows * f + 2 * f * width + 2 * rows * width),
            transcendentals=0,
        ),
        name="expert_back",
    )(at, own, other, *pieces, w_down)


class Moves:
    def __init__(self, owners):
        self.owners = owners
        self.lines = owners // 4

    def go(self, x, where):
        perm = [
            (ep * 2 + core, where(ep, core)) for ep in range(self.owners) for core in range(2)
        ]
        return lax.ppermute(x, ("ep", "pd"), perm)

    def along_z(self, x, turn):
        return self.go(x, lambda ep, core: (ep ^ (4 * turn)) * 2 + core)

    def across(self, x, turn):
        return self.go(x, lambda ep, core: (ep ^ turn) * 2 + core)

    def cores(self, x):
        return self.go(x, lambda ep, core: ep * 2 + 1 - core)


def body(
    prompt_kv,
    page_owner,
    page_slot,
    page_fill,
    queries,
    new_kv,
    moe_input,
    expert_routes,
    route_probs,
    w_gate,
    w_up,
    w_down,
):
    owners = lax.axis_size("ep")
    me = lax.axis_index("ep").astype(jnp.int32)
    me_ref = me.reshape(1)
    core = lax.axis_index("pd").astype(jnp.int32)
    pages, _, page_len, heads, width = prompt_kv.shape
    requests, steps, q_heads, _ = queries.shape
    d = moe_input.shape[2]
    tokens = requests * steps
    slots = owners * CAP

    moves = Moves(owners)
    top = expert_routes.shape[2]
    lanes = -(-3 * owners // 128) * 128
    at = jnp.stack([me, core])
    own_core = core.reshape(1)
    mine = pl.pallas_call(
        functools.partial(pack_kernel, owners),
        out_shape=jax.ShapeDtypeStruct((tokens, d // 2 + lanes), jnp.bfloat16),
        in_specs=[smem()] + [vmem()] * 3,
        out_specs=vmem(),
        name="pack_tokens",
    )(
        own_core,
        moe_input.transpose(1, 0, 2).reshape(tokens, d),
        expert_routes.reshape(tokens, top),
        route_probs.transpose(1, 0, 2).reshape(tokens, top),
    )
    fresh = new_kv.transpose(2, 3, 0, 1, 4).reshape(2, heads, tokens, width)
    fresh = jnp.pad(fresh, ((0, 0), (0, 0), (0, 128 - tokens), (0, 0)))
    tables = [t.reshape(owners, pages) for t in (page_owner, page_slot, page_fill)]

    sets = [range(0, moves.lines, 2), range(1, moves.lines, 2)]
    line = [
        jnp.concatenate([moves.along_z(mine, turn) if turn else mine for turn in chips], axis=0)
        for chips in sets
    ]
    line[1], prompt_kv = lax.optimization_barrier((line[1], prompt_kv))
    send = pl.pallas_call(
        functools.partial(page_kernel, pages),
        out_shape=jax.ShapeDtypeStruct((slots, 2, heads, page_len, width), jnp.bfloat16),
        in_specs=[smem(), smem()] + [vmem()] * 3,
        out_specs=vmem(),
        scratch_shapes=[pltpu.SMEM((owners,), jnp.int32)],
        compiler_params=pltpu.CompilerParams(vmem_limit_bytes=room(*[prompt_kv] * 5, w_gate, w_up)),
        name="quantize_pages",
    )(me_ref, page_owner.reshape(-1), prompt_kv.transpose(0, 1, 3, 2, 4), w_gate, w_up)
    cache = lax.all_to_all(send, "ep", split_axis=0, concat_axis=0, tiled=True)
    near = [line[0]] + [moves.across(line[0], turn) for turn in (1, 2, 3)]
    far = [line[1]] + [moves.across(line[1], turn) for turn in (1, 2, 3)]
    near = [jnp.concatenate(near, axis=0)]
    others = [moves.cores(x) for x in near + far]
    parts = expert_front(own_core, near + far, w_gate, w_up, None)
    others, cache = lax.optimization_barrier((others, cache))
    hidden = expert_front(own_core, others, w_gate, w_up, parts)
    other_hidden = moves.cores(hidden)

    half = near[0].shape[0]
    sums = []
    for begin, pieces in ((half, far), (0, near)):
        keep, *send = expert_back(owners, begin, at, hidden, other_hidden, w_down, pieces)
        for turn, rows in zip((1, 2, 3), send):
            keep = keep + moves.across(rows, turn).astype(jnp.float32)
        sums.append(keep)
    moe = sums[1][:tokens]
    for chips, rows in zip(sets, reversed(sums)):
        for i, turn in enumerate(chips):
            if turn:
                block = rows[i * tokens : (i + 1) * tokens].astype(jnp.bfloat16)
                moe = moe + moves.along_z(block, turn).astype(jnp.float32)
    attn_out = pl.pallas_call(
        functools.partial(attention_kernel, pages),
        out_shape=jax.ShapeDtypeStruct(queries.shape, jnp.bfloat16),
        in_specs=[smem()] + [vmem()] * 6,
        out_specs=vmem(),
        compiler_params=pltpu.CompilerParams(
            vmem_limit_bytes=8 * MIB + 16 * slots * page_len * tokens * q_heads
        ),
        name="attention",
    )(
        me_ref,
        *tables,
        queries,
        cache,
        fresh,
    )
    moe = moe.astype(jnp.bfloat16)
    moe_out = moe.reshape(steps, requests, d // 2).transpose(1, 0, 2)

    return (attn_out, moe_out)


def solution(mesh):
    return jax.shard_map(
        body,
        mesh=mesh,
        in_specs=(
            P(("grp", "ep"), None, None, "pd", None),
            P("grp", None),
            P("grp"),
            P("grp"),
            P(("grp", "ep"), None, "pd", None),
            P(("grp", "ep"), None, None, "pd", None),
            P(("grp", "ep"), None, None),
            P(None, ("grp", "ep"), None),
            P(("grp", "ep"), None, None),
            P("ep", None, "pd"),
            P("ep", None, "pd"),
            P("ep", None, "pd"),
        ),
        out_specs=(P(("grp", "ep"), None, "pd", None), P(("grp", "ep"), None, "pd")),
        check_vma=False,
    )
```

```python
import functools
import math

import jax
import jax.numpy as jnp
from jax import lax
from jax.experimental import pallas as pl
from jax.experimental.pallas import tpu as pltpu
from jax.sharding import PartitionSpec as P

CAP = 2
LIMIT = 448.0
MIB = 1024 * 1024


def vmem():
    return pl.BlockSpec(memory_space=pltpu.VMEM)


def smem():
    return pl.BlockSpec(memory_space=pltpu.SMEM)


def page_kernel(pages, me_ref, owner_ref, kv_ref, send_ref, count_ref):
    values = kv_ref[...].astype(jnp.float32)
    largest = jnp.max(jnp.abs(values), axis=(3, 4), keepdims=True)
    scale = jnp.full(largest.shape, 2.0 ** (-16), jnp.float32)
    inverse = jnp.full(largest.shape, 2.0**16, jnp.float32)
    for exponent in range(-16, 4):
        exceeds = largest > LIMIT * 2.0**exponent
        scale = jnp.where(exceeds, scale * 2.0, scale)
        inverse = jnp.where(exceeds, inverse * 0.5, inverse)
    scaled = values * inverse
    magnitude = jnp.abs(scaled)
    step = jnp.full(scaled.shape, 2.0 ** (-9), jnp.float32)
    back = jnp.full(scaled.shape, 2.0**9, jnp.float32)
    for exponent in range(-5, 9):
        exceeds = magnitude >= 2.0**exponent
        step = jnp.where(exceeds, step * 2.0, step)
        back = jnp.where(exceeds, back * 0.5, back)
    levels = jnp.minimum(jnp.floor(magnitude * back + 0.5) * step, LIMIT)
    cache = (jnp.where(scaled < 0.0, -levels, levels) * scale).astype(jnp.bfloat16)

    send_ref[...] = jnp.zeros(send_ref.shape, send_ref.dtype)

    def clear(o, carry):
        count_ref[o] = 0
        return carry

    lax.fori_loop(0, count_ref.shape[0], clear, 0)
    first = me_ref[0] * pages
    for page in range(pages):
        owner = owner_ref[first + page]
        rank = count_ref[owner]
        count_ref[owner] = rank + 1
        send_ref[pl.ds(owner * CAP + rank, 1)] = cache[page : page + 1]


def attention_kernel(
    pages, me_ref, owner_ref, slot_ref, fill_ref, q_ref, cache_ref, fresh_ref, after_ref, out_ref
):
    owners = owner_ref.shape[0]
    slots, _, heads, page_len, width = cache_ref.shape
    requests, steps, q_heads, _ = q_ref.shape
    group = q_heads // heads
    rows = requests * steps * group
    mine = (owner_ref[...] == me_ref[0]).astype(jnp.float32)
    before = (
        lax.broadcasted_iota(jnp.int32, (pages, pages), 0)
        < lax.broadcasted_iota(jnp.int32, (pages, pages), 1)
    ).astype(jnp.float32)
    rank = jnp.dot(mine, before, preferred_element_type=jnp.float32)
    code = (slot_ref[...] * (page_len + 1) + fill_ref[...]).astype(jnp.float32)
    columns = slots * page_len
    place = lax.broadcasted_iota(jnp.int32, (owners, columns), 1)
    source = lax.broadcasted_iota(jnp.int32, (owners, columns), 0)
    spread = jnp.zeros((owners, columns), jnp.float32)
    for c in range(CAP):
        held = jnp.sum(
            jnp.where((mine > 0.0) & (rank == float(c)), code, 0.0), axis=1, keepdims=True
        )
        spread = jnp.where(place // page_len == source * CAP + c, held, spread)
    line = jnp.sum(spread, axis=0, keepdims=True).astype(jnp.int32)
    request_of = line // (page_len + 1)
    fill_of = line - request_of * (page_len + 1)
    position = lax.broadcasted_iota(jnp.int32, (1, columns), 1) % page_len
    request_of = jnp.where(position < fill_of, request_of, -1)
    row_request = lax.broadcasted_iota(jnp.int32, (rows, 1), 0) // (steps * group)
    visible = row_request == request_of
    token = lax.broadcasted_iota(jnp.int32, (rows, 1), 0) // group
    first = row_request * steps
    fresh_at = lax.broadcasted_iota(jnp.int32, (1, fresh_ref.shape[2]), 1)
    fresh_visible = (fresh_at >= first) & (fresh_at <= token)
    factor = 1.0 / math.sqrt(width)
    contract = (((1,), (1,)), ((), ()))
    for head in range(heads):
        q = q_ref[:, :, head * group : (head + 1) * group, :].reshape(rows, width)
        keys = cache_ref[:, 0, head].reshape(columns, width)
        values = cache_ref[:, 1, head].reshape(columns, width)
        scores = lax.dot_general(q, keys, contract, preferred_element_type=jnp.float32) * factor
        fresh = (
            lax.dot_general(q, fresh_ref[0, head], contract, preferred_element_type=jnp.float32)
            * factor
        )
        scores = jnp.where(visible, scores, -jnp.inf)
        fresh = jnp.where(fresh_visible, fresh, -jnp.inf)
        peak = jnp.maximum(
            jnp.max(scores, axis=1, keepdims=True), jnp.max(fresh, axis=1, keepdims=True)
        )
        weight = jnp.exp(scores - peak)
        fresh_weight = jnp.exp(fresh - peak)
        total = jnp.sum(weight, axis=1, keepdims=True) + jnp.sum(
            fresh_weight, axis=1, keepdims=True
        )
        mixed = jnp.dot(
            weight.astype(jnp.bfloat16), values, preferred_element_type=jnp.float32
        ) + jnp.dot(
            fresh_weight.astype(jnp.bfloat16), fresh_ref[1, head], preferred_element_type=jnp.float32
        )
        out_ref[:, :, head * group : (head + 1) * group, :] = (
            (mixed / total).astype(out_ref.dtype).reshape(requests, steps, group, width)
        )


def pack_kernel(experts, core_ref, x_ref, route_ref, prob_ref, out_ref):
    half = x_ref.shape[1] // 2
    begin = pl.multiple_of(core_ref[0] * half, 128)
    out_ref[:, :half] = x_ref[:, pl.ds(begin, half)]
    shape = (x_ref.shape[0], out_ref.shape[1] - half)
    lane = lax.broadcasted_iota(jnp.int32, shape, 1)
    expert = lane % experts
    part = lane // experts
    dense = jnp.zeros(shape, jnp.float32)
    for k in range(route_ref.shape[1]):
        dense += jnp.where(route_ref[:, k : k + 1] == expert, prob_ref[:, k : k + 1], 0.0)
    high = dense.astype(jnp.bfloat16).astype(jnp.float32)
    middle = (dense - high).astype(jnp.bfloat16).astype(jnp.float32)
    low = dense - high - middle
    chosen = jnp.where(part == 0, high, jnp.where(part == 1, middle, low))
    out_ref[:, half:] = jnp.where(part < 3, chosen, 0.0).astype(out_ref.dtype)


def partial_kernel(chunks, core_ref, x_ref, gate_ref, up_ref, gate_sum, up_sum):
    half = gate_ref.shape[1] // 2
    depth = half // chunks
    for c in range(chunks):
        at = slice(c * depth, (c + 1) * depth)
        rows = pl.ds(pl.multiple_of(core_ref[0] * half + c * depth, 128), depth)
        for weight, total in ((gate_ref, gate_sum), (up_ref, up_sum)):
            part = jnp.dot(x_ref[:, at], weight[0, rows], preferred_element_type=jnp.float32)
            total[...] = part if c == 0 else total[...] + part


def hidden_kernel(
    chunks, core_ref, sr_ref, r2_ref, gate_ref, up_ref, g0_ref, u0_ref, g1_ref, u1_ref, out_ref, sums
):
    half = gate_ref.shape[1] // 2
    depth = half // chunks
    group = sr_ref.shape[0] // 2
    for c in range(chunks):
        at = slice(c * depth, (c + 1) * depth)
        rows = pl.ds(pl.multiple_of((1 - core_ref[0]) * half + c * depth, 128), depth)
        x = jnp.concatenate(
            [sr_ref[:group, at], r2_ref[:group, at], sr_ref[group:, at], r2_ref[group:, at]],
            axis=0,
        )
        for i, (weight, early, late) in enumerate(
            ((gate_ref, g0_ref, g1_ref), (up_ref, u0_ref, u1_ref))
        ):
            part = jnp.dot(x, weight[0, rows], preferred_element_type=jnp.float32)
            if c == 0:
                sums[i, : 2 * group] = early[...] + part[: 2 * group]
                sums[i, 2 * group :] = late[...] + part[2 * group :]
            else:
                sums[i] += part
    gate = sums[0]
    out_ref[...] = (gate / (1.0 + jnp.exp(-gate)) * sums[1]).astype(out_ref.dtype)


def room(*arrays):
    return sum(math.prod(a.shape) * a.dtype.itemsize for a in arrays) * 9 // 8 + 4 * MIB


def expert_partial(core, x, w_gate, w_up):
    tokens = x.shape[0]
    d, f = w_gate.shape[1:]
    total = jax.ShapeDtypeStruct((tokens, f), jnp.float32)
    return pl.pallas_call(
        functools.partial(partial_kernel, 4),
        in_specs=[smem()] + [vmem()] * 3,
        out_specs=[vmem(), vmem()],
        out_shape=[total, total],
        compiler_params=pltpu.CompilerParams(vmem_limit_bytes=room(x, w_gate, w_up, total, total)),
        cost_estimate=pl.CostEstimate(
            flops=2 * tokens * d * f,
            bytes_accessed=tokens * d + 2 * d * f + 8 * tokens * f,
            transcendentals=0,
        ),
        name="expert_partial",
    )(core, x, w_gate, w_up)


def expert_hidden(core, sr, r2, w_gate, w_up, parts):
    tokens = 2 * sr.shape[0]
    d, f = w_gate.shape[1:]
    total = jax.ShapeDtypeStruct((tokens, f), jnp.float32)
    return pl.pallas_call(
        functools.partial(hidden_kernel, 4),
        in_specs=[smem()] + [vmem()] * 8,
        out_specs=vmem(),
        out_shape=jax.ShapeDtypeStruct((tokens, f), jnp.bfloat16),
        scratch_shapes=[pltpu.VMEM((2, tokens, f), jnp.float32)],
        compiler_params=pltpu.CompilerParams(
            vmem_limit_bytes=room(sr, r2, w_gate, w_up, *[total] * 5)
        ),
        cost_estimate=pl.CostEstimate(
            flops=2 * tokens * d * f,
            bytes_accessed=tokens * d + 2 * d * f + 10 * tokens * f,
            transcendentals=tokens * f,
        ),
        name="expert_hidden",
    )(core, sr, r2, w_gate, w_up, *parts)


def back_kernel(
    experts, begin, chunks, at_ref, own_ref, other_ref, sr_ref, r2_ref, down_ref, keep_ref, *send_refs
):
    block = down_ref.shape[2] // chunks
    f = own_ref.shape[1]
    piece = keep_ref.shape[0]
    group = sr_ref.shape[0] // 2
    lanes = 128 * (-(-3 * experts // 128))
    core = at_ref[1]

    def rows(ref, order):
        return jnp.concatenate(
            [ref[i * group + begin : i * group + begin + piece] for i in order], axis=0
        )

    own = rows(own_ref, (0, 1, 2, 3))
    other = rows(other_ref, (0, 2, 1, 3))
    first = pl.multiple_of(core * f, 128)
    rest = pl.multiple_of((1 - core) * f, 128)
    probs = jnp.concatenate(
        [
            ref[i * group + begin : i * group + begin + piece, ref.shape[1] - lanes :].astype(
                jnp.float32
            )
            for ref in (sr_ref, r2_ref)
            for i in (0, 1)
        ],
        axis=0,
    )
    lane = lax.broadcasted_iota(jnp.int32, probs.shape, 1)
    mine = lane % experts == at_ref[0]
    weight = jnp.sum(jnp.where(mine, probs, 0.0), axis=1, keepdims=True)
    for c in range(chunks):
        at = slice(c * block, (c + 1) * block)
        total = jnp.dot(own, down_ref[0, pl.ds(first, f), at], preferred_element_type=jnp.float32)
        total += jnp.dot(
            other, down_ref[0, pl.ds(rest, f), at], preferred_element_type=jnp.float32
        )
        total = total * weight
        keep_ref[:, at] = total[:piece]
        for i, ref in enumerate(send_refs):
            ref[:, at] = total[(i + 1) * piece : (i + 2) * piece].astype(ref.dtype)


def expert_back(experts, begin, piece, at, own, other, w_down, sr, r2):
    f = own.shape[1]
    width = w_down.shape[2]
    rows = 4 * piece
    send = jax.ShapeDtypeStruct((piece, width), jnp.bfloat16)
    keep = jax.ShapeDtypeStruct((piece, width), jnp.float32)
    return pl.pallas_call(
        functools.partial(back_kernel, experts, begin, 4),
        out_shape=[keep, send, send, send],
        in_specs=[smem()] + [vmem()] * 5,
        out_specs=[vmem()] * 4,
        compiler_params=pltpu.CompilerParams(
            vmem_limit_bytes=room(own, other, w_down, sr, r2, *[keep] * 4)
        ),
        cost_estimate=pl.CostEstimate(
            flops=4 * rows * f * width,
            bytes_accessed=2 * (4 * rows * f + 2 * f * width + 2 * rows * width),
            transcendentals=0,
        ),
        name="expert_back",
    )(at, own, other, sr, r2, w_down)


class Moves:
    def __init__(self, owners):
        self.owners = owners
        self.lines = owners // 4

    def go(self, x, where):
        perm = [
            (ep * 2 + core, where(ep, core)) for ep in range(self.owners) for core in range(2)
        ]
        return lax.ppermute(x, ("ep", "pd"), perm)

    def along_z(self, x, turn):
        return self.go(x, lambda ep, core: (ep ^ (4 * turn)) * 2 + core)

    def flip(self, x, turn):
        return self.go(x, lambda ep, core: (ep ^ (1 << ((core + turn) % 2))) * 2 + core)

    def diagonal(self, x):
        return self.go(x, lambda ep, core: (ep ^ 3) * 2 + core)

    def cores(self, x):
        return self.go(x, lambda ep, core: ep * 2 + 1 - core)


def body(
    prompt_kv,
    page_owner,
    page_slot,
    page_fill,
    queries,
    new_kv,
    moe_input,
    expert_routes,
    route_probs,
    w_gate,
    w_up,
    w_down,
):
    owners = lax.axis_size("ep")
    me = lax.axis_index("ep").astype(jnp.int32)
    me_ref = me.reshape(1)
    core = lax.axis_index("pd").astype(jnp.int32)
    pages, _, page_len, heads, width = prompt_kv.shape
    requests, steps, q_heads, _ = queries.shape
    d = moe_input.shape[2]
    tokens = requests * steps
    slots = owners * CAP

    moves = Moves(owners)
    top = expert_routes.shape[2]
    lanes = -(-3 * owners // 128) * 128
    at = jnp.stack([me, core])
    own_core = core.reshape(1)
    mine = pl.pallas_call(
        functools.partial(pack_kernel, owners),
        out_shape=jax.ShapeDtypeStruct((tokens, d // 2 + lanes), jnp.bfloat16),
        in_specs=[smem()] + [vmem()] * 3,
        out_specs=vmem(),
        name="pack_tokens",
    )(
        own_core,
        moe_input.transpose(1, 0, 2).reshape(tokens, d),
        expert_routes.reshape(tokens, top),
        route_probs.transpose(1, 0, 2).reshape(tokens, top),
    )
    send = pl.pallas_call(
        functools.partial(page_kernel, pages),
        out_shape=jax.ShapeDtypeStruct((slots, 2, heads, page_len, width), jnp.bfloat16),
        in_specs=[smem(), smem()] + [vmem()],
        out_specs=vmem(),
        scratch_shapes=[pltpu.SMEM((owners,), jnp.int32)],
        compiler_params=pltpu.CompilerParams(vmem_limit_bytes=room(*[prompt_kv] * 5)),
        name="quantize_pages",
    )(me_ref, page_owner.reshape(-1), prompt_kv.transpose(0, 1, 3, 2, 4))

    sets = [range(0, moves.lines, 2), range(1, moves.lines, 2)]
    line = [moves.along_z(mine, turn) if turn else mine for chips in sets for turn in chips]
    line = jnp.concatenate(line, axis=0)
    line, send = lax.optimization_barrier((line, send))
    fresh = new_kv.transpose(2, 3, 0, 1, 4).reshape(2, heads, tokens, width)
    fresh = jnp.pad(fresh, ((0, 0), (0, 0), (0, 128 - tokens), (0, 0)))
    tables = [t.reshape(owners, pages) for t in (page_owner, page_slot, page_fill)]
    sr = jnp.concatenate([line, moves.flip(line, 0)], axis=0)
    sr, fresh, tables = lax.optimization_barrier((sr, fresh, tables))
    r2 = moves.flip(sr, 1)

    cache = lax.all_to_all(send, "ep", split_axis=0, concat_axis=0, tiled=True)

    early = expert_partial(own_core, sr, w_gate, w_up)
    r2, cache, early = lax.optimization_barrier((r2, cache, early))
    other_sr, other_r2 = moves.cores(sr), moves.cores(r2)
    parts = early + expert_partial(own_core, r2, w_gate, w_up)
    hidden = expert_hidden(own_core, other_sr, other_r2, w_gate, w_up, parts)
    other_hidden = moves.cores(hidden)
    piece = line.shape[0] // 2
    backs = [
        expert_back(owners, begin, piece, at, hidden, other_hidden, w_down, sr, r2)
        for begin in (piece, 0)
    ]
    attn_out = pl.pallas_call(
        functools.partial(attention_kernel, pages),
        out_shape=jax.ShapeDtypeStruct(queries.shape, jnp.bfloat16),
        in_specs=[smem()] + [vmem()] * 6 + [pl.BlockSpec(memory_space=pl.ANY)],
        out_specs=vmem(),
        compiler_params=pltpu.CompilerParams(
            vmem_limit_bytes=8 * MIB + 16 * slots * page_len * tokens * q_heads
        ),
        name="attention",
    )(
        me_ref,
        *tables,
        queries,
        cache,
        fresh,
        backs[1][1],
    )
    sums = []
    for total, *send in backs:
        for rows in (moves.flip(send[0], 0), moves.flip(send[1], 1), moves.diagonal(send[2])):
            total = total + rows.astype(jnp.float32)
        sums.append(total)
    sums[0], attn_out = lax.optimization_barrier((sums[0], attn_out))
    moe = sums[1][:tokens]
    for chips, rows in zip(sets, reversed(sums)):
        for i, turn in enumerate(chips):
            if turn:
                block = rows[i * tokens : (i + 1) * tokens].astype(jnp.bfloat16)
                moe = moe + moves.along_z(block, turn).astype(jnp.float32)
    moe = moe.astype(jnp.bfloat16)
    moe_out = moe.reshape(steps, requests, d // 2).transpose(1, 0, 2)

    return (attn_out, moe_out)


def solution(mesh):
    return jax.shard_map(
        body,
        mesh=mesh,
        in_specs=(
            P(("grp", "ep"), None, None, "pd", None),
            P("grp", None),
            P("grp"),
            P("grp"),
            P(("grp", "ep"), None, "pd", None),
            P(("grp", "ep"), None, None, "pd", None),
            P(("grp", "ep"), None, None),
            P(None, ("grp", "ep"), None),
            P(("grp", "ep"), None, None),
            P("ep", None, "pd"),
            P("ep", None, "pd"),
            P("ep", None, "pd"),
        ),
        out_specs=(P(("grp", "ep"), None, "pd", None), P(("grp", "ep"), None, "pd")),
        check_vma=False,
    )
```

```python
import functools
import math

import jax
import jax.numpy as jnp
from jax import lax
from jax.experimental import pallas as pl
from jax.experimental.pallas import tpu as pltpu
from jax.sharding import PartitionSpec as P

CAP = 2
LIMIT = 448.0
MIB = 1024 * 1024


def vmem():
    return pl.BlockSpec(memory_space=pltpu.VMEM)


def smem():
    return pl.BlockSpec(memory_space=pltpu.SMEM)


def page_kernel(pages, me_ref, owner_ref, kv_ref, send_ref, count_ref):
    values = kv_ref[...].astype(jnp.float32)
    largest = jnp.max(jnp.abs(values), axis=(3, 4), keepdims=True)
    scale = jnp.full(largest.shape, 2.0 ** (-16), jnp.float32)
    inverse = jnp.full(largest.shape, 2.0**16, jnp.float32)
    for exponent in range(-16, 4):
        exceeds = largest > LIMIT * 2.0**exponent
        scale = jnp.where(exceeds, scale * 2.0, scale)
        inverse = jnp.where(exceeds, inverse * 0.5, inverse)
    scaled = values * inverse
    magnitude = jnp.abs(scaled)
    step = jnp.full(scaled.shape, 2.0 ** (-9), jnp.float32)
    back = jnp.full(scaled.shape, 2.0**9, jnp.float32)
    for exponent in range(-5, 9):
        exceeds = magnitude >= 2.0**exponent
        step = jnp.where(exceeds, step * 2.0, step)
        back = jnp.where(exceeds, back * 0.5, back)
    levels = jnp.minimum(jnp.floor(magnitude * back + 0.5) * step, LIMIT)
    cache = (jnp.where(scaled < 0.0, -levels, levels) * scale).astype(jnp.bfloat16)

    send_ref[...] = jnp.zeros(send_ref.shape, send_ref.dtype)

    def clear(o, carry):
        count_ref[o] = 0
        return carry

    lax.fori_loop(0, count_ref.shape[0], clear, 0)
    first = me_ref[0] * pages
    for page in range(pages):
        owner = owner_ref[first + page]
        rank = count_ref[owner]
        count_ref[owner] = rank + 1
        send_ref[pl.ds(owner * CAP + rank, 1)] = cache[page : page + 1]


def attention_kernel(
    pages, me_ref, owner_ref, slot_ref, fill_ref, q_ref, cache_ref, fresh_ref, after_ref, out_ref
):
    owners = owner_ref.shape[0]
    slots, _, heads, page_len, width = cache_ref.shape
    requests, steps, q_heads, _ = q_ref.shape
    group = q_heads // heads
    rows = requests * steps * group
    mine = (owner_ref[...] == me_ref[0]).astype(jnp.float32)
    before = (
        lax.broadcasted_iota(jnp.int32, (pages, pages), 0)
        < lax.broadcasted_iota(jnp.int32, (pages, pages), 1)
    ).astype(jnp.float32)
    rank = jnp.dot(mine, before, preferred_element_type=jnp.float32)
    code = (slot_ref[...] * (page_len + 1) + fill_ref[...]).astype(jnp.float32)
    columns = slots * page_len
    place = lax.broadcasted_iota(jnp.int32, (owners, columns), 1)
    source = lax.broadcasted_iota(jnp.int32, (owners, columns), 0)
    spread = jnp.zeros((owners, columns), jnp.float32)
    for c in range(CAP):
        held = jnp.sum(
            jnp.where((mine > 0.0) & (rank == float(c)), code, 0.0), axis=1, keepdims=True
        )
        spread = jnp.where(place // page_len == source * CAP + c, held, spread)
    line = jnp.sum(spread, axis=0, keepdims=True).astype(jnp.int32)
    request_of = line // (page_len + 1)
    fill_of = line - request_of * (page_len + 1)
    position = lax.broadcasted_iota(jnp.int32, (1, columns), 1) % page_len
    request_of = jnp.where(position < fill_of, request_of, -1)
    row_request = lax.broadcasted_iota(jnp.int32, (rows, 1), 0) // (steps * group)
    visible = row_request == request_of
    token = lax.broadcasted_iota(jnp.int32, (rows, 1), 0) // group
    first = row_request * steps
    fresh_at = lax.broadcasted_iota(jnp.int32, (1, fresh_ref.shape[2]), 1)
    fresh_visible = (fresh_at >= first) & (fresh_at <= token)
    factor = 1.0 / math.sqrt(width)
    contract = (((1,), (1,)), ((), ()))
    for head in range(heads):
        q = q_ref[:, :, head * group : (head + 1) * group, :].reshape(rows, width)
        keys = cache_ref[:, 0, head].reshape(columns, width)
        values = cache_ref[:, 1, head].reshape(columns, width)
        scores = lax.dot_general(q, keys, contract, preferred_element_type=jnp.float32) * factor
        fresh = (
            lax.dot_general(q, fresh_ref[0, head], contract, preferred_element_type=jnp.float32)
            * factor
        )
        scores = jnp.where(visible, scores, -jnp.inf)
        fresh = jnp.where(fresh_visible, fresh, -jnp.inf)
        peak = jnp.maximum(
            jnp.max(scores, axis=1, keepdims=True), jnp.max(fresh, axis=1, keepdims=True)
        )
        weight = jnp.exp(scores - peak)
        fresh_weight = jnp.exp(fresh - peak)
        total = jnp.sum(weight, axis=1, keepdims=True) + jnp.sum(
            fresh_weight, axis=1, keepdims=True
        )
        mixed = jnp.dot(
            weight.astype(jnp.bfloat16), values, preferred_element_type=jnp.float32
        ) + jnp.dot(
            fresh_weight.astype(jnp.bfloat16), fresh_ref[1, head], preferred_element_type=jnp.float32
        )
        out_ref[:, :, head * group : (head + 1) * group, :] = (
            (mixed / total).astype(out_ref.dtype).reshape(requests, steps, group, width)
        )


def pack_kernel(experts, core_ref, x_ref, route_ref, prob_ref, out_ref):
    half = x_ref.shape[1] // 2
    begin = pl.multiple_of(core_ref[0] * half, 128)
    out_ref[:, :half] = x_ref[:, pl.ds(begin, half)]
    shape = (x_ref.shape[0], out_ref.shape[1] - half)
    lane = lax.broadcasted_iota(jnp.int32, shape, 1)
    expert = lane % experts
    part = lane // experts
    dense = jnp.zeros(shape, jnp.float32)
    for k in range(route_ref.shape[1]):
        dense += jnp.where(route_ref[:, k : k + 1] == expert, prob_ref[:, k : k + 1], 0.0)
    high = dense.astype(jnp.bfloat16).astype(jnp.float32)
    middle = (dense - high).astype(jnp.bfloat16).astype(jnp.float32)
    low = dense - high - middle
    chosen = jnp.where(part == 0, high, jnp.where(part == 1, middle, low))
    out_ref[:, half:] = jnp.where(part < 3, chosen, 0.0).astype(out_ref.dtype)


def partial_kernel(chunks, core_ref, x_ref, gate_ref, up_ref, gate_sum, up_sum):
    half = gate_ref.shape[1] // 2
    depth = half // chunks
    for c in range(chunks):
        at = slice(c * depth, (c + 1) * depth)
        rows = pl.ds(pl.multiple_of(core_ref[0] * half + c * depth, 128), depth)
        for weight, total in ((gate_ref, gate_sum), (up_ref, up_sum)):
            part = jnp.dot(x_ref[:, at], weight[0, rows], preferred_element_type=jnp.float32)
            total[...] = part if c == 0 else total[...] + part


def hidden_kernel(
    chunks, core_ref, sr_ref, r2_ref, gate_ref, up_ref, g0_ref, u0_ref, g1_ref, u1_ref, out_ref, sums
):
    half = gate_ref.shape[1] // 2
    depth = half // chunks
    group = sr_ref.shape[0] // 2
    for c in range(chunks):
        at = slice(c * depth, (c + 1) * depth)
        rows = pl.ds(pl.multiple_of((1 - core_ref[0]) * half + c * depth, 128), depth)
        x = jnp.concatenate(
            [sr_ref[:group, at], r2_ref[:group, at], sr_ref[group:, at], r2_ref[group:, at]],
            axis=0,
        )
        for i, (weight, early, late) in enumerate(
            ((gate_ref, g0_ref, g1_ref), (up_ref, u0_ref, u1_ref))
        ):
            part = jnp.dot(x, weight[0, rows], preferred_element_type=jnp.float32)
            if c == 0:
                sums[i, : 2 * group] = early[...] + part[: 2 * group]
                sums[i, 2 * group :] = late[...] + part[2 * group :]
            else:
                sums[i] += part
    gate = sums[0]
    out_ref[...] = (gate / (1.0 + jnp.exp(-gate)) * sums[1]).astype(out_ref.dtype)


def room(*arrays):
    return sum(math.prod(a.shape) * a.dtype.itemsize for a in arrays) * 9 // 8 + 4 * MIB


def expert_partial(core, x, w_gate, w_up):
    tokens = x.shape[0]
    d, f = w_gate.shape[1:]
    total = jax.ShapeDtypeStruct((tokens, f), jnp.float32)
    return pl.pallas_call(
        functools.partial(partial_kernel, 4),
        in_specs=[smem()] + [vmem()] * 3,
        out_specs=[vmem(), vmem()],
        out_shape=[total, total],
        compiler_params=pltpu.CompilerParams(vmem_limit_bytes=room(x, w_gate, w_up, total, total)),
        cost_estimate=pl.CostEstimate(
            flops=2 * tokens * d * f,
            bytes_accessed=tokens * d + 2 * d * f + 8 * tokens * f,
            transcendentals=0,
        ),
        name="expert_partial",
    )(core, x, w_gate, w_up)


def expert_hidden(core, sr, r2, w_gate, w_up, parts):
    tokens = 2 * sr.shape[0]
    d, f = w_gate.shape[1:]
    total = jax.ShapeDtypeStruct((tokens, f), jnp.float32)
    return pl.pallas_call(
        functools.partial(hidden_kernel, 4),
        in_specs=[smem()] + [vmem()] * 8,
        out_specs=vmem(),
        out_shape=jax.ShapeDtypeStruct((tokens, f), jnp.bfloat16),
        scratch_shapes=[pltpu.VMEM((2, tokens, f), jnp.float32)],
        compiler_params=pltpu.CompilerParams(
            vmem_limit_bytes=room(sr, r2, w_gate, w_up, *[total] * 5)
        ),
        cost_estimate=pl.CostEstimate(
            flops=2 * tokens * d * f,
            bytes_accessed=tokens * d + 2 * d * f + 10 * tokens * f,
            transcendentals=tokens * f,
        ),
        name="expert_hidden",
    )(core, sr, r2, w_gate, w_up, *parts)


def back_kernel(
    experts, begin, chunks, at_ref, own_ref, other_ref, sr_ref, r2_ref, down_ref, keep_ref, *send_refs
):
    block = down_ref.shape[2] // chunks
    f = own_ref.shape[1]
    piece = keep_ref.shape[0]
    group = sr_ref.shape[0] // 2
    lanes = 128 * (-(-3 * experts // 128))
    core = at_ref[1]

    def rows(ref, order):
        return jnp.concatenate(
            [ref[i * group + begin : i * group + begin + piece] for i in order], axis=0
        )

    own = rows(own_ref, (0, 1, 2, 3))
    other = rows(other_ref, (0, 2, 1, 3))
    first = pl.multiple_of(core * f, 128)
    rest = pl.multiple_of((1 - core) * f, 128)
    probs = jnp.concatenate(
        [
            ref[i * group + begin : i * group + begin + piece, ref.shape[1] - lanes :].astype(
                jnp.float32
            )
            for ref in (sr_ref, r2_ref)
            for i in (0, 1)
        ],
        axis=0,
    )
    lane = lax.broadcasted_iota(jnp.int32, probs.shape, 1)
    mine = lane % experts == at_ref[0]
    weight = jnp.sum(jnp.where(mine, probs, 0.0), axis=1, keepdims=True)
    for c in range(chunks):
        at = slice(c * block, (c + 1) * block)
        total = jnp.dot(own, down_ref[0, pl.ds(first, f), at], preferred_element_type=jnp.float32)
        total += jnp.dot(
            other, down_ref[0, pl.ds(rest, f), at], preferred_element_type=jnp.float32
        )
        total = total * weight
        keep_ref[:, at] = total[:piece]
        for i, ref in enumerate(send_refs):
            ref[:, at] = total[(i + 1) * piece : (i + 2) * piece].astype(ref.dtype)


def expert_back(experts, begin, piece, at, own, other, w_down, sr, r2):
    f = own.shape[1]
    width = w_down.shape[2]
    rows = 4 * piece
    send = jax.ShapeDtypeStruct((piece, width), jnp.bfloat16)
    keep = jax.ShapeDtypeStruct((piece, width), jnp.float32)
    return pl.pallas_call(
        functools.partial(back_kernel, experts, begin, 4),
        out_shape=[keep, send, send, send],
        in_specs=[smem()] + [vmem()] * 5,
        out_specs=[vmem()] * 4,
        compiler_params=pltpu.CompilerParams(
            vmem_limit_bytes=room(own, other, w_down, sr, r2, *[keep] * 4)
        ),
        cost_estimate=pl.CostEstimate(
            flops=4 * rows * f * width,
            bytes_accessed=2 * (4 * rows * f + 2 * f * width + 2 * rows * width),
            transcendentals=0,
        ),
        name="expert_back",
    )(at, own, other, sr, r2, w_down)


class Moves:
    def __init__(self, owners):
        self.owners = owners
        self.lines = owners // 4

    def go(self, x, where):
        perm = [
            (ep * 2 + core, where(ep, core)) for ep in range(self.owners) for core in range(2)
        ]
        return lax.ppermute(x, ("ep", "pd"), perm)

    def along_z(self, x, turn):
        return self.go(x, lambda ep, core: (ep ^ (4 * turn)) * 2 + core)

    def flip(self, x, turn):
        return self.go(x, lambda ep, core: (ep ^ (1 << ((core + turn) % 2))) * 2 + core)

    def diagonal(self, x):
        return self.go(x, lambda ep, core: (ep ^ 3) * 2 + core)

    def cores(self, x):
        return self.go(x, lambda ep, core: ep * 2 + 1 - core)


def body(
    prompt_kv,
    page_owner,
    page_slot,
    page_fill,
    queries,
    new_kv,
    moe_input,
    expert_routes,
    route_probs,
    w_gate,
    w_up,
    w_down,
):
    owners = lax.axis_size("ep")
    me = lax.axis_index("ep").astype(jnp.int32)
    me_ref = me.reshape(1)
    core = lax.axis_index("pd").astype(jnp.int32)
    pages, _, page_len, heads, width = prompt_kv.shape
    requests, steps, q_heads, _ = queries.shape
    d = moe_input.shape[2]
    tokens = requests * steps
    slots = owners * CAP

    moves = Moves(owners)
    top = expert_routes.shape[2]
    lanes = -(-3 * owners // 128) * 128
    at = jnp.stack([me, core])
    own_core = core.reshape(1)
    mine = pl.pallas_call(
        functools.partial(pack_kernel, owners),
        out_shape=jax.ShapeDtypeStruct((tokens, d // 2 + lanes), jnp.bfloat16),
        in_specs=[smem()] + [vmem()] * 3,
        out_specs=vmem(),
        compiler_params=pltpu.CompilerParams(vmem_limit_bytes=room(moe_input, moe_input)),
        name="pack_tokens",
    )(
        own_core,
        moe_input.transpose(1, 0, 2).reshape(tokens, d),
        expert_routes.reshape(tokens, top),
        route_probs.transpose(1, 0, 2).reshape(tokens, top),
    )
    send = pl.pallas_call(
        functools.partial(page_kernel, pages),
        out_shape=jax.ShapeDtypeStruct((slots, 2, heads, page_len, width), jnp.bfloat16),
        in_specs=[smem(), smem()] + [vmem()],
        out_specs=vmem(),
        scratch_shapes=[pltpu.SMEM((owners,), jnp.int32)],
        compiler_params=pltpu.CompilerParams(vmem_limit_bytes=room(*[prompt_kv] * 5)),
        name="quantize_pages",
    )(me_ref, page_owner.reshape(-1), prompt_kv.transpose(0, 1, 3, 2, 4))

    sets = [range(0, moves.lines, 2), range(1, moves.lines, 2)]
    line = [moves.along_z(mine, turn) if turn else mine for chips in sets for turn in chips]
    line = jnp.concatenate(line, axis=0)
    line, send = lax.optimization_barrier((line, send))
    fresh = new_kv.transpose(2, 3, 0, 1, 4).reshape(2, heads, tokens, width)
    fresh = jnp.pad(fresh, ((0, 0), (0, 0), (0, 128 - tokens), (0, 0)))
    tables = [t.reshape(owners, pages) for t in (page_owner, page_slot, page_fill)]
    sr = jnp.concatenate([line, moves.flip(line, 0)], axis=0)
    sr, fresh, tables = lax.optimization_barrier((sr, fresh, tables))
    r2 = moves.flip(sr, 1)

    cache = lax.all_to_all(send, "ep", split_axis=0, concat_axis=0, tiled=True)

    early = expert_partial(own_core, sr, w_gate, w_up)
    r2, cache, early = lax.optimization_barrier((r2, cache, early))
    other_sr, other_r2 = moves.cores(sr), moves.cores(r2)
    parts = early + expert_partial(own_core, r2, w_gate, w_up)
    hidden = expert_hidden(own_core, other_sr, other_r2, w_gate, w_up, parts)
    other_hidden = moves.cores(hidden)
    piece = line.shape[0] // 2
    backs = [
        expert_back(owners, begin, piece, at, hidden, other_hidden, w_down, sr, r2)
        for begin in (piece, 0)
    ]
    attn_out = pl.pallas_call(
        functools.partial(attention_kernel, pages),
        out_shape=jax.ShapeDtypeStruct(queries.shape, jnp.bfloat16),
        in_specs=[smem()] + [vmem()] * 6 + [pl.BlockSpec(memory_space=pl.ANY)],
        out_specs=vmem(),
        compiler_params=pltpu.CompilerParams(
            vmem_limit_bytes=8 * MIB + 16 * slots * page_len * tokens * q_heads
        ),
        name="attention",
    )(
        me_ref,
        *tables,
        queries,
        cache,
        fresh,
        backs[1][1],
    )
    sums = []
    for total, *send in backs:
        for rows in (moves.flip(send[0], 0), moves.flip(send[1], 1), moves.diagonal(send[2])):
            total = total + rows.astype(jnp.float32)
        sums.append(total)
    sums[0], attn_out = lax.optimization_barrier((sums[0], attn_out))
    moe = sums[1][:tokens]
    for chips, rows in zip(sets, reversed(sums)):
        for i, turn in enumerate(chips):
            if turn:
                block = rows[i * tokens : (i + 1) * tokens].astype(jnp.bfloat16)
                moe = moe + moves.along_z(block, turn).astype(jnp.float32)
    moe = moe.astype(jnp.bfloat16)
    moe_out = moe.reshape(steps, requests, d // 2).transpose(1, 0, 2)

    return (attn_out, moe_out)


def solution(mesh):
    return jax.shard_map(
        body,
        mesh=mesh,
        in_specs=(
            P(("grp", "ep"), None, None, "pd", None),
            P("grp", None),
            P("grp"),
            P("grp"),
            P(("grp", "ep"), None, "pd", None),
            P(("grp", "ep"), None, None, "pd", None),
            P(("grp", "ep"), None, None),
            P(None, ("grp", "ep"), None),
            P(("grp", "ep"), None, None),
            P("ep", None, "pd"),
            P("ep", None, "pd"),
            P("ep", None, "pd"),
        ),
        out_specs=(P(("grp", "ep"), None, "pd", None), P(("grp", "ep"), None, "pd")),
        check_vma=False,
    )
```

```python
import functools
import math

import jax
import jax.numpy as jnp
from jax import lax
from jax.experimental import pallas as pl
from jax.experimental.pallas import tpu as pltpu
from jax.sharding import PartitionSpec as P

CAP = 2
LIMIT = 448.0
MIB = 1024 * 1024


def vmem():
    return pl.BlockSpec(memory_space=pltpu.VMEM)


def smem():
    return pl.BlockSpec(memory_space=pltpu.SMEM)


def page_kernel(pages, me_ref, owner_ref, kv_ref, *refs):
    out_refs, placed_ref, count_ref = refs[:4], refs[4], refs[5]
    values = kv_ref[...].astype(jnp.float32)
    largest = jnp.max(jnp.abs(values), axis=(3, 4), keepdims=True)
    scale = jnp.full(largest.shape, 2.0 ** (-16), jnp.float32)
    inverse = jnp.full(largest.shape, 2.0**16, jnp.float32)
    for exponent in range(-16, -6):
        exceeds = largest > LIMIT * 2.0**exponent
        scale = jnp.where(exceeds, scale * 2.0, scale)
        inverse = jnp.where(exceeds, inverse * 0.5, inverse)
    scaled = values * inverse
    rest = jnp.abs(scaled) * 2.0**6
    step = jnp.full(scaled.shape, 2.0 ** (-9), jnp.float32)
    for bits in (8, 4, 2, 1):
        exceeds = rest >= 2.0**bits
        rest = jnp.where(exceeds, rest * 2.0**-bits, rest)
        step = jnp.where(exceeds, step * 2.0**bits, step)
    levels = jnp.minimum(jnp.floor(rest * 8.0 + 0.5) * step, LIMIT)
    cache = (jnp.where(scaled < 0.0, -levels, levels) * scale).astype(jnp.bfloat16)

    placed_ref[...] = jnp.zeros(placed_ref.shape, placed_ref.dtype)

    def clear(o, carry):
        count_ref[o] = 0
        return carry

    lax.fori_loop(0, count_ref.shape[0], clear, 0)
    me = me_ref[0]
    slots = out_refs[0].shape[0]
    for page in range(pages):
        owner = owner_ref[me * pages + page]
        rank = count_ref[owner]
        count_ref[owner] = rank + 1
        apart = owner ^ me
        slot = (apart & 3) * slots + (apart >> 2) * CAP + rank
        placed_ref[pl.ds(slot, 1)] = cache[page : page + 1]
    for k, ref in enumerate(out_refs):
        ref[...] = placed_ref[k * slots : (k + 1) * slots]


def regroup_kernel(*refs):
    in_refs, out_refs = refs[:4], refs[4:]
    for z, out in enumerate(out_refs):
        for k, ref in enumerate(in_refs):
            out[k * CAP : (k + 1) * CAP] = ref[z * CAP : (z + 1) * CAP]


def attention_kernel(
    pages, me_ref, owner_ref, slot_ref, fill_ref, q_ref, fresh_ref, after_ref, *refs
):
    cache_refs, out_ref = refs[:-1], refs[-1]
    owners = owner_ref.shape[0]
    _, _, heads, page_len, width = cache_refs[0].shape
    slots = owners * CAP
    requests, steps, q_heads, _ = q_ref.shape
    group = q_heads // heads
    rows = requests * steps * group
    mine = (owner_ref[...] == me_ref[0]).astype(jnp.float32)
    before = (
        lax.broadcasted_iota(jnp.int32, (pages, pages), 0)
        < lax.broadcasted_iota(jnp.int32, (pages, pages), 1)
    ).astype(jnp.float32)
    rank = jnp.dot(mine, before, preferred_element_type=jnp.float32)
    code = (slot_ref[...] * (page_len + 1) + fill_ref[...]).astype(jnp.float32)
    columns = slots * page_len
    place = lax.broadcasted_iota(jnp.int32, (owners, columns), 1)
    source = lax.broadcasted_iota(jnp.int32, (owners, columns), 0)
    spread = jnp.zeros((owners, columns), jnp.float32)
    for c in range(CAP):
        held = jnp.sum(
            jnp.where((mine > 0.0) & (rank == float(c)), code, 0.0), axis=1, keepdims=True
        )
        spread = jnp.where(place // page_len == (source ^ me_ref[0]) * CAP + c, held, spread)
    line = jnp.sum(spread, axis=0, keepdims=True).astype(jnp.int32)
    request_of = line // (page_len + 1)
    fill_of = line - request_of * (page_len + 1)
    position = lax.broadcasted_iota(jnp.int32, (1, columns), 1) % page_len
    request_of = jnp.where(position < fill_of, request_of, -1)
    row_request = lax.broadcasted_iota(jnp.int32, (rows, 1), 0) // (steps * group)
    visible = row_request == request_of
    token = lax.broadcasted_iota(jnp.int32, (rows, 1), 0) // group
    first = row_request * steps
    fresh_at = lax.broadcasted_iota(jnp.int32, (1, fresh_ref.shape[2]), 1)
    fresh_visible = (fresh_at >= first) & (fresh_at <= token)
    factor = 1.0 / math.sqrt(width)
    contract = (((1,), (1,)), ((), ()))
    for head in range(heads):
        q = q_ref[:, :, head * group : (head + 1) * group, :].reshape(rows, width)
        keys, values = (
            jnp.concatenate(
                [ref[:, i, head].reshape(ref.shape[0] * page_len, width) for ref in cache_refs],
                axis=0,
            )
            for i in range(2)
        )
        scores = lax.dot_general(q, keys, contract, preferred_element_type=jnp.float32) * factor
        fresh = (
            lax.dot_general(q, fresh_ref[0, head], contract, preferred_element_type=jnp.float32)
            * factor
        )
        scores = jnp.where(visible, scores, -jnp.inf)
        fresh = jnp.where(fresh_visible, fresh, -jnp.inf)
        peak = jnp.maximum(
            jnp.max(scores, axis=1, keepdims=True), jnp.max(fresh, axis=1, keepdims=True)
        )
        weight = jnp.exp(scores - peak)
        fresh_weight = jnp.exp(fresh - peak)
        total = jnp.sum(weight, axis=1, keepdims=True) + jnp.sum(
            fresh_weight, axis=1, keepdims=True
        )
        mixed = jnp.dot(
            weight.astype(jnp.bfloat16), values, preferred_element_type=jnp.float32
        ) + jnp.dot(
            fresh_weight.astype(jnp.bfloat16), fresh_ref[1, head], preferred_element_type=jnp.float32
        )
        out_ref[:, :, head * group : (head + 1) * group, :] = (
            (mixed / total).astype(out_ref.dtype).reshape(requests, steps, group, width)
        )


def pack_kernel(experts, core_ref, x_ref, route_ref, prob_ref, out_ref):
    half = x_ref.shape[1] // 2
    begin = pl.multiple_of(core_ref[0] * half, 128)
    out_ref[:, :half] = x_ref[:, pl.ds(begin, half)]
    shape = (x_ref.shape[0], out_ref.shape[1] - half)
    lane = lax.broadcasted_iota(jnp.int32, shape, 1)
    expert = lane % experts
    part = lane // experts
    dense = jnp.zeros(shape, jnp.float32)
    for k in range(route_ref.shape[1]):
        dense += jnp.where(route_ref[:, k : k + 1] == expert, prob_ref[:, k : k + 1], 0.0)
    high = dense.astype(jnp.bfloat16).astype(jnp.float32)
    middle = (dense - high).astype(jnp.bfloat16).astype(jnp.float32)
    low = dense - high - middle
    chosen = jnp.where(part == 0, high, jnp.where(part == 1, middle, low))
    out_ref[:, half:] = jnp.where(part < 3, chosen, 0.0).astype(out_ref.dtype)


def partial_kernel(chunks, core_ref, x_ref, gate_ref, up_ref, gate_sum, up_sum):
    half = gate_ref.shape[1] // 2
    depth = half // chunks
    for c in range(chunks):
        at = slice(c * depth, (c + 1) * depth)
        rows = pl.ds(pl.multiple_of(core_ref[0] * half + c * depth, 128), depth)
        for weight, total in ((gate_ref, gate_sum), (up_ref, up_sum)):
            part = jnp.dot(x_ref[:, at], weight[0, rows], preferred_element_type=jnp.float32)
            total[...] = part if c == 0 else total[...] + part


def hidden_kernel(
    chunks, core_ref, sr_ref, r2_ref, gate_ref, up_ref, g0_ref, u0_ref, g1_ref, u1_ref, out_ref, sums
):
    half = gate_ref.shape[1] // 2
    depth = half // chunks
    group = sr_ref.shape[0] // 2
    for c in range(chunks):
        at = slice(c * depth, (c + 1) * depth)
        rows = pl.ds(pl.multiple_of((1 - core_ref[0]) * half + c * depth, 128), depth)
        x = jnp.concatenate(
            [sr_ref[:group, at], r2_ref[:group, at], sr_ref[group:, at], r2_ref[group:, at]],
            axis=0,
        )
        for i, (weight, early, late) in enumerate(
            ((gate_ref, g0_ref, g1_ref), (up_ref, u0_ref, u1_ref))
        ):
            part = jnp.dot(x, weight[0, rows], preferred_element_type=jnp.float32)
            if c == 0:
                sums[i, : 2 * group] = early[...] + part[: 2 * group]
                sums[i, 2 * group :] = late[...] + part[2 * group :]
            else:
                sums[i] += part
    gate = sums[0]
    out_ref[...] = (gate / (1.0 + jnp.exp(-gate)) * sums[1]).astype(out_ref.dtype)


def room(*arrays):
    return sum(math.prod(a.shape) * a.dtype.itemsize for a in arrays) * 9 // 8 + 4 * MIB


def expert_partial(core, x, w_gate, w_up):
    tokens = x.shape[0]
    d, f = w_gate.shape[1:]
    total = jax.ShapeDtypeStruct((tokens, f), jnp.float32)
    return pl.pallas_call(
        functools.partial(partial_kernel, 4),
        in_specs=[smem()] + [vmem()] * 3,
        out_specs=[vmem(), vmem()],
        out_shape=[total, total],
        compiler_params=pltpu.CompilerParams(vmem_limit_bytes=room(x, w_gate, w_up, total, total)),
        cost_estimate=pl.CostEstimate(
            flops=2 * tokens * d * f,
            bytes_accessed=tokens * d + 2 * d * f + 8 * tokens * f,
            transcendentals=0,
        ),
        name="expert_partial",
    )(core, x, w_gate, w_up)


def expert_hidden(core, sr, r2, w_gate, w_up, parts):
    tokens = 2 * sr.shape[0]
    d, f = w_gate.shape[1:]
    total = jax.ShapeDtypeStruct((tokens, f), jnp.float32)
    return pl.pallas_call(
        functools.partial(hidden_kernel, 4),
        in_specs=[smem()] + [vmem()] * 8,
        out_specs=vmem(),
        out_shape=jax.ShapeDtypeStruct((tokens, f), jnp.bfloat16),
        scratch_shapes=[pltpu.VMEM((2, tokens, f), jnp.float32)],
        compiler_params=pltpu.CompilerParams(
            vmem_limit_bytes=room(sr, r2, w_gate, w_up, *[total] * 5)
        ),
        cost_estimate=pl.CostEstimate(
            flops=2 * tokens * d * f,
            bytes_accessed=tokens * d + 2 * d * f + 10 * tokens * f,
            transcendentals=tokens * f,
        ),
        name="expert_hidden",
    )(core, sr, r2, w_gate, w_up, *parts)


def back_kernel(
    experts, begin, chunks, at_ref, own_ref, other_ref, sr_ref, r2_ref, down_ref, keep_ref, *send_refs
):
    block = down_ref.shape[2] // chunks
    f = own_ref.shape[1]
    piece = keep_ref.shape[0]
    group = sr_ref.shape[0] // 2
    lanes = 128 * (-(-3 * experts // 128))
    core = at_ref[1]

    def rows(ref, order):
        return jnp.concatenate(
            [ref[i * group + begin : i * group + begin + piece] for i in order], axis=0
        )

    own = rows(own_ref, (0, 1, 2, 3))
    other = rows(other_ref, (0, 2, 1, 3))
    first = pl.multiple_of(core * f, 128)
    rest = pl.multiple_of((1 - core) * f, 128)
    probs = jnp.concatenate(
        [
            ref[i * group + begin : i * group + begin + piece, ref.shape[1] - lanes :].astype(
                jnp.float32
            )
            for ref in (sr_ref, r2_ref)
            for i in (0, 1)
        ],
        axis=0,
    )
    lane = lax.broadcasted_iota(jnp.int32, probs.shape, 1)
    mine = lane % experts == at_ref[0]
    weight = jnp.sum(jnp.where(mine, probs, 0.0), axis=1, keepdims=True)
    for c in range(chunks):
        at = slice(c * block, (c + 1) * block)
        total = jnp.dot(own, down_ref[0, pl.ds(first, f), at], preferred_element_type=jnp.float32)
        total += jnp.dot(
            other, down_ref[0, pl.ds(rest, f), at], preferred_element_type=jnp.float32
        )
        total = total * weight
        keep_ref[:, at] = total[:piece]
        for i, ref in enumerate(send_refs):
            ref[:, at] = total[(i + 1) * piece : (i + 2) * piece].astype(ref.dtype)


def expert_back(experts, begin, piece, at, own, other, w_down, sr, r2):
    f = own.shape[1]
    width = w_down.shape[2]
    rows = 4 * piece
    send = jax.ShapeDtypeStruct((piece, width), jnp.bfloat16)
    keep = jax.ShapeDtypeStruct((piece, width), jnp.float32)
    return pl.pallas_call(
        functools.partial(back_kernel, experts, begin, 4),
        out_shape=[keep, send, send, send],
        in_specs=[smem()] + [vmem()] * 5,
        out_specs=[vmem()] * 4,
        compiler_params=pltpu.CompilerParams(
            vmem_limit_bytes=room(own, other, w_down, sr, r2, *[keep] * 4)
        ),
        cost_estimate=pl.CostEstimate(
            flops=4 * rows * f * width,
            bytes_accessed=2 * (4 * rows * f + 2 * f * width + 2 * rows * width),
            transcendentals=0,
        ),
        name="expert_back",
    )(at, own, other, sr, r2, w_down)


class Moves:
    def __init__(self, owners):
        self.owners = owners
        self.lines = owners // 4

    def go(self, x, where):
        perm = [
            (ep * 2 + core, where(ep, core)) for ep in range(self.owners) for core in range(2)
        ]
        return lax.ppermute(x, ("ep", "pd"), perm)

    def along_z(self, x, turn):
        return self.go(x, lambda ep, core: (ep ^ (4 * turn)) * 2 + core)

    def flip(self, x, turn):
        return self.go(x, lambda ep, core: (ep ^ (1 << ((core + turn) % 2))) * 2 + core)

    def across(self, x, turn):
        return self.go(x, lambda ep, core: (ep ^ turn) * 2 + core)

    def cores(self, x):
        return self.go(x, lambda ep, core: ep * 2 + 1 - core)


def body(
    prompt_kv,
    page_owner,
    page_slot,
    page_fill,
    queries,
    new_kv,
    moe_input,
    expert_routes,
    route_probs,
    w_gate,
    w_up,
    w_down,
):
    owners = lax.axis_size("ep")
    me = lax.axis_index("ep").astype(jnp.int32)
    me_ref = me.reshape(1)
    core = lax.axis_index("pd").astype(jnp.int32)
    pages, _, page_len, heads, width = prompt_kv.shape
    requests, steps, q_heads, _ = queries.shape
    d = moe_input.shape[2]
    tokens = requests * steps
    slots = owners * CAP

    moves = Moves(owners)
    top = expert_routes.shape[2]
    lanes = -(-3 * owners // 128) * 128
    at = jnp.stack([me, core])
    own_core = core.reshape(1)
    mine = pl.pallas_call(
        functools.partial(pack_kernel, owners),
        out_shape=jax.ShapeDtypeStruct((tokens, d // 2 + lanes), jnp.bfloat16),
        in_specs=[smem()] + [vmem()] * 3,
        out_specs=vmem(),
        compiler_params=pltpu.CompilerParams(vmem_limit_bytes=room(moe_input, moe_input)),
        name="pack_tokens",
    )(
        own_core,
        moe_input.transpose(1, 0, 2).reshape(tokens, d),
        expert_routes.reshape(tokens, top),
        route_probs.transpose(1, 0, 2).reshape(tokens, top),
    )
    page_shape = (moves.lines * CAP, 2, heads, page_len, width)
    pages_out = jax.ShapeDtypeStruct(page_shape, jnp.bfloat16)
    send = pl.pallas_call(
        functools.partial(page_kernel, pages),
        out_shape=[pages_out] * 4,
        in_specs=[smem(), smem(), vmem()],
        out_specs=[vmem()] * 4,
        scratch_shapes=[
            pltpu.VMEM((slots,) + page_shape[1:], jnp.bfloat16),
            pltpu.SMEM((owners,), jnp.int32),
        ],
        compiler_params=pltpu.CompilerParams(vmem_limit_bytes=room(*[prompt_kv] * 8)),
        name="quantize_pages",
    )(me_ref, page_owner.reshape(-1), prompt_kv.transpose(0, 1, 3, 2, 4))

    sets = [range(0, moves.lines, 2), range(1, moves.lines, 2)]
    line = [moves.along_z(mine, turn) if turn else mine for chips in sets for turn in chips]
    line = jnp.concatenate(line, axis=0)
    line, send = lax.optimization_barrier((line, send))
    held = [send[0]] + [moves.across(send[turn], turn) for turn in (1, 2, 3)]
    held = pl.pallas_call(
        regroup_kernel,
        out_shape=[jax.ShapeDtypeStruct((4 * CAP,) + page_shape[1:], jnp.bfloat16)] * moves.lines,
        in_specs=[vmem()] * 4,
        out_specs=[vmem()] * moves.lines,
        compiler_params=pltpu.CompilerParams(vmem_limit_bytes=room(*[pages_out] * 8)),
        name="regroup_pages",
    )(*held)
    fresh = new_kv.transpose(2, 3, 0, 1, 4).reshape(2, heads, tokens, width)
    fresh = jnp.pad(fresh, ((0, 0), (0, 0), (0, 128 - tokens), (0, 0)))
    tables = [t.reshape(owners, pages) for t in (page_owner, page_slot, page_fill)]
    sr = jnp.concatenate([line, moves.flip(line, 0)], axis=0)
    sr, held, fresh, tables = lax.optimization_barrier((sr, held, fresh, tables))
    cache = [moves.along_z(x, turn) if turn else x for turn, x in enumerate(held)]
    r2 = moves.flip(sr, 1)


    early = expert_partial(own_core, sr, w_gate, w_up)
    r2, early = lax.optimization_barrier((r2, early))
    other_sr, other_r2 = moves.cores(sr), moves.cores(r2)
    parts = early + expert_partial(own_core, r2, w_gate, w_up)
    core_then, cache = lax.optimization_barrier((own_core, cache))
    hidden = expert_hidden(core_then, other_sr, other_r2, w_gate, w_up, parts)
    other_hidden = moves.cores(hidden)
    piece = line.shape[0] // 2
    backs = [
        expert_back(owners, begin, piece, at, hidden, other_hidden, w_down, sr, r2)
        for begin in (piece, 0)
    ]
    attn_out = pl.pallas_call(
        functools.partial(attention_kernel, pages),
        out_shape=jax.ShapeDtypeStruct(queries.shape, jnp.bfloat16),
        in_specs=[smem()]
        + [vmem()] * 5
        + [pl.BlockSpec(memory_space=pl.ANY)]
        + [vmem()] * moves.lines,
        out_specs=vmem(),
        compiler_params=pltpu.CompilerParams(
            vmem_limit_bytes=8 * MIB + 16 * slots * page_len * tokens * q_heads
        ),
        name="attention",
    )(
        me_ref,
        *tables,
        queries,
        fresh,
        backs[1][1],
        *cache,
    )
    sums = []
    for total, *send in backs:
        for rows in (moves.flip(send[0], 0), moves.flip(send[1], 1), moves.across(send[2], 3)):
            total = total + rows.astype(jnp.float32)
        sums.append(total)
    sums[0], attn_out = lax.optimization_barrier((sums[0], attn_out))
    moe = sums[1][:tokens]
    for chips, rows in zip(sets, reversed(sums)):
        for i, turn in enumerate(chips):
            if turn:
                block = rows[i * tokens : (i + 1) * tokens].astype(jnp.bfloat16)
                moe = moe + moves.along_z(block, turn).astype(jnp.float32)
    moe = moe.astype(jnp.bfloat16)
    moe_out = moe.reshape(steps, requests, d // 2).transpose(1, 0, 2)

    return (attn_out, moe_out)


def solution(mesh):
    return jax.shard_map(
        body,
        mesh=mesh,
        in_specs=(
            P(("grp", "ep"), None, None, "pd", None),
            P("grp", None),
            P("grp"),
            P("grp"),
            P(("grp", "ep"), None, "pd", None),
            P(("grp", "ep"), None, None, "pd", None),
            P(("grp", "ep"), None, None),
            P(None, ("grp", "ep"), None),
            P(("grp", "ep"), None, None),
            P("ep", None, "pd"),
            P("ep", None, "pd"),
            P("ep", None, "pd"),
        ),
        out_specs=(P(("grp", "ep"), None, "pd", None), P(("grp", "ep"), None, "pd")),
        check_vma=False,
    )
```

```python
import functools
import math

import jax
import jax.numpy as jnp
from jax import lax
from jax.experimental import pallas as pl
from jax.experimental.pallas import tpu as pltpu
from jax.sharding import PartitionSpec as P

CAP = 2
LIMIT = 448.0
MIB = 1024 * 1024
LARGE = 49 * MIB


def vmem():
    return pl.BlockSpec(memory_space=pltpu.VMEM)


def smem():
    return pl.BlockSpec(memory_space=pltpu.SMEM)


def hbm():
    return pl.BlockSpec(memory_space=pltpu.HBM)


def page_kernel(pages, me_ref, owner_ref, kv_ref, send_ref, count_ref):
    values = kv_ref[...].astype(jnp.float32)
    largest = jnp.max(jnp.abs(values), axis=(3, 4), keepdims=True)
    scale = jnp.full(largest.shape, 2.0 ** (-16), jnp.float32)
    inverse = jnp.full(largest.shape, 2.0**16, jnp.float32)
    for exponent in range(-16, -6):
        exceeds = largest > LIMIT * 2.0**exponent
        scale = jnp.where(exceeds, scale * 2.0, scale)
        inverse = jnp.where(exceeds, inverse * 0.5, inverse)
    scaled = values * inverse
    rest = jnp.abs(scaled) * 2.0**6
    step = jnp.full(scaled.shape, 2.0 ** (-9), jnp.float32)
    for bits in (8, 4, 2, 1):
        exceeds = rest >= 2.0**bits
        rest = jnp.where(exceeds, rest * 2.0**-bits, rest)
        step = jnp.where(exceeds, step * 2.0**bits, step)
    levels = jnp.minimum(jnp.floor(rest * 8.0 + 0.5) * step, LIMIT)
    cache = (jnp.where(scaled < 0.0, -levels, levels) * scale).astype(jnp.bfloat16)

    send_ref[...] = jnp.zeros(send_ref.shape, send_ref.dtype)

    def clear(o, carry):
        count_ref[o] = 0
        return carry

    lax.fori_loop(0, count_ref.shape[0], clear, 0)
    first = me_ref[0] * pages
    for page in range(pages):
        owner = owner_ref[first + page]
        rank = count_ref[owner]
        count_ref[owner] = rank + 1
        send_ref[pl.ds(owner * CAP + rank, 1)] = cache[page : page + 1]


def attention_kernel(
    pages, me_ref, owner_ref, slot_ref, fill_ref, q_ref, cache_ref, fresh_ref, out_ref
):
    owners = owner_ref.shape[0]
    slots, _, heads, page_len, width = cache_ref.shape
    requests, steps, q_heads, _ = q_ref.shape
    group = q_heads // heads
    rows = requests * steps * group
    mine = (owner_ref[...] == me_ref[0]).astype(jnp.float32)
    before = (
        lax.broadcasted_iota(jnp.int32, (pages, pages), 0)
        < lax.broadcasted_iota(jnp.int32, (pages, pages), 1)
    ).astype(jnp.float32)
    rank = jnp.dot(mine, before, preferred_element_type=jnp.float32)
    code = (slot_ref[...] * (page_len + 1) + fill_ref[...]).astype(jnp.float32)
    columns = slots * page_len
    place = lax.broadcasted_iota(jnp.int32, (owners, columns), 1)
    source = lax.broadcasted_iota(jnp.int32, (owners, columns), 0)
    spread = jnp.zeros((owners, columns), jnp.float32)
    for c in range(CAP):
        held = jnp.sum(
            jnp.where((mine > 0.0) & (rank == float(c)), code, 0.0), axis=1, keepdims=True
        )
        spread = jnp.where(place // page_len == source * CAP + c, held, spread)
    line = jnp.sum(spread, axis=0, keepdims=True).astype(jnp.int32)
    request_of = line // (page_len + 1)
    fill_of = line - request_of * (page_len + 1)
    position = lax.broadcasted_iota(jnp.int32, (1, columns), 1) % page_len
    request_of = jnp.where(position < fill_of, request_of, -1)
    row_request = lax.broadcasted_iota(jnp.int32, (rows, 1), 0) // (steps * group)
    visible = row_request == request_of
    token = lax.broadcasted_iota(jnp.int32, (rows, 1), 0) // group
    first = row_request * steps
    fresh_at = lax.broadcasted_iota(jnp.int32, (1, fresh_ref.shape[2]), 1)
    fresh_visible = (fresh_at >= first) & (fresh_at <= token)
    factor = 1.0 / math.sqrt(width)
    contract = (((1,), (1,)), ((), ()))
    for head in range(heads):
        q = q_ref[:, :, head * group : (head + 1) * group, :].reshape(rows, width)
        keys = cache_ref[:, 0, head].reshape(columns, width)
        values = cache_ref[:, 1, head].reshape(columns, width)
        scores = lax.dot_general(q, keys, contract, preferred_element_type=jnp.float32) * factor
        fresh = (
            lax.dot_general(q, fresh_ref[0, head], contract, preferred_element_type=jnp.float32)
            * factor
        )
        scores = jnp.where(visible, scores, -jnp.inf)
        fresh = jnp.where(fresh_visible, fresh, -jnp.inf)
        peak = jnp.maximum(
            jnp.max(scores, axis=1, keepdims=True), jnp.max(fresh, axis=1, keepdims=True)
        )
        weight = jnp.exp(scores - peak)
        fresh_weight = jnp.exp(fresh - peak)
        total = jnp.sum(weight, axis=1, keepdims=True) + jnp.sum(
            fresh_weight, axis=1, keepdims=True
        )
        mixed = jnp.dot(
            weight.astype(jnp.bfloat16), values, preferred_element_type=jnp.float32
        ) + jnp.dot(
            fresh_weight.astype(jnp.bfloat16), fresh_ref[1, head], preferred_element_type=jnp.float32
        )
        out_ref[:, :, head * group : (head + 1) * group, :] = (
            (mixed / total).astype(out_ref.dtype).reshape(requests, steps, group, width)
        )


def pack_kernel(experts, core_ref, x_ref, route_ref, prob_ref, out_ref):
    half = x_ref.shape[1] // 2
    begin = pl.multiple_of(core_ref[0] * half, 128)
    out_ref[:, :half] = x_ref[:, pl.ds(begin, half)]
    shape = (x_ref.shape[0], out_ref.shape[1] - half)
    lane = lax.broadcasted_iota(jnp.int32, shape, 1)
    expert = lane % experts
    part = lane // experts
    dense = jnp.zeros(shape, jnp.float32)
    for k in range(route_ref.shape[1]):
        dense += jnp.where(route_ref[:, k : k + 1] == expert, prob_ref[:, k : k + 1], 0.0)
    high = dense.astype(jnp.bfloat16).astype(jnp.float32)
    middle = (dense - high).astype(jnp.bfloat16).astype(jnp.float32)
    low = dense - high - middle
    chosen = jnp.where(part == 0, high, jnp.where(part == 1, middle, low))
    out_ref[:, half:] = jnp.where(part < 3, chosen, 0.0).astype(out_ref.dtype)


def room(*arrays):
    return sum(math.prod(a.shape) * a.dtype.itemsize for a in arrays) * 9 // 8 + 4 * MIB


def weight_copies(half, core, gate_ref, up_ref, held, sems):
    depth = half // sems.shape[1]
    pairs = []
    for c in range(sems.shape[1]):
        rows = pl.ds(pl.multiple_of(core * half + c * depth, 128), depth)
        pairs.append(
            [
                pltpu.make_async_copy(
                    ref.at[0, rows], held.at[i, pl.ds(c * depth, depth)], sems.at[i, c]
                )
                for i, ref in enumerate((gate_ref, up_ref))
            ]
        )
    for pair in pairs:
        for copy in pair:
            copy.start()
    return pairs, depth


def partial_kernel(core_ref, sr_ref, r2_ref, gate_ref, up_ref, gate_sum, up_sum, held, sems):
    half = held.shape[1]
    pairs, depth = weight_copies(half, core_ref[0], gate_ref, up_ref, held, sems)
    for c, pair in enumerate(pairs):
        at = slice(c * depth, (c + 1) * depth)
        x = jnp.concatenate([sr_ref[:, at], r2_ref[:, at]], axis=0)
        for i, total in enumerate((gate_sum, up_sum)):
            pair[i].wait()
            part = jnp.dot(x, held[i, at], preferred_element_type=jnp.float32)
            total[...] = part if c == 0 else total[...] + part


def hidden_kernel(
    core_ref, sr_ref, r2_ref, gate_ref, up_ref, gate_part, up_part, out_ref, held, sems, sums
):
    half = held.shape[1]
    group = sr_ref.shape[0] // 2
    pairs, depth = weight_copies(half, 1 - core_ref[0], gate_ref, up_ref, held, sems)
    last = len(pairs) - 1
    for c, pair in enumerate(pairs):
        at = slice(c * depth, (c + 1) * depth)
        x = jnp.concatenate(
            [sr_ref[:group, at], r2_ref[:group, at], sr_ref[group:, at], r2_ref[group:, at]],
            axis=0,
        )
        for i, start in enumerate((gate_part, up_part)):
            pair[i].wait()
            part = jnp.dot(x, held[i, at], preferred_element_type=jnp.float32)
            sums[i] = (start[...] if c == 0 else sums[i]) + part
    gate = sums[0]
    out_ref[...] = (gate / (1.0 + jnp.exp(-gate)) * sums[1]).astype(out_ref.dtype)


def expert_front(core, rows, w_gate, w_up, parts):
    tokens = 2 * rows[0].shape[0]
    d, f = w_gate.shape[1:]
    last = parts is not None
    total = jax.ShapeDtypeStruct((tokens, f), jnp.float32)
    scratch = [pltpu.VMEM((2, d // 2, f), jnp.bfloat16), pltpu.SemaphoreType.DMA((2, 4))]
    return pl.pallas_call(
        hidden_kernel if last else partial_kernel,
        in_specs=[smem(), vmem(), vmem(), hbm(), hbm()] + ([vmem(), vmem()] if last else []),
        out_specs=vmem() if last else [vmem(), vmem()],
        scratch_shapes=scratch + ([pltpu.VMEM((2, tokens, f), jnp.float32)] if last else []),
        out_shape=jax.ShapeDtypeStruct((tokens, f), jnp.bfloat16) if last else [total, total],
        compiler_params=pltpu.CompilerParams(vmem_limit_bytes=LARGE),
        cost_estimate=pl.CostEstimate(
            flops=2 * tokens * d * f,
            bytes_accessed=tokens * d + 2 * d * f + 8 * tokens * f,
            transcendentals=tokens * f if last else 0,
        ),
        name="expert_hidden" if last else "expert_partial",
    )(core, *rows, w_gate, w_up, *(parts or ()))


def back_kernel(
    send, experts, lanes, at_ref, own_ref, other_ref, sr_ref, r2_ref, down_ref, out_ref, held, sems
):
    chunks = sems.shape[0]
    block = held.shape[1] // chunks
    copies = [
        pltpu.make_async_copy(
            down_ref.at[0, :, pl.ds(c * block, block)],
            held.at[:, pl.ds(c * block, block)],
            sems.at[c],
        )
        for c in range(chunks)
    ]
    for copy in copies:
        copy.start()
    f = own_ref.shape[1]
    group = sr_ref.shape[0] // 2
    core = at_ref[1]
    first = int(send)

    def rows(ref, a, b):
        return jnp.concatenate(
            [ref[a * group : (a + 1) * group], ref[b * group : (b + 1) * group]], axis=0
        )

    own = rows(own_ref, 1, 3) if send else rows(own_ref, 0, 2)
    other = rows(other_ref, 2, 3) if send else rows(other_ref, 0, 1)
    begin = pl.multiple_of(core * f, 128)
    rest = pl.multiple_of((1 - core) * f, 128)
    tail = slice(sr_ref.shape[1] - lanes, sr_ref.shape[1])
    picked = slice(first * group, (first + 1) * group)
    probs = jnp.concatenate(
        [sr_ref[picked, tail].astype(jnp.float32), r2_ref[picked, tail].astype(jnp.float32)],
        axis=0,
    )
    lane = lax.broadcasted_iota(jnp.int32, probs.shape, 1)
    mine = lane % experts == at_ref[0]
    weight = jnp.sum(jnp.where(mine, probs, 0.0), axis=1, keepdims=True)
    for c, copy in enumerate(copies):
        at = slice(c * block, (c + 1) * block)
        copy.wait()
        total = jnp.dot(own, held[pl.ds(begin, f), at], preferred_element_type=jnp.float32)
        total += jnp.dot(other, held[pl.ds(rest, f), at], preferred_element_type=jnp.float32)
        out_ref[:, at] = (total * weight).astype(out_ref.dtype)


def expert_back(send, experts, at, own, other, w_down, sr, r2, lanes):
    tokens, f = own.shape
    group2 = sr.shape[0]
    width = w_down.shape[2]
    return pl.pallas_call(
        functools.partial(back_kernel, send, experts, lanes),
        out_shape=jax.ShapeDtypeStruct((group2, width), jnp.bfloat16 if send else jnp.float32),
        in_specs=[smem()] + [vmem()] * 4 + [hbm()],
        out_specs=vmem(),
        scratch_shapes=[
            pltpu.VMEM(w_down.shape[1:], jnp.bfloat16),
            pltpu.SemaphoreType.DMA((4,)),
        ],
        compiler_params=pltpu.CompilerParams(vmem_limit_bytes=LARGE),
        cost_estimate=pl.CostEstimate(
            flops=2 * tokens * f * width,
            bytes_accessed=2 * (2 * tokens * f + 2 * f * width + 2 * group2 * width),
            transcendentals=0,
        ),
        name="expert_back_send" if send else "expert_back_keep",
    )(at, own, other, sr, r2, w_down)


class Moves:
    def __init__(self, owners):
        self.owners = owners
        self.lines = owners // 4

    def go(self, x, where):
        perm = [
            (ep * 2 + core, where(ep, core)) for ep in range(self.owners) for core in range(2)
        ]
        return lax.ppermute(x, ("ep", "pd"), perm)

    def along_z(self, x, shift):
        return self.go(x, lambda ep, core: (ep + 4 * shift) % self.owners * 2 + core)

    def flip(self, x, turn):
        return self.go(x, lambda ep, core: (ep ^ (1 << ((core + turn) % 2))) * 2 + core)

    def cores(self, x):
        return self.go(x, lambda ep, core: ep * 2 + 1 - core)


def body(
    prompt_kv,
    page_owner,
    page_slot,
    page_fill,
    queries,
    new_kv,
    moe_input,
    expert_routes,
    route_probs,
    w_gate,
    w_up,
    w_down,
):
    owners = lax.axis_size("ep")
    me = lax.axis_index("ep").astype(jnp.int32)
    me_ref = me.reshape(1)
    core = lax.axis_index("pd").astype(jnp.int32)
    pages, _, page_len, heads, width = prompt_kv.shape
    requests, steps, q_heads, _ = queries.shape
    d = moe_input.shape[2]
    tokens = requests * steps
    slots = owners * CAP

    moves = Moves(owners)
    top = expert_routes.shape[2]
    lanes = -(-3 * owners // 128) * 128
    at = jnp.stack([me, core])
    own_core = core.reshape(1)
    mine = pl.pallas_call(
        functools.partial(pack_kernel, owners),
        out_shape=jax.ShapeDtypeStruct((tokens, d // 2 + lanes), jnp.bfloat16),
        in_specs=[smem()] + [vmem()] * 3,
        out_specs=vmem(),
        name="pack_tokens",
    )(
        own_core,
        moe_input.transpose(1, 0, 2).reshape(tokens, d),
        expert_routes.reshape(tokens, top),
        route_probs.transpose(1, 0, 2).reshape(tokens, top),
    )
    line = [mine] + [moves.along_z(mine, -shift) for shift in range(1, moves.lines)]
    line = jnp.concatenate(line, axis=0)
    fresh = new_kv.transpose(2, 3, 0, 1, 4).reshape(2, heads, tokens, width)
    fresh = jnp.pad(fresh, ((0, 0), (0, 0), (0, 128 - tokens), (0, 0)))
    tables = [t.reshape(owners, pages) for t in (page_owner, page_slot, page_fill)]
    sr = jnp.concatenate([line, moves.flip(line, 0)], axis=0)
    sr, fresh, tables, prompt_kv = lax.optimization_barrier((sr, fresh, tables, prompt_kv))
    r2 = moves.flip(sr, 1)
    send = pl.pallas_call(
        functools.partial(page_kernel, pages),
        out_shape=jax.ShapeDtypeStruct((slots, 2, heads, page_len, width), jnp.bfloat16),
        in_specs=[smem(), smem(), vmem()],
        out_specs=vmem(),
        scratch_shapes=[pltpu.SMEM((owners,), jnp.int32)],
        compiler_params=pltpu.CompilerParams(vmem_limit_bytes=room(prompt_kv) * 4),
        name="quantize_pages",
    )(me_ref, page_owner.reshape(-1), prompt_kv.transpose(0, 1, 3, 2, 4))
    r2, send = lax.optimization_barrier((r2, send))
    cache = lax.all_to_all(send, "ep", split_axis=0, concat_axis=0, tiled=True)
    other_sr, other_r2 = moves.cores(sr), moves.cores(r2)

    parts = expert_front(own_core, (sr, r2), w_gate, w_up, None)
    hidden = expert_front(own_core, (other_sr, other_r2), w_gate, w_up, parts)
    other_hidden = moves.cores(hidden)
    at, cache = lax.optimization_barrier((at, cache))
    sent = expert_back(True, owners, at, hidden, other_hidden, w_down, sr, r2, lanes)
    kept = expert_back(False, owners, at, hidden, other_hidden, w_down, sr, r2, lanes)
    attn_out = pl.pallas_call(
        functools.partial(attention_kernel, pages),
        out_shape=jax.ShapeDtypeStruct(queries.shape, jnp.bfloat16),
        in_specs=[smem()] + [vmem()] * 6,
        out_specs=vmem(),
        compiler_params=pltpu.CompilerParams(
            vmem_limit_bytes=8 * MIB + 16 * slots * page_len * tokens * q_heads
        ),
        name="attention",
    )(
        me_ref,
        *tables,
        queries,
        cache,
        fresh,
    )
    group = moves.lines * tokens
    kept = kept + moves.flip(sent, 0).astype(jnp.float32)
    kept, attn_out = lax.optimization_barrier((kept, attn_out))
    kept = kept[:group] + moves.flip(kept[group:].astype(jnp.bfloat16), 1).astype(jnp.float32)
    moe = kept[:tokens]
    for shift in range(1, moves.lines):
        block = kept[shift * tokens : (shift + 1) * tokens].astype(jnp.bfloat16)
        moe = moe + moves.along_z(block, shift).astype(jnp.float32)
    moe = moe.astype(jnp.bfloat16)
    moe_out = moe.reshape(steps, requests, d // 2).transpose(1, 0, 2)

    return (attn_out, moe_out)


def solution(mesh):
    return jax.shard_map(
        body,
        mesh=mesh,
        in_specs=(
            P(("grp", "ep"), None, None, "pd", None),
            P("grp", None),
            P("grp"),
            P("grp"),
            P(("grp", "ep"), None, "pd", None),
            P(("grp", "ep"), None, None, "pd", None),
            P(("grp", "ep"), None, None),
            P(None, ("grp", "ep"), None),
            P(("grp", "ep"), None, None),
            P("ep", None, "pd"),
            P("ep", None, "pd"),
            P("ep", None, "pd"),
        ),
        out_specs=(P(("grp", "ep"), None, "pd", None), P(("grp", "ep"), None, "pd")),
        check_vma=False,
    )
```

```python
import functools
import math

import jax
import jax.numpy as jnp
from jax import lax
from jax.experimental import pallas as pl
from jax.experimental.pallas import tpu as pltpu
from jax.sharding import PartitionSpec as P

CAP = 2
LIMIT = 448.0
MIB = 1024 * 1024


def vmem():
    return pl.BlockSpec(memory_space=pltpu.VMEM)


def smem():
    return pl.BlockSpec(memory_space=pltpu.SMEM)


def page_kernel(pages, me_ref, owner_ref, kv_ref, send_ref, count_ref):
    values = kv_ref[...].astype(jnp.float32)
    largest = jnp.max(jnp.abs(values), axis=(3, 4), keepdims=True)
    scale = jnp.full(largest.shape, 2.0 ** (-16), jnp.float32)
    inverse = jnp.full(largest.shape, 2.0**16, jnp.float32)
    for exponent in range(-16, -6):
        exceeds = largest > LIMIT * 2.0**exponent
        scale = jnp.where(exceeds, scale * 2.0, scale)
        inverse = jnp.where(exceeds, inverse * 0.5, inverse)
    scaled = values * inverse
    rest = jnp.abs(scaled) * 2.0**6
    step = jnp.full(scaled.shape, 2.0 ** (-9), jnp.float32)
    for bits in (8, 4, 2, 1):
        exceeds = rest >= 2.0**bits
        rest = jnp.where(exceeds, rest * 2.0**-bits, rest)
        step = jnp.where(exceeds, step * 2.0**bits, step)
    levels = jnp.minimum(jnp.floor(rest * 8.0 + 0.5) * step, LIMIT)
    cache = (jnp.where(scaled < 0.0, -levels, levels) * scale).astype(jnp.bfloat16)

    send_ref[...] = jnp.zeros(send_ref.shape, send_ref.dtype)

    def clear(o, carry):
        count_ref[o] = 0
        return carry

    lax.fori_loop(0, count_ref.shape[0], clear, 0)
    first = me_ref[0] * pages
    for page in range(pages):
        owner = owner_ref[first + page]
        rank = count_ref[owner]
        count_ref[owner] = rank + 1
        send_ref[pl.ds(owner * CAP + rank, 1)] = cache[page : page + 1]


def attention_kernel(
    pages, me_ref, owner_ref, slot_ref, fill_ref, q_ref, cache_ref, fresh_ref, out_ref
):
    owners = owner_ref.shape[0]
    slots, _, heads, page_len, width = cache_ref.shape
    requests, steps, q_heads, _ = q_ref.shape
    group = q_heads // heads
    rows = requests * steps * group
    mine = (owner_ref[...] == me_ref[0]).astype(jnp.float32)
    before = (
        lax.broadcasted_iota(jnp.int32, (pages, pages), 0)
        < lax.broadcasted_iota(jnp.int32, (pages, pages), 1)
    ).astype(jnp.float32)
    rank = jnp.dot(mine, before, preferred_element_type=jnp.float32)
    code = (slot_ref[...] * (page_len + 1) + fill_ref[...]).astype(jnp.float32)
    columns = slots * page_len
    place = lax.broadcasted_iota(jnp.int32, (owners, columns), 1)
    source = lax.broadcasted_iota(jnp.int32, (owners, columns), 0)
    spread = jnp.zeros((owners, columns), jnp.float32)
    for c in range(CAP):
        held = jnp.sum(
            jnp.where((mine > 0.0) & (rank == float(c)), code, 0.0), axis=1, keepdims=True
        )
        spread = jnp.where(place // page_len == source * CAP + c, held, spread)
    line = jnp.sum(spread, axis=0, keepdims=True).astype(jnp.int32)
    request_of = line // (page_len + 1)
    fill_of = line - request_of * (page_len + 1)
    position = lax.broadcasted_iota(jnp.int32, (1, columns), 1) % page_len
    request_of = jnp.where(position < fill_of, request_of, -1)
    row_request = lax.broadcasted_iota(jnp.int32, (rows, 1), 0) // (steps * group)
    visible = row_request == request_of
    token = lax.broadcasted_iota(jnp.int32, (rows, 1), 0) // group
    first = row_request * steps
    fresh_at = lax.broadcasted_iota(jnp.int32, (1, fresh_ref.shape[2]), 1)
    fresh_visible = (fresh_at >= first) & (fresh_at <= token)
    factor = 1.0 / math.sqrt(width)
    contract = (((1,), (1,)), ((), ()))
    for head in range(heads):
        q = q_ref[:, :, head * group : (head + 1) * group, :].reshape(rows, width)
        keys = cache_ref[:, 0, head].reshape(columns, width)
        values = cache_ref[:, 1, head].reshape(columns, width)
        scores = lax.dot_general(q, keys, contract, preferred_element_type=jnp.float32) * factor
        fresh = (
            lax.dot_general(q, fresh_ref[0, head], contract, preferred_element_type=jnp.float32)
            * factor
        )
        scores = jnp.where(visible, scores, -jnp.inf)
        fresh = jnp.where(fresh_visible, fresh, -jnp.inf)
        peak = jnp.maximum(
            jnp.max(scores, axis=1, keepdims=True), jnp.max(fresh, axis=1, keepdims=True)
        )
        weight = jnp.exp(scores - peak)
        fresh_weight = jnp.exp(fresh - peak)
        total = jnp.sum(weight, axis=1, keepdims=True) + jnp.sum(
            fresh_weight, axis=1, keepdims=True
        )
        mixed = jnp.dot(
            weight.astype(jnp.bfloat16), values, preferred_element_type=jnp.float32
        ) + jnp.dot(
            fresh_weight.astype(jnp.bfloat16), fresh_ref[1, head], preferred_element_type=jnp.float32
        )
        out_ref[:, :, head * group : (head + 1) * group, :] = (
            (mixed / total).astype(out_ref.dtype).reshape(requests, steps, group, width)
        )


def pack_kernel(experts, core_ref, x_ref, route_ref, prob_ref, out_ref):
    half = x_ref.shape[1] // 2
    begin = pl.multiple_of(core_ref[0] * half, 128)
    out_ref[:, :half] = x_ref[:, pl.ds(begin, half)]
    shape = (x_ref.shape[0], out_ref.shape[1] - half)
    lane = lax.broadcasted_iota(jnp.int32, shape, 1)
    expert = lane % experts
    part = lane // experts
    dense = jnp.zeros(shape, jnp.float32)
    for k in range(route_ref.shape[1]):
        dense += jnp.where(route_ref[:, k : k + 1] == expert, prob_ref[:, k : k + 1], 0.0)
    high = dense.astype(jnp.bfloat16).astype(jnp.float32)
    middle = (dense - high).astype(jnp.bfloat16).astype(jnp.float32)
    low = dense - high - middle
    chosen = jnp.where(part == 0, high, jnp.where(part == 1, middle, low))
    out_ref[:, half:] = jnp.where(part < 3, chosen, 0.0).astype(out_ref.dtype)


def partial_kernel(chunks, core_ref, x_ref, gate_ref, up_ref, gate_sum, up_sum):
    half = gate_ref.shape[1] // 2
    depth = half // chunks
    for c in range(chunks):
        at = slice(c * depth, (c + 1) * depth)
        rows = pl.ds(pl.multiple_of(core_ref[0] * half + c * depth, 128), depth)
        for weight, total in ((gate_ref, gate_sum), (up_ref, up_sum)):
            part = jnp.dot(x_ref[:, at], weight[0, rows], preferred_element_type=jnp.float32)
            total[...] = part if c == 0 else total[...] + part


def hidden_kernel(
    chunks, core_ref, sr_ref, r2_ref, gate_ref, up_ref, g0_ref, u0_ref, g1_ref, u1_ref, out_ref, sums
):
    half = gate_ref.shape[1] // 2
    depth = half // chunks
    group = sr_ref.shape[0] // 2
    for c in range(chunks):
        at = slice(c * depth, (c + 1) * depth)
        rows = pl.ds(pl.multiple_of((1 - core_ref[0]) * half + c * depth, 128), depth)
        x = jnp.concatenate(
            [sr_ref[:group, at], r2_ref[:group, at], sr_ref[group:, at], r2_ref[group:, at]],
            axis=0,
        )
        for i, (weight, early, late) in enumerate(
            ((gate_ref, g0_ref, g1_ref), (up_ref, u0_ref, u1_ref))
        ):
            part = jnp.dot(x, weight[0, rows], preferred_element_type=jnp.float32)
            if c == 0:
                sums[i, : 2 * group] = early[...] + part[: 2 * group]
                sums[i, 2 * group :] = late[...] + part[2 * group :]
            else:
                sums[i] += part
    gate = sums[0]
    out_ref[...] = (gate / (1.0 + jnp.exp(-gate)) * sums[1]).astype(out_ref.dtype)


def room(*arrays):
    return sum(math.prod(a.shape) * a.dtype.itemsize for a in arrays) * 9 // 8 + 4 * MIB


def expert_partial(core, x, w_gate, w_up):
    tokens = x.shape[0]
    d, f = w_gate.shape[1:]
    total = jax.ShapeDtypeStruct((tokens, f), jnp.float32)
    return pl.pallas_call(
        functools.partial(partial_kernel, 4),
        in_specs=[smem()] + [vmem()] * 3,
        out_specs=[vmem(), vmem()],
        out_shape=[total, total],
        compiler_params=pltpu.CompilerParams(vmem_limit_bytes=room(x, w_gate, w_up, total, total)),
        cost_estimate=pl.CostEstimate(
            flops=2 * tokens * d * f,
            bytes_accessed=tokens * d + 2 * d * f + 8 * tokens * f,
            transcendentals=0,
        ),
        name="expert_partial",
    )(core, x, w_gate, w_up)


def expert_hidden(core, sr, r2, w_gate, w_up, parts):
    tokens = 2 * sr.shape[0]
    d, f = w_gate.shape[1:]
    total = jax.ShapeDtypeStruct((tokens, f), jnp.float32)
    return pl.pallas_call(
        functools.partial(hidden_kernel, 4),
        in_specs=[smem()] + [vmem()] * 8,
        out_specs=vmem(),
        out_shape=jax.ShapeDtypeStruct((tokens, f), jnp.bfloat16),
        scratch_shapes=[pltpu.VMEM((2, tokens, f), jnp.float32)],
        compiler_params=pltpu.CompilerParams(
            vmem_limit_bytes=room(sr, r2, w_gate, w_up, *[total] * 5)
        ),
        cost_estimate=pl.CostEstimate(
            flops=2 * tokens * d * f,
            bytes_accessed=tokens * d + 2 * d * f + 10 * tokens * f,
            transcendentals=tokens * f,
        ),
        name="expert_hidden",
    )(core, sr, r2, w_gate, w_up, *parts)


def back_kernel(
    send, experts, lanes, chunks, at_ref, own_ref, other_ref, sr_ref, r2_ref, down_ref, out_ref
):
    block = down_ref.shape[2] // chunks
    f = own_ref.shape[1]
    group = sr_ref.shape[0] // 2
    core = at_ref[1]
    first = int(send)

    def rows(ref, a, b):
        return jnp.concatenate(
            [ref[a * group : (a + 1) * group], ref[b * group : (b + 1) * group]], axis=0
        )

    own = rows(own_ref, 1, 3) if send else rows(own_ref, 0, 2)
    other = rows(other_ref, 2, 3) if send else rows(other_ref, 0, 1)
    begin = pl.multiple_of(core * f, 128)
    rest = pl.multiple_of((1 - core) * f, 128)
    tail = slice(sr_ref.shape[1] - lanes, sr_ref.shape[1])
    picked = slice(first * group, (first + 1) * group)
    probs = jnp.concatenate(
        [sr_ref[picked, tail].astype(jnp.float32), r2_ref[picked, tail].astype(jnp.float32)],
        axis=0,
    )
    lane = lax.broadcasted_iota(jnp.int32, probs.shape, 1)
    mine = lane % experts == at_ref[0]
    weight = jnp.sum(jnp.where(mine, probs, 0.0), axis=1, keepdims=True)
    for c in range(chunks):
        at = slice(c * block, (c + 1) * block)
        total = jnp.dot(own, down_ref[0, pl.ds(begin, f), at], preferred_element_type=jnp.float32)
        total += jnp.dot(
            other, down_ref[0, pl.ds(rest, f), at], preferred_element_type=jnp.float32
        )
        out_ref[:, at] = (total * weight).astype(out_ref.dtype)


def expert_back(send, experts, at, own, other, w_down, sr, r2, lanes):
    tokens, f = own.shape
    group2 = sr.shape[0]
    width = w_down.shape[2]
    out = jax.ShapeDtypeStruct((group2, width), jnp.bfloat16 if send else jnp.float32)
    return pl.pallas_call(
        functools.partial(back_kernel, send, experts, lanes, 4),
        out_shape=out,
        in_specs=[smem()] + [vmem()] * 5,
        out_specs=vmem(),
        compiler_params=pltpu.CompilerParams(
            vmem_limit_bytes=room(own, other, w_down, sr, r2, out, out)
        ),
        cost_estimate=pl.CostEstimate(
            flops=2 * tokens * f * width,
            bytes_accessed=2 * (2 * tokens * f + 2 * f * width + 2 * group2 * width),
            transcendentals=0,
        ),
        name="expert_back_send" if send else "expert_back_keep",
    )(at, own, other, sr, r2, w_down)


class Moves:
    def __init__(self, owners):
        self.owners = owners
        self.lines = owners // 4

    def go(self, x, where):
        perm = [
            (ep * 2 + core, where(ep, core)) for ep in range(self.owners) for core in range(2)
        ]
        return lax.ppermute(x, ("ep", "pd"), perm)

    def along_z(self, x, shift):
        return self.go(x, lambda ep, core: (ep + 4 * shift) % self.owners * 2 + core)

    def flip(self, x, turn):
        return self.go(x, lambda ep, core: (ep ^ (1 << ((core + turn) % 2))) * 2 + core)

    def cores(self, x):
        return self.go(x, lambda ep, core: ep * 2 + 1 - core)


def body(
    prompt_kv,
    page_owner,
    page_slot,
    page_fill,
    queries,
    new_kv,
    moe_input,
    expert_routes,
    route_probs,
    w_gate,
    w_up,
    w_down,
):
    owners = lax.axis_size("ep")
    me = lax.axis_index("ep").astype(jnp.int32)
    me_ref = me.reshape(1)
    core = lax.axis_index("pd").astype(jnp.int32)
    pages, _, page_len, heads, width = prompt_kv.shape
    requests, steps, q_heads, _ = queries.shape
    d = moe_input.shape[2]
    tokens = requests * steps
    slots = owners * CAP

    moves = Moves(owners)
    top = expert_routes.shape[2]
    lanes = -(-3 * owners // 128) * 128
    at = jnp.stack([me, core])
    own_core = core.reshape(1)
    mine = pl.pallas_call(
        functools.partial(pack_kernel, owners),
        out_shape=jax.ShapeDtypeStruct((tokens, d // 2 + lanes), jnp.bfloat16),
        in_specs=[smem()] + [vmem()] * 3,
        out_specs=vmem(),
        name="pack_tokens",
    )(
        own_core,
        moe_input.transpose(1, 0, 2).reshape(tokens, d),
        expert_routes.reshape(tokens, top),
        route_probs.transpose(1, 0, 2).reshape(tokens, top),
    )
    send = pl.pallas_call(
        functools.partial(page_kernel, pages),
        out_shape=jax.ShapeDtypeStruct((slots, 2, heads, page_len, width), jnp.bfloat16),
        in_specs=[smem(), smem(), vmem()],
        out_specs=vmem(),
        scratch_shapes=[pltpu.SMEM((owners,), jnp.int32)],
        compiler_params=pltpu.CompilerParams(vmem_limit_bytes=room(prompt_kv) * 4),
        name="quantize_pages",
    )(me_ref, page_owner.reshape(-1), prompt_kv.transpose(0, 1, 3, 2, 4))
    line = [mine] + [moves.along_z(mine, -shift) for shift in range(1, moves.lines)]
    line = jnp.concatenate(line, axis=0)
    fresh = new_kv.transpose(2, 3, 0, 1, 4).reshape(2, heads, tokens, width)
    fresh = jnp.pad(fresh, ((0, 0), (0, 0), (0, 128 - tokens), (0, 0)))
    tables = [t.reshape(owners, pages) for t in (page_owner, page_slot, page_fill)]
    line, send = lax.optimization_barrier((line, send))
    sr = jnp.concatenate([line, moves.flip(line, 0)], axis=0)
    sr, fresh, tables = lax.optimization_barrier((sr, fresh, tables))
    r2 = moves.flip(sr, 1)
    cache = lax.all_to_all(send, "ep", split_axis=0, concat_axis=0, tiled=True)
    core_then, cache = lax.optimization_barrier((own_core, cache))
    early = expert_partial(core_then, sr, w_gate, w_up)
    r2, early = lax.optimization_barrier((r2, early))
    other_sr, other_r2 = moves.cores(sr), moves.cores(r2)
    parts = early + expert_partial(own_core, r2, w_gate, w_up)
    hidden = expert_hidden(own_core, other_sr, other_r2, w_gate, w_up, parts)
    other_hidden = moves.cores(hidden)
    sent = expert_back(True, owners, at, hidden, other_hidden, w_down, sr, r2, lanes)
    kept = expert_back(False, owners, at, hidden, other_hidden, w_down, sr, r2, lanes)
    attn_out = pl.pallas_call(
        functools.partial(attention_kernel, pages),
        out_shape=jax.ShapeDtypeStruct(queries.shape, jnp.bfloat16),
        in_specs=[smem()] + [vmem()] * 6,
        out_specs=vmem(),
        compiler_params=pltpu.CompilerParams(
            vmem_limit_bytes=8 * MIB + 16 * slots * page_len * tokens * q_heads
        ),
        name="attention",
    )(
        me_ref,
        *tables,
        queries,
        cache,
        fresh,
    )
    group = moves.lines * tokens
    kept = kept + moves.flip(sent, 0).astype(jnp.float32)
    kept, attn_out = lax.optimization_barrier((kept, attn_out))
    kept = kept[:group] + moves.flip(kept[group:].astype(jnp.bfloat16), 1).astype(jnp.float32)
    moe = kept[:tokens]
    for shift in range(1, moves.lines):
        block = kept[shift * tokens : (shift + 1) * tokens].astype(jnp.bfloat16)
        moe = moe + moves.along_z(block, shift).astype(jnp.float32)
    moe = moe.astype(jnp.bfloat16)
    moe_out = moe.reshape(steps, requests, d // 2).transpose(1, 0, 2)

    return (attn_out, moe_out)


def solution(mesh):
    return jax.shard_map(
        body,
        mesh=mesh,
        in_specs=(
            P(("grp", "ep"), None, None, "pd", None),
            P("grp", None),
            P("grp"),
            P("grp"),
            P(("grp", "ep"), None, "pd", None),
            P(("grp", "ep"), None, None, "pd", None),
            P(("grp", "ep"), None, None),
            P(None, ("grp", "ep"), None),
            P(("grp", "ep"), None, None),
            P("ep", None, "pd"),
            P("ep", None, "pd"),
            P("ep", None, "pd"),
        ),
        out_specs=(P(("grp", "ep"), None, "pd", None), P(("grp", "ep"), None, "pd")),
        check_vma=False,
    )
```

```python
import functools
import math

import jax
import jax.numpy as jnp
from jax import lax
from jax.experimental import pallas as pl
from jax.experimental.pallas import tpu as pltpu
from jax.sharding import PartitionSpec as P

CAP = 2
LIMIT = 448.0
MIB = 1024 * 1024


def vmem():
    return pl.BlockSpec(memory_space=pltpu.VMEM)


def smem():
    return pl.BlockSpec(memory_space=pltpu.SMEM)


def page_kernel(pages, me_ref, owner_ref, kv_ref, send_ref, count_ref):
    values = kv_ref[...].astype(jnp.float32)
    largest = jnp.max(jnp.abs(values), axis=(3, 4), keepdims=True)
    scale = jnp.full(largest.shape, 2.0 ** (-16), jnp.float32)
    inverse = jnp.full(largest.shape, 2.0**16, jnp.float32)
    for exponent in range(-16, -6):
        exceeds = largest > LIMIT * 2.0**exponent
        scale = jnp.where(exceeds, scale * 2.0, scale)
        inverse = jnp.where(exceeds, inverse * 0.5, inverse)
    scaled = values * inverse
    rest = jnp.abs(scaled) * 2.0**6
    step = jnp.full(scaled.shape, 2.0 ** (-9), jnp.float32)
    for bits in (8, 4, 2, 1):
        exceeds = rest >= 2.0**bits
        rest = jnp.where(exceeds, rest * 2.0**-bits, rest)
        step = jnp.where(exceeds, step * 2.0**bits, step)
    levels = jnp.minimum(jnp.floor(rest * 8.0 + 0.5) * step, LIMIT)
    cache = (jnp.where(scaled < 0.0, -levels, levels) * scale).astype(jnp.bfloat16)

    send_ref[...] = jnp.zeros(send_ref.shape, send_ref.dtype)

    def clear(o, carry):
        count_ref[o] = 0
        return carry

    lax.fori_loop(0, count_ref.shape[0], clear, 0)
    first = me_ref[0] * pages
    for page in range(pages):
        owner = owner_ref[first + page]
        rank = count_ref[owner]
        count_ref[owner] = rank + 1
        send_ref[pl.ds(owner * CAP + rank, 1)] = cache[page : page + 1]


def attention_kernel(
    pages, me_ref, owner_ref, slot_ref, fill_ref, q_ref, cache_ref, fresh_ref, out_ref
):
    owners = owner_ref.shape[0]
    slots, _, heads, page_len, width = cache_ref.shape
    requests, steps, q_heads, _ = q_ref.shape
    group = q_heads // heads
    rows = requests * steps * group
    mine = (owner_ref[...] == me_ref[0]).astype(jnp.float32)
    before = (
        lax.broadcasted_iota(jnp.int32, (pages, pages), 0)
        < lax.broadcasted_iota(jnp.int32, (pages, pages), 1)
    ).astype(jnp.float32)
    rank = jnp.dot(mine, before, preferred_element_type=jnp.float32)
    code = (slot_ref[...] * (page_len + 1) + fill_ref[...]).astype(jnp.float32)
    columns = slots * page_len
    place = lax.broadcasted_iota(jnp.int32, (owners, columns), 1)
    source = lax.broadcasted_iota(jnp.int32, (owners, columns), 0)
    spread = jnp.zeros((owners, columns), jnp.float32)
    for c in range(CAP):
        held = jnp.sum(
            jnp.where((mine > 0.0) & (rank == float(c)), code, 0.0), axis=1, keepdims=True
        )
        spread = jnp.where(place // page_len == source * CAP + c, held, spread)
    line = jnp.sum(spread, axis=0, keepdims=True).astype(jnp.int32)
    request_of = line // (page_len + 1)
    fill_of = line - request_of * (page_len + 1)
    position = lax.broadcasted_iota(jnp.int32, (1, columns), 1) % page_len
    request_of = jnp.where(position < fill_of, request_of, -1)
    row_request = lax.broadcasted_iota(jnp.int32, (rows, 1), 0) // (steps * group)
    visible = row_request == request_of
    token = lax.broadcasted_iota(jnp.int32, (rows, 1), 0) // group
    first = row_request * steps
    fresh_at = lax.broadcasted_iota(jnp.int32, (1, fresh_ref.shape[2]), 1)
    fresh_visible = (fresh_at >= first) & (fresh_at <= token)
    factor = 1.0 / math.sqrt(width)
    contract = (((1,), (1,)), ((), ()))
    for head in range(heads):
        q = q_ref[:, :, head * group : (head + 1) * group, :].reshape(rows, width)
        keys = cache_ref[:, 0, head].reshape(columns, width)
        values = cache_ref[:, 1, head].reshape(columns, width)
        scores = lax.dot_general(q, keys, contract, preferred_element_type=jnp.float32) * factor
        fresh = (
            lax.dot_general(q, fresh_ref[0, head], contract, preferred_element_type=jnp.float32)
            * factor
        )
        scores = jnp.where(visible, scores, -jnp.inf)
        fresh = jnp.where(fresh_visible, fresh, -jnp.inf)
        peak = jnp.maximum(
            jnp.max(scores, axis=1, keepdims=True), jnp.max(fresh, axis=1, keepdims=True)
        )
        weight = jnp.exp(scores - peak)
        fresh_weight = jnp.exp(fresh - peak)
        total = jnp.sum(weight, axis=1, keepdims=True) + jnp.sum(
            fresh_weight, axis=1, keepdims=True
        )
        mixed = jnp.dot(
            weight.astype(jnp.bfloat16), values, preferred_element_type=jnp.float32
        ) + jnp.dot(
            fresh_weight.astype(jnp.bfloat16), fresh_ref[1, head], preferred_element_type=jnp.float32
        )
        out_ref[:, :, head * group : (head + 1) * group, :] = (
            (mixed / total).astype(out_ref.dtype).reshape(requests, steps, group, width)
        )


def pack_kernel(experts, core_ref, x_ref, route_ref, prob_ref, out_ref):
    half = x_ref.shape[1] // 2
    begin = pl.multiple_of(core_ref[0] * half, 128)
    out_ref[:, :half] = x_ref[:, pl.ds(begin, half)]
    shape = (x_ref.shape[0], out_ref.shape[1] - half)
    lane = lax.broadcasted_iota(jnp.int32, shape, 1)
    expert = lane % experts
    part = lane // experts
    dense = jnp.zeros(shape, jnp.float32)
    for k in range(route_ref.shape[1]):
        dense += jnp.where(route_ref[:, k : k + 1] == expert, prob_ref[:, k : k + 1], 0.0)
    high = dense.astype(jnp.bfloat16).astype(jnp.float32)
    middle = (dense - high).astype(jnp.bfloat16).astype(jnp.float32)
    low = dense - high - middle
    chosen = jnp.where(part == 0, high, jnp.where(part == 1, middle, low))
    out_ref[:, half:] = jnp.where(part < 3, chosen, 0.0).astype(out_ref.dtype)


def partial_kernel(chunks, core_ref, sr_ref, r2_ref, gate_ref, up_ref, gate_sum, up_sum):
    half = gate_ref.shape[1] // 2
    depth = half // chunks
    for c in range(chunks):
        at = slice(c * depth, (c + 1) * depth)
        rows = pl.ds(pl.multiple_of(core_ref[0] * half + c * depth, 128), depth)
        x = jnp.concatenate([sr_ref[:, at], r2_ref[:, at]], axis=0)
        for weight, total in ((gate_ref, gate_sum), (up_ref, up_sum)):
            part = jnp.dot(x, weight[0, rows], preferred_element_type=jnp.float32)
            total[...] = part if c == 0 else total[...] + part


def hidden_kernel(
    chunks, core_ref, sr_ref, r2_ref, gate_ref, up_ref, gate_part, up_part, out_ref, sums
):
    half = gate_ref.shape[1] // 2
    depth = half // chunks
    group = sr_ref.shape[0] // 2
    for c in range(chunks):
        at = slice(c * depth, (c + 1) * depth)
        rows = pl.ds(pl.multiple_of((1 - core_ref[0]) * half + c * depth, 128), depth)
        x = jnp.concatenate(
            [sr_ref[:group, at], r2_ref[:group, at], sr_ref[group:, at], r2_ref[group:, at]],
            axis=0,
        )
        for i, (weight, start) in enumerate(((gate_ref, gate_part), (up_ref, up_part))):
            part = jnp.dot(x, weight[0, rows], preferred_element_type=jnp.float32)
            sums[i] = (start[...] if c == 0 else sums[i]) + part
    gate = sums[0]
    out_ref[...] = (gate / (1.0 + jnp.exp(-gate)) * sums[1]).astype(out_ref.dtype)


def room(*arrays):
    return sum(math.prod(a.shape) * a.dtype.itemsize for a in arrays) * 9 // 8 + 4 * MIB


def expert_front(core, rows, w_gate, w_up, parts):
    tokens = 2 * rows[0].shape[0]
    d, f = w_gate.shape[1:]
    last = parts is not None
    total = jax.ShapeDtypeStruct((tokens, f), jnp.float32)
    scratch = [pltpu.VMEM((2, tokens, f), jnp.float32)] if last else []
    return pl.pallas_call(
        functools.partial(hidden_kernel if last else partial_kernel, 4),
        in_specs=[smem()] + [vmem()] * (6 if last else 4),
        out_specs=vmem() if last else [vmem(), vmem()],
        scratch_shapes=scratch,
        out_shape=jax.ShapeDtypeStruct((tokens, f), jnp.bfloat16) if last else [total, total],
        compiler_params=pltpu.CompilerParams(
            vmem_limit_bytes=room(*rows, w_gate, w_up, *[total] * (5 if last else 2))
        ),
        cost_estimate=pl.CostEstimate(
            flops=2 * tokens * d * f,
            bytes_accessed=tokens * d + 2 * d * f + 8 * tokens * f,
            transcendentals=tokens * f if last else 0,
        ),
        name="expert_hidden" if last else "expert_partial",
    )(core, *rows, w_gate, w_up, *(parts or ()))


def back_kernel(
    send, experts, lanes, chunks, at_ref, own_ref, other_ref, sr_ref, r2_ref, down_ref, out_ref
):
    block = down_ref.shape[2] // chunks
    f = own_ref.shape[1]
    group = sr_ref.shape[0] // 2
    core = at_ref[1]
    first = int(send)

    def rows(ref, a, b):
        return jnp.concatenate(
            [ref[a * group : (a + 1) * group], ref[b * group : (b + 1) * group]], axis=0
        )

    own = rows(own_ref, 1, 3) if send else rows(own_ref, 0, 2)
    other = rows(other_ref, 2, 3) if send else rows(other_ref, 0, 1)
    begin = pl.multiple_of(core * f, 128)
    rest = pl.multiple_of((1 - core) * f, 128)
    tail = slice(sr_ref.shape[1] - lanes, sr_ref.shape[1])
    picked = slice(first * group, (first + 1) * group)
    probs = jnp.concatenate(
        [sr_ref[picked, tail].astype(jnp.float32), r2_ref[picked, tail].astype(jnp.float32)],
        axis=0,
    )
    lane = lax.broadcasted_iota(jnp.int32, probs.shape, 1)
    mine = lane % experts == at_ref[0]
    weight = jnp.sum(jnp.where(mine, probs, 0.0), axis=1, keepdims=True)
    for c in range(chunks):
        at = slice(c * block, (c + 1) * block)
        total = jnp.dot(own, down_ref[0, pl.ds(begin, f), at], preferred_element_type=jnp.float32)
        total += jnp.dot(
            other, down_ref[0, pl.ds(rest, f), at], preferred_element_type=jnp.float32
        )
        out_ref[:, at] = (total * weight).astype(out_ref.dtype)


def expert_back(send, experts, at, own, other, w_down, sr, r2, lanes):
    tokens, f = own.shape
    group2 = sr.shape[0]
    width = w_down.shape[2]
    out = jax.ShapeDtypeStruct((group2, width), jnp.bfloat16 if send else jnp.float32)
    return pl.pallas_call(
        functools.partial(back_kernel, send, experts, lanes, 4),
        out_shape=out,
        in_specs=[smem()] + [vmem()] * 5,
        out_specs=vmem(),
        compiler_params=pltpu.CompilerParams(
            vmem_limit_bytes=room(own, other, w_down, sr, r2, out, out)
        ),
        cost_estimate=pl.CostEstimate(
            flops=2 * tokens * f * width,
            bytes_accessed=2 * (2 * tokens * f + 2 * f * width + 2 * group2 * width),
            transcendentals=0,
        ),
        name="expert_back_send" if send else "expert_back_keep",
    )(at, own, other, sr, r2, w_down)


class Moves:
    def __init__(self, owners):
        self.owners = owners
        self.lines = owners // 4

    def go(self, x, where):
        perm = [
            (ep * 2 + core, where(ep, core)) for ep in range(self.owners) for core in range(2)
        ]
        return lax.ppermute(x, ("ep", "pd"), perm)

    def along_z(self, x, shift):
        return self.go(x, lambda ep, core: (ep + 4 * shift) % self.owners * 2 + core)

    def flip(self, x, turn):
        return self.go(x, lambda ep, core: (ep ^ (1 << ((core + turn) % 2))) * 2 + core)

    def cores(self, x):
        return self.go(x, lambda ep, core: ep * 2 + 1 - core)


def body(
    prompt_kv,
    page_owner,
    page_slot,
    page_fill,
    queries,
    new_kv,
    moe_input,
    expert_routes,
    route_probs,
    w_gate,
    w_up,
    w_down,
):
    owners = lax.axis_size("ep")
    me = lax.axis_index("ep").astype(jnp.int32)
    me_ref = me.reshape(1)
    core = lax.axis_index("pd").astype(jnp.int32)
    pages, _, page_len, heads, width = prompt_kv.shape
    requests, steps, q_heads, _ = queries.shape
    d = moe_input.shape[2]
    tokens = requests * steps
    slots = owners * CAP

    moves = Moves(owners)
    top = expert_routes.shape[2]
    lanes = -(-3 * owners // 128) * 128
    at = jnp.stack([me, core])
    own_core = core.reshape(1)
    mine = pl.pallas_call(
        functools.partial(pack_kernel, owners),
        out_shape=jax.ShapeDtypeStruct((tokens, d // 2 + lanes), jnp.bfloat16),
        in_specs=[smem()] + [vmem()] * 3,
        out_specs=vmem(),
        name="pack_tokens",
    )(
        own_core,
        moe_input.transpose(1, 0, 2).reshape(tokens, d),
        expert_routes.reshape(tokens, top),
        route_probs.transpose(1, 0, 2).reshape(tokens, top),
    )
    send = pl.pallas_call(
        functools.partial(page_kernel, pages),
        out_shape=jax.ShapeDtypeStruct((slots, 2, heads, page_len, width), jnp.bfloat16),
        in_specs=[smem(), smem(), vmem()],
        out_specs=vmem(),
        scratch_shapes=[pltpu.SMEM((owners,), jnp.int32)],
        compiler_params=pltpu.CompilerParams(vmem_limit_bytes=room(prompt_kv) * 4),
        name="quantize_pages",
    )(me_ref, page_owner.reshape(-1), prompt_kv.transpose(0, 1, 3, 2, 4))
    line = [mine] + [moves.along_z(mine, -shift) for shift in range(1, moves.lines)]
    line = jnp.concatenate(line, axis=0)
    fresh = new_kv.transpose(2, 3, 0, 1, 4).reshape(2, heads, tokens, width)
    fresh = jnp.pad(fresh, ((0, 0), (0, 0), (0, 128 - tokens), (0, 0)))
    tables = [t.reshape(owners, pages) for t in (page_owner, page_slot, page_fill)]
    line, send = lax.optimization_barrier((line, send))
    sr = jnp.concatenate([line, moves.flip(line, 0)], axis=0)
    sr, fresh, tables = lax.optimization_barrier((sr, fresh, tables))
    r2 = moves.flip(sr, 1)
    cache = lax.all_to_all(send, "ep", split_axis=0, concat_axis=0, tiled=True)
    r2, cache = lax.optimization_barrier((r2, cache))
    other_sr, other_r2 = moves.cores(sr), moves.cores(r2)

    parts = expert_front(own_core, (sr, r2), w_gate, w_up, None)
    hidden = expert_front(own_core, (other_sr, other_r2), w_gate, w_up, parts)
    other_hidden = moves.cores(hidden)
    sent = expert_back(True, owners, at, hidden, other_hidden, w_down, sr, r2, lanes)
    kept = expert_back(False, owners, at, hidden, other_hidden, w_down, sr, r2, lanes)
    attn_out = pl.pallas_call(
        functools.partial(attention_kernel, pages),
        out_shape=jax.ShapeDtypeStruct(queries.shape, jnp.bfloat16),
        in_specs=[smem()] + [vmem()] * 6,
        out_specs=vmem(),
        compiler_params=pltpu.CompilerParams(vmem_limit_bytes=8 * MIB + 16 * slots * page_len * tokens * q_heads),
        name="attention",
    )(
        me_ref,
        *tables,
        queries,
        cache,
        fresh,
    )
    group = moves.lines * tokens
    kept = kept + moves.flip(sent, 0).astype(jnp.float32)
    kept, attn_out = lax.optimization_barrier((kept, attn_out))
    kept = kept[:group] + moves.flip(kept[group:].astype(jnp.bfloat16), 1).astype(jnp.float32)
    moe = kept[:tokens]
    for shift in range(1, moves.lines):
        block = kept[shift * tokens : (shift + 1) * tokens].astype(jnp.bfloat16)
        moe = moe + moves.along_z(block, shift).astype(jnp.float32)
    moe = moe.astype(jnp.bfloat16)
    moe_out = moe.reshape(steps, requests, d // 2).transpose(1, 0, 2)

    return (attn_out, moe_out)


def solution(mesh):
    return jax.shard_map(
        body,
        mesh=mesh,
        in_specs=(
            P(("grp", "ep"), None, None, "pd", None),
            P("grp", None),
            P("grp"),
            P("grp"),
            P(("grp", "ep"), None, "pd", None),
            P(("grp", "ep"), None, None, "pd", None),
            P(("grp", "ep"), None, None),
            P(None, ("grp", "ep"), None),
            P(("grp", "ep"), None, None),
            P("ep", None, "pd"),
            P("ep", None, "pd"),
            P("ep", None, "pd"),
        ),
        out_specs=(P(("grp", "ep"), None, "pd", None), P(("grp", "ep"), None, "pd")),
        check_vma=False,
    )
```

```python
import functools
import math

import jax
import jax.numpy as jnp
from jax import lax
from jax.experimental import pallas as pl
from jax.experimental.pallas import tpu as pltpu
from jax.sharding import PartitionSpec as P

CAP = 2
LIMIT = 448.0
MIB = 1024 * 1024


def vmem():
    return pl.BlockSpec(memory_space=pltpu.VMEM)


def smem():
    return pl.BlockSpec(memory_space=pltpu.SMEM)


def page_kernel(pages, me_ref, owner_ref, kv_ref, send_ref, count_ref):
    values = kv_ref[...].astype(jnp.float32)
    largest = jnp.max(jnp.abs(values), axis=(3, 4), keepdims=True)
    scale = jnp.full(largest.shape, 2.0 ** (-16), jnp.float32)
    inverse = jnp.full(largest.shape, 2.0**16, jnp.float32)
    for exponent in range(-16, -6):
        exceeds = largest > LIMIT * 2.0**exponent
        scale = jnp.where(exceeds, scale * 2.0, scale)
        inverse = jnp.where(exceeds, inverse * 0.5, inverse)
    scaled = values * inverse
    rest = jnp.abs(scaled) * 2.0**6
    step = jnp.full(scaled.shape, 2.0 ** (-9), jnp.float32)
    for bits in (8, 4, 2, 1):
        exceeds = rest >= 2.0**bits
        rest = jnp.where(exceeds, rest * 2.0**-bits, rest)
        step = jnp.where(exceeds, step * 2.0**bits, step)
    levels = jnp.minimum(jnp.floor(rest * 8.0 + 0.5) * step, LIMIT)
    cache = (jnp.where(scaled < 0.0, -levels, levels) * scale).astype(jnp.bfloat16)

    send_ref[...] = jnp.zeros(send_ref.shape, send_ref.dtype)

    def clear(o, carry):
        count_ref[o] = 0
        return carry

    lax.fori_loop(0, count_ref.shape[0], clear, 0)
    first = me_ref[0] * pages
    for page in range(pages):
        owner = owner_ref[first + page]
        rank = count_ref[owner]
        count_ref[owner] = rank + 1
        send_ref[pl.ds(owner * CAP + rank, 1)] = cache[page : page + 1]


def attention_kernel(
    pages, me_ref, owner_ref, slot_ref, fill_ref, q_ref, cache_ref, fresh_ref, out_ref
):
    owners = owner_ref.shape[0]
    slots, _, heads, page_len, width = cache_ref.shape
    requests, steps, q_heads, _ = q_ref.shape
    group = q_heads // heads
    rows = requests * steps * group
    mine = (owner_ref[...] == me_ref[0]).astype(jnp.float32)
    before = (
        lax.broadcasted_iota(jnp.int32, (pages, pages), 0)
        < lax.broadcasted_iota(jnp.int32, (pages, pages), 1)
    ).astype(jnp.float32)
    rank = jnp.dot(mine, before, preferred_element_type=jnp.float32)
    code = (slot_ref[...] * (page_len + 1) + fill_ref[...]).astype(jnp.float32)
    columns = slots * page_len
    place = lax.broadcasted_iota(jnp.int32, (owners, columns), 1)
    source = lax.broadcasted_iota(jnp.int32, (owners, columns), 0)
    spread = jnp.zeros((owners, columns), jnp.float32)
    for c in range(CAP):
        held = jnp.sum(
            jnp.where((mine > 0.0) & (rank == float(c)), code, 0.0), axis=1, keepdims=True
        )
        spread = jnp.where(place // page_len == source * CAP + c, held, spread)
    line = jnp.sum(spread, axis=0, keepdims=True).astype(jnp.int32)
    request_of = line // (page_len + 1)
    fill_of = line - request_of * (page_len + 1)
    position = lax.broadcasted_iota(jnp.int32, (1, columns), 1) % page_len
    request_of = jnp.where(position < fill_of, request_of, -1)
    row_request = lax.broadcasted_iota(jnp.int32, (rows, 1), 0) // (steps * group)
    visible = row_request == request_of
    token = lax.broadcasted_iota(jnp.int32, (rows, 1), 0) // group
    first = row_request * steps
    fresh_at = lax.broadcasted_iota(jnp.int32, (1, fresh_ref.shape[2]), 1)
    fresh_visible = (fresh_at >= first) & (fresh_at <= token)
    factor = 1.0 / math.sqrt(width)
    contract = (((1,), (1,)), ((), ()))
    for head in range(heads):
        q = q_ref[:, :, head * group : (head + 1) * group, :].reshape(rows, width)
        keys = cache_ref[:, 0, head].reshape(columns, width)
        values = cache_ref[:, 1, head].reshape(columns, width)
        scores = lax.dot_general(q, keys, contract, preferred_element_type=jnp.float32) * factor
        fresh = (
            lax.dot_general(q, fresh_ref[0, head], contract, preferred_element_type=jnp.float32)
            * factor
        )
        scores = jnp.where(visible, scores, -jnp.inf)
        fresh = jnp.where(fresh_visible, fresh, -jnp.inf)
        peak = jnp.maximum(
            jnp.max(scores, axis=1, keepdims=True), jnp.max(fresh, axis=1, keepdims=True)
        )
        weight = jnp.exp(scores - peak)
        fresh_weight = jnp.exp(fresh - peak)
        total = jnp.sum(weight, axis=1, keepdims=True) + jnp.sum(
            fresh_weight, axis=1, keepdims=True
        )
        mixed = jnp.dot(
            weight.astype(jnp.bfloat16), values, preferred_element_type=jnp.float32
        ) + jnp.dot(
            fresh_weight.astype(jnp.bfloat16), fresh_ref[1, head], preferred_element_type=jnp.float32
        )
        out_ref[:, :, head * group : (head + 1) * group, :] = (
            (mixed / total).astype(out_ref.dtype).reshape(requests, steps, group, width)
        )


def pack_kernel(experts, core_ref, x_ref, route_ref, prob_ref, out_ref):
    half = x_ref.shape[1] // 2
    begin = pl.multiple_of(core_ref[0] * half, 128)
    out_ref[:, :half] = x_ref[:, pl.ds(begin, half)]
    shape = (x_ref.shape[0], out_ref.shape[1] - half)
    lane = lax.broadcasted_iota(jnp.int32, shape, 1)
    expert = lane % experts
    part = lane // experts
    dense = jnp.zeros(shape, jnp.float32)
    for k in range(route_ref.shape[1]):
        dense += jnp.where(route_ref[:, k : k + 1] == expert, prob_ref[:, k : k + 1], 0.0)
    high = dense.astype(jnp.bfloat16).astype(jnp.float32)
    middle = (dense - high).astype(jnp.bfloat16).astype(jnp.float32)
    low = dense - high - middle
    chosen = jnp.where(part == 0, high, jnp.where(part == 1, middle, low))
    out_ref[:, half:] = jnp.where(part < 3, chosen, 0.0).astype(out_ref.dtype)


def partial_kernel(chunks, sr_ref, r2_ref, gate_ref, up_ref, gate_sum, up_sum):
    half = gate_ref.shape[0]
    depth = half // chunks
    for c in range(chunks):
        at = slice(c * depth, (c + 1) * depth)
        x = jnp.concatenate([sr_ref[:, at], r2_ref[:, at]], axis=0)
        for weight, total in ((gate_ref, gate_sum), (up_ref, up_sum)):
            part = jnp.dot(x, weight[at], preferred_element_type=jnp.float32)
            total[...] = part if c == 0 else total[...] + part


def hidden_kernel(
    chunks, sr_ref, r2_ref, gate_ref, up_ref, gate_part, up_part, out_ref, sums
):
    half = gate_ref.shape[0]
    depth = half // chunks
    group = sr_ref.shape[0] // 2
    for c in range(chunks):
        at = slice(c * depth, (c + 1) * depth)
        x = jnp.concatenate(
            [sr_ref[:group, at], r2_ref[:group, at], sr_ref[group:, at], r2_ref[group:, at]],
            axis=0,
        )
        for i, (weight, start) in enumerate(((gate_ref, gate_part), (up_ref, up_part))):
            part = jnp.dot(x, weight[at], preferred_element_type=jnp.float32)
            sums[i] = (start[...] if c == 0 else sums[i]) + part
    gate = sums[0]
    out_ref[...] = (gate / (1.0 + jnp.exp(-gate)) * sums[1]).astype(out_ref.dtype)


def room(*arrays):
    return sum(math.prod(a.shape) * a.dtype.itemsize for a in arrays) * 9 // 8 + 4 * MIB


def expert_front(rows, w_gate, w_up, parts):
    tokens = 2 * rows[0].shape[0]
    half, f = w_gate.shape
    last = parts is not None
    total = jax.ShapeDtypeStruct((tokens, f), jnp.float32)
    scratch = [pltpu.VMEM((2, tokens, f), jnp.float32)] if last else []
    return pl.pallas_call(
        functools.partial(hidden_kernel if last else partial_kernel, 4),
        in_specs=[vmem()] * (6 if last else 4),
        out_specs=vmem() if last else [vmem(), vmem()],
        scratch_shapes=scratch,
        out_shape=jax.ShapeDtypeStruct((tokens, f), jnp.bfloat16) if last else [total, total],
        compiler_params=pltpu.CompilerParams(
            vmem_limit_bytes=room(*rows, w_gate, w_up, *[total] * (5 if last else 2))
        ),
        cost_estimate=pl.CostEstimate(
            flops=4 * tokens * half * f,
            bytes_accessed=2 * tokens * half + 4 * half * f + 8 * tokens * f,
            transcendentals=tokens * f if last else 0,
        ),
        name="expert_hidden" if last else "expert_partial",
    )(*rows, w_gate, w_up, *(parts or ()))


def back_kernel(
    send, experts, lanes, chunks, at_ref, own_ref, other_ref, sr_ref, r2_ref, down_ref, out_ref
):
    block = down_ref.shape[2] // chunks
    f = own_ref.shape[1]
    group = sr_ref.shape[0] // 2
    core = at_ref[1]
    first = int(send)

    def rows(ref, a, b):
        return jnp.concatenate(
            [ref[a * group : (a + 1) * group], ref[b * group : (b + 1) * group]], axis=0
        )

    own = rows(own_ref, 1, 3) if send else rows(own_ref, 0, 2)
    other = rows(other_ref, 2, 3) if send else rows(other_ref, 0, 1)
    begin = pl.multiple_of(core * f, 128)
    rest = pl.multiple_of((1 - core) * f, 128)
    tail = slice(sr_ref.shape[1] - lanes, sr_ref.shape[1])
    picked = slice(first * group, (first + 1) * group)
    probs = jnp.concatenate(
        [sr_ref[picked, tail].astype(jnp.float32), r2_ref[picked, tail].astype(jnp.float32)],
        axis=0,
    )
    lane = lax.broadcasted_iota(jnp.int32, probs.shape, 1)
    mine = lane % experts == at_ref[0]
    weight = jnp.sum(jnp.where(mine, probs, 0.0), axis=1, keepdims=True)
    for c in range(chunks):
        at = slice(c * block, (c + 1) * block)
        total = jnp.dot(own, down_ref[0, pl.ds(begin, f), at], preferred_element_type=jnp.float32)
        total += jnp.dot(
            other, down_ref[0, pl.ds(rest, f), at], preferred_element_type=jnp.float32
        )
        out_ref[:, at] = (total * weight).astype(out_ref.dtype)


def expert_back(send, experts, at, own, other, w_down, sr, r2, lanes):
    tokens, f = own.shape
    group2 = sr.shape[0]
    width = w_down.shape[2]
    out = jax.ShapeDtypeStruct((group2, width), jnp.bfloat16 if send else jnp.float32)
    return pl.pallas_call(
        functools.partial(back_kernel, send, experts, lanes, 4),
        out_shape=out,
        in_specs=[smem()] + [vmem()] * 5,
        out_specs=vmem(),
        compiler_params=pltpu.CompilerParams(
            vmem_limit_bytes=room(own, other, w_down, sr, r2, out, out)
        ),
        cost_estimate=pl.CostEstimate(
            flops=2 * tokens * f * width,
            bytes_accessed=2 * (2 * tokens * f + 2 * f * width + 2 * group2 * width),
            transcendentals=0,
        ),
        name="expert_back_send" if send else "expert_back_keep",
    )(at, own, other, sr, r2, w_down)


class Moves:
    def __init__(self, owners):
        self.owners = owners
        self.lines = owners // 4

    def go(self, x, where):
        perm = [
            (ep * 2 + core, where(ep, core)) for ep in range(self.owners) for core in range(2)
        ]
        return lax.ppermute(x, ("ep", "pd"), perm)

    def along_z(self, x, shift):
        return self.go(x, lambda ep, core: (ep + 4 * shift) % self.owners * 2 + core)

    def flip(self, x, turn):
        return self.go(x, lambda ep, core: (ep ^ (1 << ((core + turn) % 2))) * 2 + core)

    def cores(self, x):
        return self.go(x, lambda ep, core: ep * 2 + 1 - core)


def body(
    prompt_kv,
    page_owner,
    page_slot,
    page_fill,
    queries,
    new_kv,
    moe_input,
    expert_routes,
    route_probs,
    w_gate,
    w_up,
    w_down,
):
    owners = lax.axis_size("ep")
    me = lax.axis_index("ep").astype(jnp.int32)
    me_ref = me.reshape(1)
    core = lax.axis_index("pd").astype(jnp.int32)
    pages, _, page_len, heads, width = prompt_kv.shape
    requests, steps, q_heads, _ = queries.shape
    d = moe_input.shape[2]
    tokens = requests * steps
    slots = owners * CAP

    moves = Moves(owners)
    top = expert_routes.shape[2]
    lanes = -(-3 * owners // 128) * 128
    at = jnp.stack([me, core])
    own_core = core.reshape(1)
    mine = pl.pallas_call(
        functools.partial(pack_kernel, owners),
        out_shape=jax.ShapeDtypeStruct((tokens, d // 2 + lanes), jnp.bfloat16),
        in_specs=[smem()] + [vmem()] * 3,
        out_specs=vmem(),
        name="pack_tokens",
    )(
        own_core,
        moe_input.transpose(1, 0, 2).reshape(tokens, d),
        expert_routes.reshape(tokens, top),
        route_probs.transpose(1, 0, 2).reshape(tokens, top),
    )
    send = pl.pallas_call(
        functools.partial(page_kernel, pages),
        out_shape=jax.ShapeDtypeStruct((slots, 2, heads, page_len, width), jnp.bfloat16),
        in_specs=[smem(), smem(), vmem()],
        out_specs=vmem(),
        scratch_shapes=[pltpu.SMEM((owners,), jnp.int32)],
        compiler_params=pltpu.CompilerParams(vmem_limit_bytes=room(prompt_kv) * 4),
        name="quantize_pages",
    )(me_ref, page_owner.reshape(-1), prompt_kv.transpose(0, 1, 3, 2, 4))
    line = [mine] + [moves.along_z(mine, -shift) for shift in range(1, moves.lines)]
    line = jnp.concatenate(line, axis=0)
    fresh = new_kv.transpose(2, 3, 0, 1, 4).reshape(2, heads, tokens, width)
    fresh = jnp.pad(fresh, ((0, 0), (0, 0), (0, 128 - tokens), (0, 0)))
    tables = [t.reshape(owners, pages) for t in (page_owner, page_slot, page_fill)]
    line, send = lax.optimization_barrier((line, send))
    sr = jnp.concatenate([line, moves.flip(line, 0)], axis=0)
    sr, fresh, tables = lax.optimization_barrier((sr, fresh, tables))
    r2 = moves.flip(sr, 1)
    cache = lax.all_to_all(send, "ep", split_axis=0, concat_axis=0, tiled=True)
    core_then, cache = lax.optimization_barrier((core, cache))

    def weights_of(half):
        return [
            lax.dynamic_slice_in_dim(w[0], half * (d // 2), d // 2, axis=0) for w in (w_gate, w_up)
        ]

    near_weights = weights_of(core_then)
    r2, near_weights = lax.optimization_barrier((r2, near_weights))
    other_sr, other_r2 = moves.cores(sr), moves.cores(r2)

    parts = expert_front((sr, r2), *near_weights, None)
    hidden = expert_front((other_sr, other_r2), *weights_of(1 - core_then), parts)
    other_hidden = moves.cores(hidden)
    sent = expert_back(True, owners, at, hidden, other_hidden, w_down, sr, r2, lanes)
    kept = expert_back(False, owners, at, hidden, other_hidden, w_down, sr, r2, lanes)
    attn_out = pl.pallas_call(
        functools.partial(attention_kernel, pages),
        out_shape=jax.ShapeDtypeStruct(queries.shape, jnp.bfloat16),
        in_specs=[smem()] + [vmem()] * 6,
        out_specs=vmem(),
        compiler_params=pltpu.CompilerParams(vmem_limit_bytes=8 * MIB + 16 * slots * page_len * tokens * q_heads),
        name="attention",
    )(
        me_ref,
        *tables,
        queries,
        cache,
        fresh,
    )
    group = moves.lines * tokens
    kept = kept + moves.flip(sent, 0).astype(jnp.float32)
    kept, attn_out = lax.optimization_barrier((kept, attn_out))
    kept = kept[:group] + moves.flip(kept[group:].astype(jnp.bfloat16), 1).astype(jnp.float32)
    moe = kept[:tokens]
    for shift in range(1, moves.lines):
        block = kept[shift * tokens : (shift + 1) * tokens].astype(jnp.bfloat16)
        moe = moe + moves.along_z(block, shift).astype(jnp.float32)
    moe = moe.astype(jnp.bfloat16)
    moe_out = moe.reshape(steps, requests, d // 2).transpose(1, 0, 2)

    return (attn_out, moe_out)


def solution(mesh):
    return jax.shard_map(
        body,
        mesh=mesh,
        in_specs=(
            P(("grp", "ep"), None, None, "pd", None),
            P("grp", None),
            P("grp"),
            P("grp"),
            P(("grp", "ep"), None, "pd", None),
            P(("grp", "ep"), None, None, "pd", None),
            P(("grp", "ep"), None, None),
            P(None, ("grp", "ep"), None),
            P(("grp", "ep"), None, None),
            P("ep", None, "pd"),
            P("ep", None, "pd"),
            P("ep", None, "pd"),
        ),
        out_specs=(P(("grp", "ep"), None, "pd", None), P(("grp", "ep"), None, "pd")),
        check_vma=False,
    )
```

```python
import functools
import math

import jax
import jax.numpy as jnp
from jax import lax
from jax.experimental import pallas as pl
from jax.experimental.pallas import tpu as pltpu
from jax.sharding import PartitionSpec as P

CAP = 2
LIMIT = 448.0
MIB = 1024 * 1024


def vmem():
    return pl.BlockSpec(memory_space=pltpu.VMEM)


def smem():
    return pl.BlockSpec(memory_space=pltpu.SMEM)


def page_kernel(pages, me_ref, owner_ref, kv_ref, send_ref, count_ref):
    values = kv_ref[...].astype(jnp.float32)
    largest = jnp.max(jnp.abs(values), axis=(3, 4), keepdims=True)
    scale = jnp.full(largest.shape, 2.0 ** (-16), jnp.float32)
    inverse = jnp.full(largest.shape, 2.0**16, jnp.float32)
    for exponent in range(-16, -6):
        exceeds = largest > LIMIT * 2.0**exponent
        scale = jnp.where(exceeds, scale * 2.0, scale)
        inverse = jnp.where(exceeds, inverse * 0.5, inverse)
    scaled = values * inverse
    rest = jnp.abs(scaled) * 2.0**6
    step = jnp.full(scaled.shape, 2.0 ** (-9), jnp.float32)
    for bits in (8, 4, 2, 1):
        exceeds = rest >= 2.0**bits
        rest = jnp.where(exceeds, rest * 2.0**-bits, rest)
        step = jnp.where(exceeds, step * 2.0**bits, step)
    levels = jnp.minimum(jnp.floor(rest * 8.0 + 0.5) * step, LIMIT)
    cache = (jnp.where(scaled < 0.0, -levels, levels) * scale).astype(jnp.bfloat16)

    send_ref[...] = jnp.zeros(send_ref.shape, send_ref.dtype)

    def clear(o, carry):
        count_ref[o] = 0
        return carry

    lax.fori_loop(0, count_ref.shape[0], clear, 0)
    first = me_ref[0] * pages
    for page in range(pages):
        owner = owner_ref[first + page]
        rank = count_ref[owner]
        count_ref[owner] = rank + 1
        send_ref[pl.ds(owner * CAP + rank, 1)] = cache[page : page + 1]


def attention_kernel(
    pages, me_ref, owner_ref, slot_ref, fill_ref, q_ref, cache_ref, fresh_ref, out_ref
):
    owners = owner_ref.shape[0]
    slots, _, heads, page_len, width = cache_ref.shape
    requests, steps, q_heads, _ = q_ref.shape
    group = q_heads // heads
    rows = requests * steps * group
    mine = (owner_ref[...] == me_ref[0]).astype(jnp.float32)
    before = (
        lax.broadcasted_iota(jnp.int32, (pages, pages), 0)
        < lax.broadcasted_iota(jnp.int32, (pages, pages), 1)
    ).astype(jnp.float32)
    rank = jnp.dot(mine, before, preferred_element_type=jnp.float32)
    code = (slot_ref[...] * (page_len + 1) + fill_ref[...]).astype(jnp.float32)
    columns = slots * page_len
    place = lax.broadcasted_iota(jnp.int32, (owners, columns), 1)
    source = lax.broadcasted_iota(jnp.int32, (owners, columns), 0)
    spread = jnp.zeros((owners, columns), jnp.float32)
    for c in range(CAP):
        held = jnp.sum(
            jnp.where((mine > 0.0) & (rank == float(c)), code, 0.0), axis=1, keepdims=True
        )
        spread = jnp.where(place // page_len == source * CAP + c, held, spread)
    line = jnp.sum(spread, axis=0, keepdims=True).astype(jnp.int32)
    request_of = line // (page_len + 1)
    fill_of = line - request_of * (page_len + 1)
    position = lax.broadcasted_iota(jnp.int32, (1, columns), 1) % page_len
    request_of = jnp.where(position < fill_of, request_of, -1)
    row_request = lax.broadcasted_iota(jnp.int32, (rows, 1), 0) // (steps * group)
    visible = row_request == request_of
    token = lax.broadcasted_iota(jnp.int32, (rows, 1), 0) // group
    first = row_request * steps
    fresh_at = lax.broadcasted_iota(jnp.int32, (1, fresh_ref.shape[2]), 1)
    fresh_visible = (fresh_at >= first) & (fresh_at <= token)
    factor = 1.0 / math.sqrt(width)
    contract = (((1,), (1,)), ((), ()))
    for head in range(heads):
        q = q_ref[:, :, head * group : (head + 1) * group, :].reshape(rows, width)
        keys = cache_ref[:, 0, head].reshape(columns, width)
        values = cache_ref[:, 1, head].reshape(columns, width)
        scores = lax.dot_general(q, keys, contract, preferred_element_type=jnp.float32) * factor
        fresh = (
            lax.dot_general(q, fresh_ref[0, head], contract, preferred_element_type=jnp.float32)
            * factor
        )
        scores = jnp.where(visible, scores, -jnp.inf)
        fresh = jnp.where(fresh_visible, fresh, -jnp.inf)
        peak = jnp.maximum(
            jnp.max(scores, axis=1, keepdims=True), jnp.max(fresh, axis=1, keepdims=True)
        )
        weight = jnp.exp(scores - peak)
        fresh_weight = jnp.exp(fresh - peak)
        total = jnp.sum(weight, axis=1, keepdims=True) + jnp.sum(
            fresh_weight, axis=1, keepdims=True
        )
        mixed = jnp.dot(
            weight.astype(jnp.bfloat16), values, preferred_element_type=jnp.float32
        ) + jnp.dot(
            fresh_weight.astype(jnp.bfloat16), fresh_ref[1, head], preferred_element_type=jnp.float32
        )
        out_ref[:, :, head * group : (head + 1) * group, :] = (
            (mixed / total).astype(out_ref.dtype).reshape(requests, steps, group, width)
        )


def pack_kernel(experts, core_ref, x_ref, route_ref, prob_ref, out_ref):
    half = x_ref.shape[1] // 2
    begin = pl.multiple_of(core_ref[0] * half, 128)
    out_ref[:, :half] = x_ref[:, pl.ds(begin, half)]
    shape = (x_ref.shape[0], out_ref.shape[1] - half)
    lane = lax.broadcasted_iota(jnp.int32, shape, 1)
    expert = lane % experts
    part = lane // experts
    dense = jnp.zeros(shape, jnp.float32)
    for k in range(route_ref.shape[1]):
        dense += jnp.where(route_ref[:, k : k + 1] == expert, prob_ref[:, k : k + 1], 0.0)
    high = dense.astype(jnp.bfloat16).astype(jnp.float32)
    middle = (dense - high).astype(jnp.bfloat16).astype(jnp.float32)
    low = dense - high - middle
    chosen = jnp.where(part == 0, high, jnp.where(part == 1, middle, low))
    out_ref[:, half:] = jnp.where(part < 3, chosen, 0.0).astype(out_ref.dtype)


def partial_kernel(chunks, sr_ref, r2_ref, gate_ref, up_ref, gate_sum, up_sum):
    half = gate_ref.shape[0]
    depth = half // chunks
    for c in range(chunks):
        at = slice(c * depth, (c + 1) * depth)
        x = jnp.concatenate([sr_ref[:, at], r2_ref[:, at]], axis=0)
        for weight, total in ((gate_ref, gate_sum), (up_ref, up_sum)):
            part = jnp.dot(x, weight[at], preferred_element_type=jnp.float32)
            total[...] = part if c == 0 else total[...] + part


def hidden_kernel(
    chunks, sr_ref, r2_ref, gate_ref, up_ref, gate_part, up_part, out_ref, sums
):
    half = gate_ref.shape[0]
    depth = half // chunks
    group = sr_ref.shape[0] // 2
    for c in range(chunks):
        at = slice(c * depth, (c + 1) * depth)
        x = jnp.concatenate(
            [sr_ref[:group, at], r2_ref[:group, at], sr_ref[group:, at], r2_ref[group:, at]],
            axis=0,
        )
        for i, (weight, start) in enumerate(((gate_ref, gate_part), (up_ref, up_part))):
            part = jnp.dot(x, weight[at], preferred_element_type=jnp.float32)
            sums[i] = (start[...] if c == 0 else sums[i]) + part
    gate = sums[0]
    out_ref[...] = (gate / (1.0 + jnp.exp(-gate)) * sums[1]).astype(out_ref.dtype)


def room(*arrays):
    return sum(math.prod(a.shape) * a.dtype.itemsize for a in arrays) * 9 // 8 + 4 * MIB


def expert_front(rows, w_gate, w_up, parts):
    tokens = 2 * rows[0].shape[0]
    half, f = w_gate.shape
    last = parts is not None
    total = jax.ShapeDtypeStruct((tokens, f), jnp.float32)
    scratch = [pltpu.VMEM((2, tokens, f), jnp.float32)] if last else []
    return pl.pallas_call(
        functools.partial(hidden_kernel if last else partial_kernel, 4),
        in_specs=[vmem()] * (6 if last else 4),
        out_specs=vmem() if last else [vmem(), vmem()],
        scratch_shapes=scratch,
        out_shape=jax.ShapeDtypeStruct((tokens, f), jnp.bfloat16) if last else [total, total],
        compiler_params=pltpu.CompilerParams(
            vmem_limit_bytes=room(*rows, w_gate, w_up, *[total] * (5 if last else 2))
        ),
        cost_estimate=pl.CostEstimate(
            flops=4 * tokens * half * f,
            bytes_accessed=2 * tokens * half + 4 * half * f + 8 * tokens * f,
            transcendentals=tokens * f if last else 0,
        ),
        name="expert_hidden" if last else "expert_partial",
    )(*rows, w_gate, w_up, *(parts or ()))


def back_kernel(
    send, experts, lanes, chunks, at_ref, own_ref, other_ref, sr_ref, r2_ref, down_ref, out_ref
):
    block = down_ref.shape[2] // chunks
    f = own_ref.shape[1]
    group = sr_ref.shape[0] // 2
    core = at_ref[1]
    first = int(send)

    def rows(ref, a, b):
        return jnp.concatenate(
            [ref[a * group : (a + 1) * group], ref[b * group : (b + 1) * group]], axis=0
        )

    own = rows(own_ref, 1, 3) if send else rows(own_ref, 0, 2)
    other = rows(other_ref, 2, 3) if send else rows(other_ref, 0, 1)
    begin = pl.multiple_of(core * f, 128)
    rest = pl.multiple_of((1 - core) * f, 128)
    tail = slice(sr_ref.shape[1] - lanes, sr_ref.shape[1])
    picked = slice(first * group, (first + 1) * group)
    probs = jnp.concatenate(
        [sr_ref[picked, tail].astype(jnp.float32), r2_ref[picked, tail].astype(jnp.float32)],
        axis=0,
    )
    lane = lax.broadcasted_iota(jnp.int32, probs.shape, 1)
    mine = lane % experts == at_ref[0]
    weight = jnp.sum(jnp.where(mine, probs, 0.0), axis=1, keepdims=True)
    for c in range(chunks):
        at = slice(c * block, (c + 1) * block)
        total = jnp.dot(own, down_ref[0, pl.ds(begin, f), at], preferred_element_type=jnp.float32)
        total += jnp.dot(
            other, down_ref[0, pl.ds(rest, f), at], preferred_element_type=jnp.float32
        )
        out_ref[:, at] = (total * weight).astype(out_ref.dtype)


def expert_back(send, experts, at, own, other, w_down, sr, r2, lanes):
    tokens, f = own.shape
    group2 = sr.shape[0]
    width = w_down.shape[2]
    out = jax.ShapeDtypeStruct((group2, width), jnp.bfloat16 if send else jnp.float32)
    return pl.pallas_call(
        functools.partial(back_kernel, send, experts, lanes, 4),
        out_shape=out,
        in_specs=[smem()] + [vmem()] * 5,
        out_specs=vmem(),
        compiler_params=pltpu.CompilerParams(
            vmem_limit_bytes=room(own, other, w_down, sr, r2, out, out)
        ),
        cost_estimate=pl.CostEstimate(
            flops=2 * tokens * f * width,
            bytes_accessed=2 * (2 * tokens * f + 2 * f * width + 2 * group2 * width),
            transcendentals=0,
        ),
        name="expert_back_send" if send else "expert_back_keep",
    )(at, own, other, sr, r2, w_down)


class Moves:
    def __init__(self, owners):
        self.owners = owners
        self.lines = owners // 4

    def go(self, x, where):
        perm = [
            (ep * 2 + core, where(ep, core)) for ep in range(self.owners) for core in range(2)
        ]
        return lax.ppermute(x, ("ep", "pd"), perm)

    def along_z(self, x, turn):
        return self.go(x, lambda ep, core: (ep ^ (4 * turn)) * 2 + core)

    def flip(self, x, turn):
        return self.go(x, lambda ep, core: (ep ^ (1 << ((core + turn) % 2))) * 2 + core)

    def cores(self, x):
        return self.go(x, lambda ep, core: ep * 2 + 1 - core)


def body(
    prompt_kv,
    page_owner,
    page_slot,
    page_fill,
    queries,
    new_kv,
    moe_input,
    expert_routes,
    route_probs,
    w_gate,
    w_up,
    w_down,
):
    owners = lax.axis_size("ep")
    me = lax.axis_index("ep").astype(jnp.int32)
    me_ref = me.reshape(1)
    core = lax.axis_index("pd").astype(jnp.int32)
    pages, _, page_len, heads, width = prompt_kv.shape
    requests, steps, q_heads, _ = queries.shape
    d = moe_input.shape[2]
    tokens = requests * steps
    slots = owners * CAP

    moves = Moves(owners)
    top = expert_routes.shape[2]
    lanes = -(-3 * owners // 128) * 128
    at = jnp.stack([me, core])
    own_core = core.reshape(1)
    mine = pl.pallas_call(
        functools.partial(pack_kernel, owners),
        out_shape=jax.ShapeDtypeStruct((tokens, d // 2 + lanes), jnp.bfloat16),
        in_specs=[smem()] + [vmem()] * 3,
        out_specs=vmem(),
        name="pack_tokens",
    )(
        own_core,
        moe_input.transpose(1, 0, 2).reshape(tokens, d),
        expert_routes.reshape(tokens, top),
        route_probs.transpose(1, 0, 2).reshape(tokens, top),
    )
    send = pl.pallas_call(
        functools.partial(page_kernel, pages),
        out_shape=jax.ShapeDtypeStruct((slots, 2, heads, page_len, width), jnp.bfloat16),
        in_specs=[smem(), smem(), vmem()],
        out_specs=vmem(),
        scratch_shapes=[pltpu.SMEM((owners,), jnp.int32)],
        compiler_params=pltpu.CompilerParams(vmem_limit_bytes=room(prompt_kv) * 4),
        name="quantize_pages",
    )(me_ref, page_owner.reshape(-1), prompt_kv.transpose(0, 1, 3, 2, 4))
    line = [mine] + [moves.along_z(mine, shift) for shift in range(1, moves.lines)]
    line = jnp.concatenate(line, axis=0)
    fresh = new_kv.transpose(2, 3, 0, 1, 4).reshape(2, heads, tokens, width)
    fresh = jnp.pad(fresh, ((0, 0), (0, 0), (0, 128 - tokens), (0, 0)))
    tables = [t.reshape(owners, pages) for t in (page_owner, page_slot, page_fill)]
    line, send = lax.optimization_barrier((line, send))
    sr = jnp.concatenate([line, moves.flip(line, 0)], axis=0)
    sr, fresh, tables = lax.optimization_barrier((sr, fresh, tables))
    r2 = moves.flip(sr, 1)
    cache = lax.all_to_all(send, "ep", split_axis=0, concat_axis=0, tiled=True)
    core_then, cache = lax.optimization_barrier((core, cache))

    def weights_of(half):
        return [
            lax.dynamic_slice_in_dim(w[0], half * (d // 2), d // 2, axis=0) for w in (w_gate, w_up)
        ]

    near_weights = weights_of(core_then)
    r2, near_weights = lax.optimization_barrier((r2, near_weights))
    other_sr, other_r2 = moves.cores(sr), moves.cores(r2)

    parts = expert_front((sr, r2), *near_weights, None)
    hidden = expert_front((other_sr, other_r2), *weights_of(1 - core_then), parts)
    other_hidden = moves.cores(hidden)
    sent = expert_back(True, owners, at, hidden, other_hidden, w_down, sr, r2, lanes)
    kept = expert_back(False, owners, at, hidden, other_hidden, w_down, sr, r2, lanes)
    attn_out = pl.pallas_call(
        functools.partial(attention_kernel, pages),
        out_shape=jax.ShapeDtypeStruct(queries.shape, jnp.bfloat16),
        in_specs=[smem()] + [vmem()] * 6,
        out_specs=vmem(),
        compiler_params=pltpu.CompilerParams(vmem_limit_bytes=8 * MIB + 16 * slots * page_len * tokens * q_heads),
        name="attention",
    )(
        me_ref,
        *tables,
        queries,
        cache,
        fresh,
    )
    group = moves.lines * tokens
    kept = kept + moves.flip(sent, 0).astype(jnp.float32)
    kept, attn_out = lax.optimization_barrier((kept, attn_out))
    kept = kept[:group] + moves.flip(kept[group:].astype(jnp.bfloat16), 1).astype(jnp.float32)
    moe = kept[:tokens]
    for shift in range(1, moves.lines):
        block = kept[shift * tokens : (shift + 1) * tokens].astype(jnp.bfloat16)
        moe = moe + moves.along_z(block, shift).astype(jnp.float32)
    moe = moe.astype(jnp.bfloat16)
    moe_out = moe.reshape(steps, requests, d // 2).transpose(1, 0, 2)

    return (attn_out, moe_out)


def solution(mesh):
    return jax.shard_map(
        body,
        mesh=mesh,
        in_specs=(
            P(("grp", "ep"), None, None, "pd", None),
            P("grp", None),
            P("grp"),
            P("grp"),
            P(("grp", "ep"), None, "pd", None),
            P(("grp", "ep"), None, None, "pd", None),
            P(("grp", "ep"), None, None),
            P(None, ("grp", "ep"), None),
            P(("grp", "ep"), None, None),
            P("ep", None, "pd"),
            P("ep", None, "pd"),
            P("ep", None, "pd"),
        ),
        out_specs=(P(("grp", "ep"), None, "pd", None), P(("grp", "ep"), None, "pd")),
        check_vma=False,
    )
```

```python
import functools
import math

import jax
import jax.numpy as jnp
from jax import lax
from jax.experimental import pallas as pl
from jax.experimental.pallas import tpu as pltpu
from jax.sharding import PartitionSpec as P

CAP = 2
LIMIT = 448.0
MIB = 1024 * 1024


def vmem():
    return pl.BlockSpec(memory_space=pltpu.VMEM)


def smem():
    return pl.BlockSpec(memory_space=pltpu.SMEM)


def page_kernel(pages, me_ref, owner_ref, kv_ref, send_ref, count_ref):
    values = kv_ref[...].astype(jnp.float32)
    largest = jnp.max(jnp.abs(values), axis=(3, 4), keepdims=True)
    scale = jnp.full(largest.shape, 2.0 ** (-16), jnp.float32)
    inverse = jnp.full(largest.shape, 2.0**16, jnp.float32)
    for exponent in range(-16, -6):
        exceeds = largest > LIMIT * 2.0**exponent
        scale = jnp.where(exceeds, scale * 2.0, scale)
        inverse = jnp.where(exceeds, inverse * 0.5, inverse)
    scaled = values * inverse
    rest = jnp.abs(scaled) * 2.0**6
    step = jnp.full(scaled.shape, 2.0 ** (-9), jnp.float32)
    for bits in (8, 4, 2, 1):
        exceeds = rest >= 2.0**bits
        rest = jnp.where(exceeds, rest * 2.0**-bits, rest)
        step = jnp.where(exceeds, step * 2.0**bits, step)
    levels = jnp.minimum(jnp.floor(rest * 8.0 + 0.5) * step, LIMIT)
    cache = (jnp.where(scaled < 0.0, -levels, levels) * scale).astype(jnp.bfloat16)

    send_ref[...] = jnp.zeros(send_ref.shape, send_ref.dtype)

    def clear(o, carry):
        count_ref[o] = 0
        return carry

    lax.fori_loop(0, count_ref.shape[0], clear, 0)
    first = me_ref[0] * pages
    for page in range(pages):
        owner = owner_ref[first + page]
        rank = count_ref[owner]
        count_ref[owner] = rank + 1
        send_ref[pl.ds(owner * CAP + rank, 1)] = cache[page : page + 1]


def attention_kernel(
    pages, me_ref, owner_ref, slot_ref, fill_ref, q_ref, cache_ref, fresh_ref, out_ref
):
    owners = owner_ref.shape[0]
    slots, _, heads, page_len, width = cache_ref.shape
    requests, steps, q_heads, _ = q_ref.shape
    group = q_heads // heads
    rows = requests * steps * group
    mine = (owner_ref[...] == me_ref[0]).astype(jnp.float32)
    before = (
        lax.broadcasted_iota(jnp.int32, (pages, pages), 0)
        < lax.broadcasted_iota(jnp.int32, (pages, pages), 1)
    ).astype(jnp.float32)
    rank = jnp.dot(mine, before, preferred_element_type=jnp.float32)
    code = (slot_ref[...] * (page_len + 1) + fill_ref[...]).astype(jnp.float32)
    columns = slots * page_len
    place = lax.broadcasted_iota(jnp.int32, (owners, columns), 1)
    source = lax.broadcasted_iota(jnp.int32, (owners, columns), 0)
    spread = jnp.zeros((owners, columns), jnp.float32)
    for c in range(CAP):
        held = jnp.sum(
            jnp.where((mine > 0.0) & (rank == float(c)), code, 0.0), axis=1, keepdims=True
        )
        spread = jnp.where(place // page_len == source * CAP + c, held, spread)
    line = jnp.sum(spread, axis=0, keepdims=True).astype(jnp.int32)
    request_of = line // (page_len + 1)
    fill_of = line - request_of * (page_len + 1)
    position = lax.broadcasted_iota(jnp.int32, (1, columns), 1) % page_len
    request_of = jnp.where(position < fill_of, request_of, -1)
    row_request = lax.broadcasted_iota(jnp.int32, (rows, 1), 0) // (steps * group)
    visible = row_request == request_of
    token = lax.broadcasted_iota(jnp.int32, (rows, 1), 0) // group
    first = row_request * steps
    fresh_at = lax.broadcasted_iota(jnp.int32, (1, fresh_ref.shape[2]), 1)
    fresh_visible = (fresh_at >= first) & (fresh_at <= token)
    factor = 1.0 / math.sqrt(width)
    contract = (((1,), (1,)), ((), ()))
    for head in range(heads):
        q = q_ref[:, :, head * group : (head + 1) * group, :].reshape(rows, width)
        keys = cache_ref[:, 0, head].reshape(columns, width)
        values = cache_ref[:, 1, head].reshape(columns, width)
        scores = lax.dot_general(q, keys, contract, preferred_element_type=jnp.float32) * factor
        fresh = (
            lax.dot_general(q, fresh_ref[0, head], contract, preferred_element_type=jnp.float32)
            * factor
        )
        scores = jnp.where(visible, scores, -jnp.inf)
        fresh = jnp.where(fresh_visible, fresh, -jnp.inf)
        peak = jnp.maximum(
            jnp.max(scores, axis=1, keepdims=True), jnp.max(fresh, axis=1, keepdims=True)
        )
        weight = jnp.exp(scores - peak)
        fresh_weight = jnp.exp(fresh - peak)
        total = jnp.sum(weight, axis=1, keepdims=True) + jnp.sum(
            fresh_weight, axis=1, keepdims=True
        )
        mixed = jnp.dot(
            weight.astype(jnp.bfloat16), values, preferred_element_type=jnp.float32
        ) + jnp.dot(
            fresh_weight.astype(jnp.bfloat16), fresh_ref[1, head], preferred_element_type=jnp.float32
        )
        out_ref[:, :, head * group : (head + 1) * group, :] = (
            (mixed / total).astype(out_ref.dtype).reshape(requests, steps, group, width)
        )


def pack_kernel(experts, core_ref, x_ref, route_ref, prob_ref, out_ref):
    half = x_ref.shape[1]
    out_ref[:, :half] = x_ref[...]
    shape = (x_ref.shape[0], out_ref.shape[1] - half)
    lane = lax.broadcasted_iota(jnp.int32, shape, 1)
    expert = lane % experts
    part = lane // experts
    dense = jnp.zeros(shape, jnp.float32)
    for k in range(route_ref.shape[1]):
        dense += jnp.where(route_ref[:, k : k + 1] == expert, prob_ref[:, k : k + 1], 0.0)
    high = dense.astype(jnp.bfloat16).astype(jnp.float32)
    middle = (dense - high).astype(jnp.bfloat16).astype(jnp.float32)
    low = dense - high - middle
    chosen = jnp.where(part == 0, high, jnp.where(part == 1, middle, low))
    out_ref[:, half:] = jnp.where(part < 3, chosen, 0.0).astype(out_ref.dtype)


def partial_kernel(chunks, sr_ref, r2_ref, gate_ref, up_ref, gate_sum, up_sum):
    half = gate_ref.shape[0]
    depth = half // chunks
    for c in range(chunks):
        at = slice(c * depth, (c + 1) * depth)
        x = jnp.concatenate([sr_ref[:, at], r2_ref[:, at]], axis=0)
        for weight, total in ((gate_ref, gate_sum), (up_ref, up_sum)):
            part = jnp.dot(x, weight[at], preferred_element_type=jnp.float32)
            total[...] = part if c == 0 else total[...] + part


def hidden_kernel(
    chunks, sr_ref, r2_ref, gate_ref, up_ref, gate_part, up_part, out_ref, sums
):
    half = gate_ref.shape[0]
    depth = half // chunks
    group = sr_ref.shape[0] // 2
    for c in range(chunks):
        at = slice(c * depth, (c + 1) * depth)
        x = jnp.concatenate(
            [sr_ref[:group, at], r2_ref[:group, at], sr_ref[group:, at], r2_ref[group:, at]],
            axis=0,
        )
        for i, (weight, start) in enumerate(((gate_ref, gate_part), (up_ref, up_part))):
            part = jnp.dot(x, weight[at], preferred_element_type=jnp.float32)
            sums[i] = (start[...] if c == 0 else sums[i]) + part
    gate = sums[0]
    out_ref[...] = (gate / (1.0 + jnp.exp(-gate)) * sums[1]).astype(out_ref.dtype)


def room(*arrays):
    return sum(math.prod(a.shape) * a.dtype.itemsize for a in arrays) * 9 // 8 + 4 * MIB


def expert_front(rows, w_gate, w_up, parts):
    tokens = 2 * rows[0].shape[0]
    half, f = w_gate.shape
    last = parts is not None
    total = jax.ShapeDtypeStruct((tokens, f), jnp.float32)
    scratch = [pltpu.VMEM((2, tokens, f), jnp.float32)] if last else []
    return pl.pallas_call(
        functools.partial(hidden_kernel if last else partial_kernel, 4),
        in_specs=[vmem()] * (6 if last else 4),
        out_specs=vmem() if last else [vmem(), vmem()],
        scratch_shapes=scratch,
        out_shape=jax.ShapeDtypeStruct((tokens, f), jnp.bfloat16) if last else [total, total],
        compiler_params=pltpu.CompilerParams(
            vmem_limit_bytes=room(*rows, w_gate, w_up, *[total] * (5 if last else 2))
        ),
        cost_estimate=pl.CostEstimate(
            flops=4 * tokens * half * f,
            bytes_accessed=2 * tokens * half + 4 * half * f + 8 * tokens * f,
            transcendentals=tokens * f if last else 0,
        ),
        name="expert_hidden" if last else "expert_partial",
    )(*rows, w_gate, w_up, *(parts or ()))


def back_kernel(
    send, experts, lanes, chunks, at_ref, own_ref, other_ref, sr_ref, r2_ref, down_ref, out_ref
):
    block = down_ref.shape[2] // chunks
    f = own_ref.shape[1]
    group = sr_ref.shape[0] // 2
    core = at_ref[1]
    first = int(send)

    def rows(ref, a, b):
        return jnp.concatenate(
            [ref[a * group : (a + 1) * group], ref[b * group : (b + 1) * group]], axis=0
        )

    own = rows(own_ref, 1, 3) if send else rows(own_ref, 0, 2)
    other = rows(other_ref, 2, 3) if send else rows(other_ref, 0, 1)
    begin = pl.multiple_of(core * f, 128)
    rest = pl.multiple_of((1 - core) * f, 128)
    tail = slice(sr_ref.shape[1] - lanes, sr_ref.shape[1])
    picked = slice(first * group, (first + 1) * group)
    probs = jnp.concatenate(
        [sr_ref[picked, tail].astype(jnp.float32), r2_ref[picked, tail].astype(jnp.float32)],
        axis=0,
    )
    lane = lax.broadcasted_iota(jnp.int32, probs.shape, 1)
    mine = lane % experts == at_ref[0]
    weight = jnp.sum(jnp.where(mine, probs, 0.0), axis=1, keepdims=True)
    for c in range(chunks):
        at = slice(c * block, (c + 1) * block)
        total = jnp.dot(own, down_ref[0, pl.ds(begin, f), at], preferred_element_type=jnp.float32)
        total += jnp.dot(
            other, down_ref[0, pl.ds(rest, f), at], preferred_element_type=jnp.float32
        )
        out_ref[:, at] = (total * weight).astype(out_ref.dtype)


def expert_back(send, experts, at, own, other, w_down, sr, r2, lanes):
    tokens, f = own.shape
    group2 = sr.shape[0]
    width = w_down.shape[2]
    out = jax.ShapeDtypeStruct((group2, width), jnp.bfloat16 if send else jnp.float32)
    return pl.pallas_call(
        functools.partial(back_kernel, send, experts, lanes, 4),
        out_shape=out,
        in_specs=[smem()] + [vmem()] * 5,
        out_specs=vmem(),
        compiler_params=pltpu.CompilerParams(
            vmem_limit_bytes=room(own, other, w_down, sr, r2, out, out)
        ),
        cost_estimate=pl.CostEstimate(
            flops=2 * tokens * f * width,
            bytes_accessed=2 * (2 * tokens * f + 2 * f * width + 2 * group2 * width),
            transcendentals=0,
        ),
        name="expert_back_send" if send else "expert_back_keep",
    )(at, own, other, sr, r2, w_down)


class Moves:
    def __init__(self, owners):
        self.owners = owners
        self.lines = owners // 4

    def go(self, x, where):
        perm = [
            (ep * 2 + core, where(ep, core)) for ep in range(self.owners) for core in range(2)
        ]
        return lax.ppermute(x, ("ep", "pd"), perm)

    def along_z(self, x, shift):
        return self.go(x, lambda ep, core: (ep + 4 * shift) % self.owners * 2 + core)

    def flip(self, x, turn):
        return self.go(x, lambda ep, core: (ep ^ (1 << ((core + turn) % 2))) * 2 + core)

    def cores(self, x):
        return self.go(x, lambda ep, core: ep * 2 + 1 - core)


def body(
    prompt_kv,
    page_owner,
    page_slot,
    page_fill,
    queries,
    new_kv,
    moe_input,
    expert_routes,
    route_probs,
    w_gate,
    w_up,
    w_down,
):
    owners = lax.axis_size("ep")
    me = lax.axis_index("ep").astype(jnp.int32)
    me_ref = me.reshape(1)
    core = lax.axis_index("pd").astype(jnp.int32)
    pages, _, page_len, heads, width = prompt_kv.shape
    requests, steps, q_heads, _ = queries.shape
    d = moe_input.shape[2]
    tokens = requests * steps
    slots = owners * CAP

    moves = Moves(owners)
    top = expert_routes.shape[2]
    lanes = -(-3 * owners // 128) * 128
    at = jnp.stack([me, core])
    own_core = core.reshape(1)
    mine = pl.pallas_call(
        functools.partial(pack_kernel, owners),
        out_shape=jax.ShapeDtypeStruct((tokens, d // 2 + lanes), jnp.bfloat16),
        grid_spec=pltpu.PrefetchScalarGridSpec(
            num_scalar_prefetch=1,
            grid=(1,),
            in_specs=[
                pl.BlockSpec((tokens, d // 2), lambda i, core: (0, core[0])),
                pl.BlockSpec((tokens, top), lambda i, core: (0, 0)),
                pl.BlockSpec((tokens, top), lambda i, core: (0, 0)),
            ],
            out_specs=pl.BlockSpec((tokens, d // 2 + lanes), lambda i, core: (0, 0)),
        ),
        name="pack_tokens",
    )(
        own_core,
        moe_input.transpose(1, 0, 2).reshape(tokens, d),
        expert_routes.reshape(tokens, top),
        route_probs.transpose(1, 0, 2).reshape(tokens, top),
    )
    send = pl.pallas_call(
        functools.partial(page_kernel, pages),
        out_shape=jax.ShapeDtypeStruct((slots, 2, heads, page_len, width), jnp.bfloat16),
        in_specs=[smem(), smem(), vmem()],
        out_specs=vmem(),
        scratch_shapes=[pltpu.SMEM((owners,), jnp.int32)],
        compiler_params=pltpu.CompilerParams(vmem_limit_bytes=room(prompt_kv) * 4),
        name="quantize_pages",
    )(me_ref, page_owner.reshape(-1), prompt_kv.transpose(0, 1, 3, 2, 4))
    line = [mine] + [moves.along_z(mine, -shift) for shift in range(1, moves.lines)]
    line = jnp.concatenate(line, axis=0)
    fresh = new_kv.transpose(2, 3, 0, 1, 4).reshape(2, heads, tokens, width)
    fresh = jnp.pad(fresh, ((0, 0), (0, 0), (0, 128 - tokens), (0, 0)))
    tables = [t.reshape(owners, pages) for t in (page_owner, page_slot, page_fill)]
    line, send = lax.optimization_barrier((line, send))
    sr = jnp.concatenate([line, moves.flip(line, 0)], axis=0)
    sr, fresh, tables = lax.optimization_barrier((sr, fresh, tables))
    r2 = moves.flip(sr, 1)
    cache = lax.all_to_all(send, "ep", split_axis=0, concat_axis=0, tiled=True)
    core_then, cache = lax.optimization_barrier((core, cache))

    def weights_of(half):
        return [
            lax.dynamic_slice_in_dim(w[0], half * (d // 2), d // 2, axis=0) for w in (w_gate, w_up)
        ]

    near_weights = weights_of(core_then)
    r2, near_weights = lax.optimization_barrier((r2, near_weights))
    other_sr, other_r2 = moves.cores(sr), moves.cores(r2)

    parts = expert_front((sr, r2), *near_weights, None)
    hidden = expert_front((other_sr, other_r2), *weights_of(1 - core_then), parts)
    other_hidden = moves.cores(hidden)
    sent = expert_back(True, owners, at, hidden, other_hidden, w_down, sr, r2, lanes)
    kept = expert_back(False, owners, at, hidden, other_hidden, w_down, sr, r2, lanes)
    attn_out = pl.pallas_call(
        functools.partial(attention_kernel, pages),
        out_shape=jax.ShapeDtypeStruct(queries.shape, jnp.bfloat16),
        in_specs=[smem()] + [vmem()] * 6,
        out_specs=vmem(),
        compiler_params=pltpu.CompilerParams(vmem_limit_bytes=8 * MIB + 16 * slots * page_len * tokens * q_heads),
        name="attention",
    )(
        me_ref,
        *tables,
        queries,
        cache,
        fresh,
    )
    group = moves.lines * tokens
    kept = kept + moves.flip(sent, 0).astype(jnp.float32)
    kept, attn_out = lax.optimization_barrier((kept, attn_out))
    kept = kept[:group] + moves.flip(kept[group:].astype(jnp.bfloat16), 1).astype(jnp.float32)
    moe = kept[:tokens]
    for shift in range(1, moves.lines):
        block = kept[shift * tokens : (shift + 1) * tokens].astype(jnp.bfloat16)
        moe = moe + moves.along_z(block, shift).astype(jnp.float32)
    moe = moe.astype(jnp.bfloat16)
    moe_out = moe.reshape(steps, requests, d // 2).transpose(1, 0, 2)

    return (attn_out, moe_out)


def solution(mesh):
    return jax.shard_map(
        body,
        mesh=mesh,
        in_specs=(
            P(("grp", "ep"), None, None, "pd", None),
            P("grp", None),
            P("grp"),
            P("grp"),
            P(("grp", "ep"), None, "pd", None),
            P(("grp", "ep"), None, None, "pd", None),
            P(("grp", "ep"), None, None),
            P(None, ("grp", "ep"), None),
            P(("grp", "ep"), None, None),
            P("ep", None, "pd"),
            P("ep", None, "pd"),
            P("ep", None, "pd"),
        ),
        out_specs=(P(("grp", "ep"), None, "pd", None), P(("grp", "ep"), None, "pd")),
        check_vma=False,
    )
```

```python
import functools
import math

import jax
import jax.numpy as jnp
from jax import lax
from jax.experimental import pallas as pl
from jax.experimental.pallas import tpu as pltpu
from jax.sharding import PartitionSpec as P

CAP = 2
LIMIT = 448.0
MIB = 1024 * 1024


def vmem():
    return pl.BlockSpec(memory_space=pltpu.VMEM)


def smem():
    return pl.BlockSpec(memory_space=pltpu.SMEM)


def page_kernel(pages, me_ref, owner_ref, kv_ref, send_ref, count_ref):
    values = kv_ref[...].astype(jnp.float32)
    largest = jnp.max(jnp.abs(values), axis=(3, 4), keepdims=True)
    scale = jnp.full(largest.shape, 2.0 ** (-16), jnp.float32)
    inverse = jnp.full(largest.shape, 2.0**16, jnp.float32)
    for exponent in range(-16, -6):
        exceeds = largest > LIMIT * 2.0**exponent
        scale = jnp.where(exceeds, scale * 2.0, scale)
        inverse = jnp.where(exceeds, inverse * 0.5, inverse)
    scaled = values * inverse
    rest = jnp.abs(scaled) * 2.0**6
    step = jnp.full(scaled.shape, 2.0 ** (-9), jnp.float32)
    for bits in (8, 4, 2, 1):
        exceeds = rest >= 2.0**bits
        rest = jnp.where(exceeds, rest * 2.0**-bits, rest)
        step = jnp.where(exceeds, step * 2.0**bits, step)
    levels = jnp.minimum(jnp.floor(rest * 8.0 + 0.5) * step, LIMIT)
    cache = (jnp.where(scaled < 0.0, -levels, levels) * scale).astype(jnp.bfloat16)

    send_ref[...] = jnp.zeros(send_ref.shape, send_ref.dtype)

    def clear(o, carry):
        count_ref[o] = 0
        return carry

    lax.fori_loop(0, count_ref.shape[0], clear, 0)
    first = me_ref[0] * pages
    for page in range(pages):
        owner = owner_ref[first + page]
        rank = count_ref[owner]
        count_ref[owner] = rank + 1
        send_ref[pl.ds(owner * CAP + rank, 1)] = cache[page : page + 1]


def attention_kernel(
    pages, me_ref, owner_ref, slot_ref, fill_ref, q_ref, cache_ref, fresh_ref, out_ref
):
    owners = owner_ref.shape[0]
    slots, _, heads, page_len, width = cache_ref.shape
    requests, steps, q_heads, _ = q_ref.shape
    group = q_heads // heads
    rows = requests * steps * group
    mine = (owner_ref[...] == me_ref[0]).astype(jnp.float32)
    before = (
        lax.broadcasted_iota(jnp.int32, (pages, pages), 0)
        < lax.broadcasted_iota(jnp.int32, (pages, pages), 1)
    ).astype(jnp.float32)
    rank = jnp.dot(mine, before, preferred_element_type=jnp.float32)
    code = (slot_ref[...] * (page_len + 1) + fill_ref[...]).astype(jnp.float32)
    columns = slots * page_len
    place = lax.broadcasted_iota(jnp.int32, (owners, columns), 1)
    source = lax.broadcasted_iota(jnp.int32, (owners, columns), 0)
    spread = jnp.zeros((owners, columns), jnp.float32)
    for c in range(CAP):
        held = jnp.sum(
            jnp.where((mine > 0.0) & (rank == float(c)), code, 0.0), axis=1, keepdims=True
        )
        spread = jnp.where(place // page_len == source * CAP + c, held, spread)
    line = jnp.sum(spread, axis=0, keepdims=True).astype(jnp.int32)
    request_of = line // (page_len + 1)
    fill_of = line - request_of * (page_len + 1)
    position = lax.broadcasted_iota(jnp.int32, (1, columns), 1) % page_len
    request_of = jnp.where(position < fill_of, request_of, -1)
    row_request = lax.broadcasted_iota(jnp.int32, (rows, 1), 0) // (steps * group)
    visible = row_request == request_of
    token = lax.broadcasted_iota(jnp.int32, (rows, 1), 0) // group
    first = row_request * steps
    fresh_at = lax.broadcasted_iota(jnp.int32, (1, fresh_ref.shape[2]), 1)
    fresh_visible = (fresh_at >= first) & (fresh_at <= token)
    factor = 1.0 / math.sqrt(width)
    contract = (((1,), (1,)), ((), ()))
    for head in range(heads):
        q = q_ref[:, :, head * group : (head + 1) * group, :].reshape(rows, width)
        keys = cache_ref[:, 0, head].reshape(columns, width)
        values = cache_ref[:, 1, head].reshape(columns, width)
        scores = lax.dot_general(q, keys, contract, preferred_element_type=jnp.float32) * factor
        fresh = (
            lax.dot_general(q, fresh_ref[0, head], contract, preferred_element_type=jnp.float32)
            * factor
        )
        scores = jnp.where(visible, scores, -jnp.inf)
        fresh = jnp.where(fresh_visible, fresh, -jnp.inf)
        peak = jnp.maximum(
            jnp.max(scores, axis=1, keepdims=True), jnp.max(fresh, axis=1, keepdims=True)
        )
        weight = jnp.exp(scores - peak)
        fresh_weight = jnp.exp(fresh - peak)
        total = jnp.sum(weight, axis=1, keepdims=True) + jnp.sum(
            fresh_weight, axis=1, keepdims=True
        )
        mixed = jnp.dot(
            weight.astype(jnp.bfloat16), values, preferred_element_type=jnp.float32
        ) + jnp.dot(
            fresh_weight.astype(jnp.bfloat16), fresh_ref[1, head], preferred_element_type=jnp.float32
        )
        out_ref[:, :, head * group : (head + 1) * group, :] = (
            (mixed / total).astype(out_ref.dtype).reshape(requests, steps, group, width)
        )


def pack_kernel(experts, core_ref, x_ref, route_ref, prob_ref, out_ref):
    half = x_ref.shape[1] // 2
    begin = pl.multiple_of(core_ref[0] * half, 128)
    out_ref[:, :half] = x_ref[:, pl.ds(begin, half)]
    shape = (x_ref.shape[0], out_ref.shape[1] - half)
    lane = lax.broadcasted_iota(jnp.int32, shape, 1)
    expert = lane % experts
    part = lane // experts
    dense = jnp.zeros(shape, jnp.float32)
    for k in range(route_ref.shape[1]):
        dense += jnp.where(route_ref[:, k : k + 1] == expert, prob_ref[:, k : k + 1], 0.0)
    high = dense.astype(jnp.bfloat16).astype(jnp.float32)
    middle = (dense - high).astype(jnp.bfloat16).astype(jnp.float32)
    low = dense - high - middle
    chosen = jnp.where(part == 0, high, jnp.where(part == 1, middle, low))
    out_ref[:, half:] = jnp.where(part < 3, chosen, 0.0).astype(out_ref.dtype)


def partial_kernel(chunks, sr_ref, r2_ref, gate_ref, up_ref, gate_sum, up_sum):
    half = gate_ref.shape[0]
    depth = half // chunks
    for c in range(chunks):
        at = slice(c * depth, (c + 1) * depth)
        x = jnp.concatenate([sr_ref[:, at], r2_ref[:, at]], axis=0)
        for weight, total in ((gate_ref, gate_sum), (up_ref, up_sum)):
            part = jnp.dot(x, weight[at], preferred_element_type=jnp.float32)
            total[...] = part if c == 0 else total[...] + part


def hidden_kernel(
    chunks, sr_ref, r2_ref, gate_ref, up_ref, gate_part, up_part, out_ref, sums
):
    half = gate_ref.shape[0]
    depth = half // chunks
    group = sr_ref.shape[0] // 2
    for c in range(chunks):
        at = slice(c * depth, (c + 1) * depth)
        x = jnp.concatenate(
            [sr_ref[:group, at], r2_ref[:group, at], sr_ref[group:, at], r2_ref[group:, at]],
            axis=0,
        )
        for i, (weight, start) in enumerate(((gate_ref, gate_part), (up_ref, up_part))):
            part = jnp.dot(x, weight[at], preferred_element_type=jnp.float32)
            sums[i] = (start[...] if c == 0 else sums[i]) + part
    gate = sums[0]
    out_ref[...] = (gate / (1.0 + jnp.exp(-gate)) * sums[1]).astype(out_ref.dtype)


def room(*arrays):
    return sum(math.prod(a.shape) * a.dtype.itemsize for a in arrays) * 9 // 8 + 4 * MIB


def expert_front(rows, w_gate, w_up, parts):
    tokens = 2 * rows[0].shape[0]
    half, f = w_gate.shape
    last = parts is not None
    total = jax.ShapeDtypeStruct((tokens, f), jnp.float32)
    scratch = [pltpu.VMEM((2, tokens, f), jnp.float32)] if last else []
    return pl.pallas_call(
        functools.partial(hidden_kernel if last else partial_kernel, 4),
        in_specs=[vmem()] * (6 if last else 4),
        out_specs=vmem() if last else [vmem(), vmem()],
        scratch_shapes=scratch,
        out_shape=jax.ShapeDtypeStruct((tokens, f), jnp.bfloat16) if last else [total, total],
        compiler_params=pltpu.CompilerParams(
            vmem_limit_bytes=room(*rows, w_gate, w_up, *[total] * (5 if last else 2))
        ),
        cost_estimate=pl.CostEstimate(
            flops=4 * tokens * half * f,
            bytes_accessed=2 * tokens * half + 4 * half * f + 8 * tokens * f,
            transcendentals=tokens * f if last else 0,
        ),
        name="expert_hidden" if last else "expert_partial",
    )(*rows, w_gate, w_up, *(parts or ()))


def back_kernel(
    send, experts, lanes, chunks, at_ref, own_ref, other_ref, sr_ref, r2_ref, down_ref, out_ref
):
    block = down_ref.shape[2] // chunks
    f = own_ref.shape[1]
    group = sr_ref.shape[0] // 2
    core = at_ref[1]
    first = int(send)

    def rows(ref, a, b):
        return jnp.concatenate(
            [ref[a * group : (a + 1) * group], ref[b * group : (b + 1) * group]], axis=0
        )

    own = rows(own_ref, 1, 3) if send else rows(own_ref, 0, 2)
    other = rows(other_ref, 2, 3) if send else rows(other_ref, 0, 1)
    begin = pl.multiple_of(core * f, 128)
    rest = pl.multiple_of((1 - core) * f, 128)
    tail = slice(sr_ref.shape[1] - lanes, sr_ref.shape[1])
    picked = slice(first * group, (first + 1) * group)
    probs = jnp.concatenate(
        [sr_ref[picked, tail].astype(jnp.float32), r2_ref[picked, tail].astype(jnp.float32)],
        axis=0,
    )
    lane = lax.broadcasted_iota(jnp.int32, probs.shape, 1)
    mine = lane % experts == at_ref[0]
    weight = jnp.sum(jnp.where(mine, probs, 0.0), axis=1, keepdims=True)
    for c in range(chunks):
        at = slice(c * block, (c + 1) * block)
        total = jnp.dot(own, down_ref[0, pl.ds(begin, f), at], preferred_element_type=jnp.float32)
        total += jnp.dot(
            other, down_ref[0, pl.ds(rest, f), at], preferred_element_type=jnp.float32
        )
        out_ref[:, at] = (total * weight).astype(out_ref.dtype)


def expert_back(send, experts, at, own, other, w_down, sr, r2, lanes):
    tokens, f = own.shape
    group2 = sr.shape[0]
    width = w_down.shape[2]
    out = jax.ShapeDtypeStruct((group2, width), jnp.bfloat16 if send else jnp.float32)
    return pl.pallas_call(
        functools.partial(back_kernel, send, experts, lanes, 4),
        out_shape=out,
        in_specs=[smem()] + [vmem()] * 5,
        out_specs=vmem(),
        compiler_params=pltpu.CompilerParams(
            vmem_limit_bytes=room(own, other, w_down, sr, r2, out, out)
        ),
        cost_estimate=pl.CostEstimate(
            flops=2 * tokens * f * width,
            bytes_accessed=2 * (2 * tokens * f + 2 * f * width + 2 * group2 * width),
            transcendentals=0,
        ),
        name="expert_back_send" if send else "expert_back_keep",
    )(at, own, other, sr, r2, w_down)


class Moves:
    def __init__(self, owners):
        self.owners = owners
        self.lines = owners // 4

    def go(self, x, where):
        perm = [
            (ep * 2 + core, where(ep, core)) for ep in range(self.owners) for core in range(2)
        ]
        return lax.ppermute(x, ("ep", "pd"), perm)

    def along_z(self, x, shift):
        return self.go(x, lambda ep, core: (ep + 4 * shift) % self.owners * 2 + core)

    def flip(self, x, turn):
        return self.go(x, lambda ep, core: (ep ^ (1 << ((core + turn) % 2))) * 2 + core)

    def cores(self, x):
        return self.go(x, lambda ep, core: ep * 2 + 1 - core)


def body(
    prompt_kv,
    page_owner,
    page_slot,
    page_fill,
    queries,
    new_kv,
    moe_input,
    expert_routes,
    route_probs,
    w_gate,
    w_up,
    w_down,
):
    owners = lax.axis_size("ep")
    me = lax.axis_index("ep").astype(jnp.int32)
    me_ref = me.reshape(1)
    core = lax.axis_index("pd").astype(jnp.int32)
    pages, _, page_len, heads, width = prompt_kv.shape
    requests, steps, q_heads, _ = queries.shape
    d = moe_input.shape[2]
    tokens = requests * steps
    slots = owners * CAP

    moves = Moves(owners)
    top = expert_routes.shape[2]
    lanes = -(-3 * owners // 128) * 128
    at = jnp.stack([me, core])
    own_core = core.reshape(1)
    mine = pl.pallas_call(
        functools.partial(pack_kernel, owners),
        out_shape=jax.ShapeDtypeStruct((tokens, d // 2 + lanes), jnp.bfloat16),
        in_specs=[smem()] + [vmem()] * 3,
        out_specs=vmem(),
        name="pack_tokens",
    )(
        own_core,
        moe_input.transpose(1, 0, 2).reshape(tokens, d),
        expert_routes.reshape(tokens, top),
        route_probs.transpose(1, 0, 2).reshape(tokens, top),
    )
    send = pl.pallas_call(
        functools.partial(page_kernel, pages),
        out_shape=jax.ShapeDtypeStruct((slots, 2, heads, page_len, width), jnp.bfloat16),
        in_specs=[smem(), smem(), vmem()],
        out_specs=vmem(),
        scratch_shapes=[pltpu.SMEM((owners,), jnp.int32)],
        compiler_params=pltpu.CompilerParams(vmem_limit_bytes=room(prompt_kv) * 4),
        name="quantize_pages",
    )(me_ref, page_owner.reshape(-1), prompt_kv.transpose(0, 1, 3, 2, 4))
    line = [mine] + [moves.along_z(mine, -shift) for shift in range(1, moves.lines)]
    line = jnp.concatenate(line, axis=0)
    fresh = new_kv.transpose(2, 3, 0, 1, 4).reshape(2, heads, tokens, width)
    fresh = jnp.pad(fresh, ((0, 0), (0, 0), (0, 128 - tokens), (0, 0)))
    tables = [t.reshape(owners, pages) for t in (page_owner, page_slot, page_fill)]
    line, send = lax.optimization_barrier((line, send))
    sr = jnp.concatenate([line, moves.flip(line, 0)], axis=0)
    sr, fresh, tables = lax.optimization_barrier((sr, fresh, tables))
    r2 = moves.flip(sr, 1)
    cache = lax.all_to_all(send, "ep", split_axis=0, concat_axis=0, tiled=True)
    core_then, cache = lax.optimization_barrier((core, cache))

    def weights_of(half):
        return [
            lax.dynamic_slice_in_dim(w[0], half * (d // 2), d // 2, axis=0) for w in (w_gate, w_up)
        ]

    near_weights = weights_of(core_then)
    r2, near_weights = lax.optimization_barrier((r2, near_weights))
    core_last, r2 = lax.optimization_barrier((core_then, r2))
    other_sr, other_r2 = moves.cores(sr), moves.cores(r2)

    parts = expert_front((sr, r2), *near_weights, None)
    hidden = expert_front((other_sr, other_r2), *weights_of(1 - core_last), parts)
    other_hidden = moves.cores(hidden)
    sent = expert_back(True, owners, at, hidden, other_hidden, w_down, sr, r2, lanes)
    kept = expert_back(False, owners, at, hidden, other_hidden, w_down, sr, r2, lanes)
    attn_out = pl.pallas_call(
        functools.partial(attention_kernel, pages),
        out_shape=jax.ShapeDtypeStruct(queries.shape, jnp.bfloat16),
        in_specs=[smem()] + [vmem()] * 6,
        out_specs=vmem(),
        compiler_params=pltpu.CompilerParams(vmem_limit_bytes=8 * MIB + 16 * slots * page_len * tokens * q_heads),
        name="attention",
    )(
        me_ref,
        *tables,
        queries,
        cache,
        fresh,
    )
    group = moves.lines * tokens
    kept = kept + moves.flip(sent, 0).astype(jnp.float32)
    kept, attn_out = lax.optimization_barrier((kept, attn_out))
    kept = kept[:group] + moves.flip(kept[group:].astype(jnp.bfloat16), 1).astype(jnp.float32)
    moe = kept[:tokens]
    for shift in range(1, moves.lines):
        block = kept[shift * tokens : (shift + 1) * tokens].astype(jnp.bfloat16)
        moe = moe + moves.along_z(block, shift).astype(jnp.float32)
    moe = moe.astype(jnp.bfloat16)
    moe_out = moe.reshape(steps, requests, d // 2).transpose(1, 0, 2)

    return (attn_out, moe_out)


def solution(mesh):
    return jax.shard_map(
        body,
        mesh=mesh,
        in_specs=(
            P(("grp", "ep"), None, None, "pd", None),
            P("grp", None),
            P("grp"),
            P("grp"),
            P(("grp", "ep"), None, "pd", None),
            P(("grp", "ep"), None, None, "pd", None),
            P(("grp", "ep"), None, None),
            P(None, ("grp", "ep"), None),
            P(("grp", "ep"), None, None),
            P("ep", None, "pd"),
            P("ep", None, "pd"),
            P("ep", None, "pd"),
        ),
        out_specs=(P(("grp", "ep"), None, "pd", None), P(("grp", "ep"), None, "pd")),
        check_vma=False,
    )
```
